128 devices in a mesh: section: 2 (over core), tensor: 8 (over x_lo, y), dp: 8 (over z, x_hi).
Axes of the slice: x: 4 (x_hi: 2, x_lo: 2; x = x_hi * 2 + x_lo), y: 4, z: 4, core: 2. Of those that a mesh axis runs over, the one named last changes fastest.
Arguments:
- inputs: bfloat16 [2, 2048, 1536], P(None, 'dp'), may hold values from -6 to 6
- cotangent: bfloat16 [2, 2048, 1536], P(None, 'dp'), may hold values from -6 to 6
- doc_lengths: int32 [2, 32], replicated, may hold values from 0 to 1792, as said below
- norm_one: bfloat16 [2, 1536], P('section'), may hold values from 0.25 to 1.75
- query_w: bfloat16 [2, 1536, 1536], P('section', None, 'tensor'), may hold values from -0.15625 to 0.15625
- key_w: bfloat16 [2, 1536, 768], P('section', None, 'tensor'), may hold values from -0.15625 to 0.15625
- value_w: bfloat16 [2, 1536, 768], P('section', None, 'tensor'), may hold values from -0.15625 to 0.15625
- out_w: bfloat16 [2, 1536, 1536], P('section', 'tensor'), may hold values from -3.5 to 3.5
- norm_two: bfloat16 [2, 1536], P('section'), may hold values from 0.25 to 1.75
- gate_w: bfloat16 [2, 1536, 4096], P('section', None, 'tensor'), may hold values from -0.15625 to 0.15625
- up_w: bfloat16 [2, 1536, 4096], P('section', None, 'tensor'), may hold values from -0.15625 to 0.15625
- down_w: bfloat16 [2, 4096, 1536], P('section', 'tensor'), may hold values from -0.09375 to 0.09375
Outputs:
- layer_outputs: bfloat16 [2, 2, 2048, 1536], P('section', None, ('dp', 'tensor'))
- input_grads: float32 [2, 2, 2048, 1536], P('section', None, ('dp', 'tensor'))
- grad_norm_one: float32 [2, 1536], P('section')
- grad_query: float32 [2, 1536, 1536], P('section', None, 'tensor')
- grad_key: float32 [2, 1536, 768], P('section', None, 'tensor')
- grad_value: float32 [2, 1536, 768], P('section', None, 'tensor')
- grad_out: float32 [2, 1536, 1536], P('section', 'tensor')
- grad_norm_two: float32 [2, 1536], P('section')
- grad_gate: float32 [2, 1536, 4096], P('section', None, 'tensor')
- grad_up: float32 [2, 1536, 4096], P('section', None, 'tensor')
- grad_down: float32 [2, 4096, 1536], P('section', 'tensor')
The draws below stay inside these ranges and needn't reach their ends.
Inputs may be any that keep to these rules, and one draw needn't show every extreme that they name: `doc_lengths`: each row lists the lengths of its documents in order, followed by zeros; they add up to 2048.
All inputs are finite; a program needn't handle non-finite values.
Results may differ from the reference program's by a relative error of at most 0.035.
Values may be sent and summed in bfloat16 or wider, within the bound.
A program may use at most 192 MiB of HBM per device.

```python
import math
import jax
import jax.numpy as jnp
from jax import lax

D = 1536
HEADS = 16
KV_HEADS = 8
HD = 96
FF = 4096
MB = 2
NDOC = 32
LENGTH = 2048
SPAN = 256


def draw_doc_lengths(key, part):
    key = jax.random.fold_in(key, 7)
    key_head, key_first, key_tail, key_short, key_pick = jax.random.split(key, 5)
    head_rows = jax.random.randint(key_head, (MB,), 2, SPAN - 2)
    first_rows = jax.random.randint(key_first, (MB,), 1, head_rows)
    tail_rows = SPAN - head_rows
    last_rows = jax.random.randint(key_tail, (MB,), 1, tail_rows)
    long_rows = jnp.full((MB,), LENGTH - SPAN, jnp.int32)
    long_table = jnp.stack([first_rows, head_rows - first_rows, long_rows, last_rows, tail_rows - last_rows], axis=1).astype(jnp.int32)
    long_table = jnp.concatenate([long_table, jnp.zeros((MB, NDOC - 5), jnp.int32)], axis=1)
    short_lo = max(1, LENGTH // 32)
    short_hi = LENGTH * 25 // 64
    pieces = jax.random.randint(key_short, (MB, NDOC), short_lo, short_hi + 1).astype(jnp.int32)
    ends = jnp.cumsum(pieces, axis=1)
    inside = ends <= LENGTH
    kept = jnp.where(inside, pieces, 0)
    count = jnp.sum(inside.astype(jnp.int32), axis=1)
    remaining = LENGTH - jnp.sum(kept, axis=1)
    slots = jnp.arange(NDOC, dtype=jnp.int32)
    short_table = kept + jnp.where(slots[None, :] == count[:, None], remaining[:, None], 0)
    picked = jax.random.randint(key_pick, (), 0, MB)
    chosen = (jnp.arange(MB, dtype=jnp.int32) == picked)[:, None]
    return jnp.where(chosen, long_table, short_table).astype(jnp.int32)


def block_scale(key, dims, cuts, low, largest):
    gain = 1.0
    for position, parts in cuts:
        steps = jax.random.uniform(jax.random.fold_in(jax.random.fold_in(key, 6), position), (parts,), jnp.float32, low / len(cuts), largest / len(cuts))
        gain = gain * jnp.repeat(jnp.exp(steps), dims[position] // parts).reshape((-1,) + (1,) * (len(dims) - 1 - position))
    return gain


def scatter_about(rng, dims, spread, limit, cuts=(), held_as=jnp.bfloat16):
    gain = block_scale(rng, dims, cuts, -0.22, 0.18) if cuts else 1.0
    values = jax.random.normal(rng, dims, jnp.float32) * spread * gain
    return jnp.minimum(jnp.maximum(values, -limit), limit).astype(held_as)


def setup_inputs(seed: int = 0) -> dict:
    streams_of = jax.random.split(jax.random.key(seed), 13)
    return {
        "inputs": scatter_about(streams_of[0], (MB, LENGTH, D), 1.0, 6.0, ((1, 8),)),
        "cotangent": scatter_about(streams_of[1], (MB, LENGTH, D), 1.0, 6.0, ((1, 8),)),
        "doc_lengths": draw_doc_lengths(jax.random.fold_in(streams_of[12], 71), 0),
        "norm_one": jnp.clip(1.0 + 0.15 * jax.random.normal(streams_of[3], (2, D), jnp.float32), 0.25, 1.75).astype(jnp.bfloat16),
        "query_w": scatter_about(streams_of[4], (2, D, HEADS * HD), D ** -0.5, 0.15625, ((0, 2), (2, 8))),
        "key_w": scatter_about(streams_of[5], (2, D, KV_HEADS * HD), D ** -0.5, 0.15625, ((0, 2), (2, 8))),
        "value_w": scatter_about(streams_of[6], (2, D, KV_HEADS * HD), D ** -0.5, 0.15625, ((0, 2), (2, 8))),
        "out_w": scatter_about(streams_of[7], (2, HEADS * HD, D), (max(1, HEADS * HD * 4 // LENGTH)) ** -0.5, 3.5, ((0, 2), (1, 8))),
        "norm_two": jnp.clip(1.0 + 0.15 * jax.random.normal(streams_of[8], (2, D), jnp.float32), 0.25, 1.75).astype(jnp.bfloat16),
        "gate_w": scatter_about(streams_of[9], (2, D, FF), D ** -0.5, 0.15625, ((0, 2), (2, 8))),
        "up_w": scatter_about(streams_of[10], (2, D, FF), D ** -0.5, 0.15625, ((0, 2), (2, 8))),
        "down_w": scatter_about(streams_of[11], (2, FF, D), FF ** -0.5, 0.09375, ((0, 2), (1, 8))),
    }


eps_norm = 1e-05
rope_base = 100000.0
masked_score = -1e+30
highest = lax.Precision.HIGHEST

@jax.custom_vjp
def low(v):
    return lax.optimization_barrier(v.astype(jnp.bfloat16)).astype(jnp.float32)

@jax.custom_vjp
def low_back(v):
    return v

def low_keep(v):
    return (low(v), None)

def low_pass(kept, grad):
    return (grad,)

def back_keep(v):
    return (v, None)

def back_low(kept, grad):
    return (low(grad),)
low.defvjp(low_keep, low_pass)
low_back.defvjp(back_keep, back_low)

def rms_norm(values, gain_row):
    factor = lax.rsqrt(lax.optimization_barrier(jnp.mean(values * values, axis=-1, keepdims=True)) + eps_norm)
    return values * factor * gain_row

def rotate(values, angles):
    half_size = values.shape[-1] // 2
    first_half = values[..., :half_size]
    second_half = values[..., half_size:]
    cosine = jnp.cos(angles)
    sine_values = jnp.sin(angles)
    return jnp.concatenate([first_half * cosine - second_half * sine_values, second_half * cosine + first_half * sine_values], axis=-1)

def doc_layout(lengths, row_start, row_count):
    doc_ends = jnp.cumsum(lengths).astype(jnp.int32)
    starts = doc_ends - lengths.astype(jnp.int32)
    places = row_start + jnp.arange(row_count, dtype=jnp.int32)
    begins = lax.optimization_barrier(jnp.max(jnp.where(starts[None, :] <= places[:, None], starts[None, :], 0), axis=1)).astype(jnp.int32)
    inverse_freq = jnp.exp(jnp.arange(HD // 2, dtype=jnp.float32) * (-2.0 * math.log(rope_base) / HD))
    angles = (places - begins).astype(jnp.float32)[:, None] * inverse_freq[None, :]
    return (places, begins, angles)

def product(left_side, right_side):
    return jnp.dot(left_side, right_side, precision=highest)

def layer(weights, layer_in, places, begins, angles):
    gain_one, query_w, key_w, value_w, out_w, gain_two, gate_w, up_w, down_w = weights
    seq_rows = layer_in.shape[0]
    group_size = HEADS // KV_HEADS
    score_scale = 1.0 / math.sqrt(HD)
    normed = low(rms_norm(layer_in, gain_one))
    queries = low_back(product(normed, query_w)).reshape(seq_rows, HEADS, HD)
    key_raw = low_back(product(normed, key_w)).reshape(seq_rows, KV_HEADS, HD)
    values = low(low_back(product(normed, value_w))).reshape(seq_rows, KV_HEADS, HD)
    queries = low(rotate(queries, angles[:, None, :])).reshape(seq_rows, KV_HEADS, group_size, HD)
    key_rot = low(rotate(key_raw, angles[:, None, :]))
    block_rows = min(512, seq_rows)

    def attend(block_number):
        first_row = block_number * block_rows
        block_queries = lax.dynamic_slice_in_dim(queries, first_row, block_rows, 0)
        block_places = lax.dynamic_slice_in_dim(places, first_row, block_rows, 0)
        block_begins = lax.dynamic_slice_in_dim(begins, first_row, block_rows, 0)
        scores = low_back(jnp.einsum('qkgd,skd->kgqs', block_queries, key_rot, precision=highest) * score_scale)
        allowed = (places[None, :] <= block_places[:, None]) & (places[None, :] >= block_begins[:, None])
        scores = jnp.where(allowed[None, None], scores, masked_score)
        soft_weights = low(jax.nn.softmax(scores, axis=-1))
        mixed_block = jnp.einsum('kgqs,skd->qkgd', soft_weights, values, precision=highest)
        return low_back(low(mixed_block.reshape(block_rows, HEADS * HD)))
    mixed_heads = lax.map(jax.checkpoint(attend), jnp.arange(seq_rows // block_rows, dtype=jnp.int32))
    mixed_heads = mixed_heads.reshape(seq_rows, HEADS * HD)
    hidden_state = layer_in + low_back(product(mixed_heads, out_w))
    normed_two = low(rms_norm(hidden_state, gain_two))
    gate_act = low_back(product(normed_two, gate_w))
    upward = low_back(product(normed_two, up_w))
    inner_act = low(jax.nn.silu(gate_act) * upward)
    return hidden_state + low_back(product(inner_act, down_w))

def reference(inputs, cotangent, doc_lengths, norm_one, query_w, key_w, value_w, out_w, norm_two, gate_w, up_w, down_w):
    stacked = (norm_one, query_w, key_w, value_w, out_w, norm_two, gate_w, up_w, down_w)
    section_weights = [tuple((weight_array[section_number].astype(jnp.float32) for weight_array in stacked)) for section_number in range(2)]
    totals = [tuple((jnp.zeros_like(item) for item in section_weights[section_number])) for section_number in range(2)]
    first_outs, second_outs, first_grads_in, second_grads_in = ([], [], [], [])
    for batch_number in range(MB):
        places, begins, angles = doc_layout(doc_lengths[batch_number], 0, LENGTH)

        def run_layer(weights, layer_in):
            return layer(weights, layer_in, places, begins, angles)
        first_out, first_back = jax.vjp(run_layer, section_weights[0], inputs[batch_number].astype(jnp.float32))
        middle = low(first_out)
        second_out, second_back = jax.vjp(run_layer, section_weights[1], middle)
        second_grads, middle_grad = second_back(cotangent[batch_number].astype(jnp.float32))
        first_grads, input_grad = first_back(low(middle_grad))
        totals[0] = tuple((total_item + grad_item for total_item, grad_item in zip(totals[0], first_grads)))
        totals[1] = tuple((total_item + grad_item for total_item, grad_item in zip(totals[1], second_grads)))
        first_outs.append(middle)
        second_outs.append(second_out)
        first_grads_in.append(input_grad)
        second_grads_in.append(middle_grad)
    layer_outputs = jnp.stack([jnp.stack(first_outs), jnp.stack(second_outs)]).astype(jnp.bfloat16)
    input_grads = jnp.stack([jnp.stack(first_grads_in), jnp.stack(second_grads_in)])
    grads = [jnp.stack([totals[0][number], totals[1][number]]) for number in range(9)]
    return (layer_outputs, input_grads, grads[0], grads[1], grads[2], grads[3], grads[4], grads[5], grads[6], grads[7], grads[8])
```

```python
import math

import jax
import jax.numpy as jnp
from jax import lax
from jax.experimental import pallas as pl
from jax.experimental.pallas import tpu as pltpu
from jax.sharding import PartitionSpec as P

MESH = pl.DeviceIdType.MESH
F32 = jnp.float32
BF16 = jnp.bfloat16

HD = 96
HALF = HD // 2
D = 1536
FF = 512
ROWS = 256
OWN = 32
SCALE = 1.0 / math.sqrt(HD)
EPS = 1e-05
ROPE = 100000.0
MASKED = -1e30


def dot(a, b):
    return lax.dot_general(a, b, (((1,), (0,)), ((), ())), preferred_element_type=F32)


def dot_nt(a, b):
    return lax.dot_general(a, b, (((1,), (1,)), ((), ())), preferred_element_type=F32)


def dot_tn(a, b):
    return lax.dot_general(a, b, (((0,), (0,)), ((), ())), preferred_element_type=F32)


def lanes_of(v):
    return lax.broadcasted_iota(jnp.int32, v.shape, 1)


def swapped(v):
    return jnp.where(lanes_of(v) < HALF, pltpu.roll(v, 128 - HALF, 1), pltpu.roll(v, HALF, 1))


def factor_of(v):
    return lax.rsqrt(jnp.mean(v * v, axis=-1, keepdims=True) + EPS)


def kernel(
    x_hbm, ct_hbm, wqkv_hbm, wo_hbm, wg_hbm, wu_hbm, wd_hbm, gains_hbm, cos_ref, sin_ref, beg_ref,
    y_out, dx_out, ga_out, gb_out, gn_out,
    wqkv, wo, wgu, wd, gains, x_v, df,
    n1, n2, q2, q2t, kv, o_f, o_b, stat_m, stat_l, gate_s, up_s, u_s, x_own, h_own,
    rsrc, land, da, do2, do2t, dgu, dq, dqkv, dkv_t, dkv_src, dkv_land, acc, s_m,
    ga, gb, za, zb, xa, xb, fa, fb, yb, dxb, dgain, dg_peer, dg_t, dg_d,
    w_l, w_s, w_r, ag_s, ag_r, rs_s, rs_r, kv_s, kv_r, dkv_s, dkv_r, out_l, out_s, out_r,
    gs, gr, zs, zr, xs, xr, cs, cr, es, er, gl, ns, nr,
):
    sec = lax.axis_index("section")
    t = lax.axis_index("tensor")
    d = lax.axis_index("dp")
    other = 1 - sec
    z, xh = d // 2, d % 2

    barrier = pltpu.get_barrier_semaphore()

    def greet(axis, me, k, _):
        pl.semaphore_signal(barrier, inc=1, device_id={axis: (me + k) % 8}, device_id_type=MESH)
        return _

    pl.semaphore_signal(barrier, inc=1, device_id={"section": other}, device_id_type=MESH)
    lax.fori_loop(1, 8, lambda k, c: greet("tensor", t, k, c), 0)
    lax.fori_loop(1, 8, lambda k, c: greet("dp", d, k, c), 0)

    x_copy = pltpu.make_async_copy(x_hbm.at[sec], x_v, w_l.at[6])
    ct_copy = pltpu.make_async_copy(ct_hbm.at[sec], df, w_l.at[7])
    own_parts = [
        (wqkv_hbm, wqkv),
        (wo_hbm, wo),
        (wg_hbm, wgu.at[:, :, 0:FF]),
        (wu_hbm, wgu.at[:, :, FF : 2 * FF]),
        (wd_hbm, wd),
        (gains_hbm, gains),
    ]
    own_copies = [pltpu.make_async_copy(a, b.at[sec], w_l.at[i]) for i, (a, b) in enumerate(own_parts)]
    x_copy.start()
    own_copies[5].start()
    for i in range(5):
        own_copies[i].start()
    ct_copy.start()
    pl.semaphore_wait(barrier, 15)
    sent_parts = [
        pltpu.make_async_remote_copy(
            src_ref=a, dst_ref=b.at[sec], send_sem=w_s.at[i], recv_sem=w_r.at[i],
            device_id={"section": other}, device_id_type=MESH,
        )
        for i, (a, b) in enumerate(own_parts)
    ]
    for i in (5, 0, 1, 2, 3, 4):
        sent_parts[i].start()

    def weight_ready(layer, *which):
        @pl.when(layer == sec)
        def _():
            for i in which:
                own_copies[i].wait()

        @pl.when(layer != sec)
        def _():
            for i in which:
                a, b = own_parts[i]
                pltpu.make_async_remote_copy(
                    src_ref=a, dst_ref=b.at[other], send_sem=w_s.at[i], recv_sem=w_r.at[i],
                    device_id={"section": other}, device_id_type=MESH,
                ).wait_recv()

    def rows_of(i):
        return pl.ds(pl.multiple_of(i * OWN, OWN), OWN)

    my_rows = rows_of(t)

    def ag_start(buf, i):
        def body(k, c):
            p = (t + k) % 8
            pltpu.make_async_remote_copy(
                src_ref=buf.at[my_rows], dst_ref=buf.at[my_rows], send_sem=ag_s.at[i, p], recv_sem=ag_r.at[i, t],
                device_id={"tensor": p}, device_id_type=MESH,
            ).start()
            return c

        lax.fori_loop(1, 8, body, 0)

    def ag_wait(buf, i):
        def body(k, c):
            p = (t + k) % 8
            copy = pltpu.make_async_remote_copy(
                src_ref=buf.at[my_rows], dst_ref=buf.at[rows_of(p)], send_sem=ag_s.at[i, p], recv_sem=ag_r.at[i, p],
                device_id={"tensor": p}, device_id_type=MESH,
            )
            copy.wait_recv()
            copy.wait_send()
            return c

        lax.fori_loop(1, 8, body, 0)

    def rs_start(i):
        def body(k, c):
            p = (t + k) % 8
            pltpu.make_async_remote_copy(
                src_ref=rsrc.at[i, rows_of(p)], dst_ref=land.at[i, t], send_sem=rs_s.at[i, p], recv_sem=rs_r.at[i, t],
                device_id={"tensor": p}, device_id_type=MESH,
            ).start()
            return c

        lax.fori_loop(1, 8, body, 0)

    def rs_sum(i):
        acc_rows = rsrc[i, my_rows, :].astype(F32)

        def body(k, total):
            p = (t + k) % 8
            copy = pltpu.make_async_remote_copy(
                src_ref=rsrc.at[i, rows_of(p)], dst_ref=land.at[i, p], send_sem=rs_s.at[i, p], recv_sem=rs_r.at[i, p],
                device_id={"tensor": p}, device_id_type=MESH,
            )
            copy.wait_recv()
            copy.wait_send()
            return total + land[i, p].astype(F32)

        return lax.fori_loop(1, 8, body, acc_rows)

    def allowed_of(j):
        rows = lax.broadcasted_iota(jnp.int32, (ROWS, ROWS), 0) + d * ROWS
        cols = lax.broadcasted_iota(jnp.int32, (ROWS, ROWS), 1) + j * ROWS
        return (cols <= rows) & (cols >= beg_ref[...][:, 0:1])

    weight_ready(0, 5)
    x_copy.wait()

    def first_norm(i, c):
        rows = pl.ds(pl.multiple_of(i * OWN, OWN), OWN)
        v = x_v[rows, :].astype(F32)
        n1[0, rows, :] = (v * factor_of(v) * gains[0, 0:1, :]).astype(BF16)
        return c

    lax.fori_loop(0, ROWS // OWN, first_norm, 0)
    x_own[0] = x_v[my_rows, :].astype(F32)

    def forward_layer(layer, c):
        @pl.when(layer == 1)
        def _():
            weight_ready(1, 5)
            v = x_own[1]
            n1[1, my_rows, :] = (v * factor_of(v) * gains[1, 0:1, :]).astype(BF16)
            ag_start(n1.at[1], 0)
            ag_wait(n1.at[1], 0)

        weight_ready(layer, 0)
        raw = dot(n1[layer], wqkv[layer])
        c0, c1, c2 = raw[:, 0:128], raw[:, 128:256], raw[:, 256:384]
        lane = lanes_of(c0)
        q1 = jnp.where(lane < 32, pltpu.roll(c0, 32, 1), pltpu.roll(c1, 32, 1))
        k0 = jnp.where(lane < 64, pltpu.roll(c1, 64, 1), pltpu.roll(c2, 64, 1))
        v0 = pltpu.roll(c2, 96, 1)
        cosine, sine = cos_ref[...], sin_ref[...]
        for h, part in ((0, c0), (1, q1)):
            turned = part * cosine + swapped(part) * sine
            q2[layer, pl.ds(h * ROWS, ROWS), :] = turned[:, 0:HD].astype(BF16)
            q2t[layer, :, pl.ds(h * ROWS, ROWS)] = jnp.transpose(turned)[0:HD, :].astype(BF16)
        turned = k0 * cosine + swapped(k0) * sine
        kv[layer, d, pl.ds(0, HD), :] = jnp.transpose(turned)[0:HD, :].astype(BF16)
        kv[layer, d, pl.ds(HD, HD), :] = jnp.transpose(v0)[0:HD, :].astype(BF16)

        def kv_copy(owner, to):
            return pltpu.make_async_remote_copy(
                src_ref=kv.at[layer, owner], dst_ref=kv.at[layer, owner], send_sem=kv_s.at[to], recv_sem=kv_r.at[owner, layer],
                device_id={"dp": to}, device_id_type=MESH,
            )

        def kv_send(k, c):
            kv_copy(d, k).start()
            return c

        lax.fori_loop(d + 1, 8, kv_send, 0)
        s_m[...] = jnp.full(s_m.shape, MASKED, F32)
        stat_l[layer] = jnp.zeros((2 * ROWS, 1), F32)
        acc[...] = jnp.zeros(acc.shape, F32)

        def attend(i, c):
            j = d - i

            @pl.when(i > 0)
            def _():
                kv_copy(j, d).wait_recv()

            allowed = allowed_of(j)
            for h in range(2):
                rows = pl.ds(h * ROWS, ROWS)
                s = dot(q2[layer, rows, :], kv[layer, j, pl.ds(0, HD), :]) * SCALE
                s = jnp.where(allowed, s, MASKED)
                old = s_m[rows, :]
                new = jnp.maximum(old, jnp.max(s, axis=-1, keepdims=True))
                p = jnp.exp(s - new)
                shrink = jnp.exp(old - new)
                s_m[rows, :] = new
                stat_l[layer, rows, :] = stat_l[layer, rows, :] * shrink + jnp.sum(p, axis=-1, keepdims=True)
                acc[rows, :] = acc[rows, :] * shrink + dot_nt(p.astype(BF16), kv[layer, j, pl.ds(HD, HD), :])
            return c

        lax.fori_loop(0, d + 1, attend, 0)
        total = stat_l[layer]
        mixed = acc[...] / total
        o_f[layer] = mixed
        o_b[layer] = mixed.astype(BF16)
        stat_m[layer] = s_m[...] + jnp.log(total)

        def kv_sent(k, c):
            kv_copy(d, k).wait_send()
            return c

        weight_ready(layer, 1)

        def out_part(n, c):
            cols = pl.ds(pl.multiple_of(n * 512, 512), 512)
            part = dot(o_b[layer, pl.ds(0, ROWS), :], wo[layer, pl.ds(0, HD), cols])
            part += dot(o_b[layer, pl.ds(ROWS, ROWS), :], wo[layer, pl.ds(HD, HD), cols])
            rsrc[0, :, cols] = part.astype(BF16)
            return c

        lax.fori_loop(0, 3, out_part, 0)
        rs_start(0)
        lax.fori_loop(d + 1, 8, kv_sent, 0)
        v = x_own[layer] + rs_sum(0)
        h_own[layer] = v
        n2[layer, my_rows, :] = (v * factor_of(v) * gains[layer, 8:9, :]).astype(BF16)
        ag_start(n2.at[layer], 1)
        ag_wait(n2.at[layer], 1)
        weight_ready(layer, 2, 3)

        def units(n, c):
            cols = pl.ds(pl.multiple_of(n * 256, 256), 256)
            upper = pl.ds(pl.multiple_of(n * 256 + FF, 256), 256)
            g = dot(n2[layer], wgu[layer, :, cols])
            up = dot(n2[layer], wgu[layer, :, upper])
            gate_s[layer, :, cols] = g
            up_s[layer, :, cols] = up
            u_s[layer, :, cols] = (g * jax.nn.sigmoid(g) * up).astype(BF16)
            return c

        lax.fori_loop(0, 2, units, 0)
        weight_ready(layer, 4)

        def down_part(n, c):
            cols = pl.ds(pl.multiple_of(n * 512, 512), 512)
            rsrc[1, :, cols] = dot(u_s[layer], wd[layer, :, cols]).astype(BF16)
            return c

        lax.fori_loop(0, 3, down_part, 0)
        rs_start(1)
        y = (h_own[layer] + rs_sum(1)).astype(BF16)
        yb[layer] = y

        @pl.when(layer == 0)
        def _():
            x_own[1] = y.astype(F32)

        row_out(layer, yb, y_out, 0)
        return c

    def row_out(layer, buf, out, i):
        @pl.when(layer == sec)
        def _():
            pltpu.make_async_copy(buf.at[layer], out.at[sec], out_l.at[i]).start()

        @pl.when(layer != sec)
        def _():
            pltpu.make_async_remote_copy(
                src_ref=buf.at[layer], dst_ref=out.at[sec], send_sem=out_s.at[i], recv_sem=out_r.at[i],
                device_id={"section": other}, device_id_type=MESH,
            ).start()

    def row_out_wait(buf, out, i):
        pltpu.make_async_copy(buf.at[sec], out.at[sec], out_l.at[i]).wait()
        copy = pltpu.make_async_remote_copy(
            src_ref=buf.at[other], dst_ref=out.at[other], send_sem=out_s.at[i], recv_sem=out_r.at[i],
            device_id={"section": other}, device_id_type=MESH,
        )
        copy.wait_send()
        copy.wait_recv()

    lax.fori_loop(0, 2, forward_layer, 0)

    ct_copy.wait()

    def to_owner(layer, buf, i):
        return pltpu.make_async_remote_copy(
            src_ref=buf.at[sec * (1 - layer)], dst_ref=buf.at[1], send_sem=gs.at[i], recv_sem=gr.at[i],
            device_id={"section": other}, device_id_type=MESH,
        )

    def z_copy(buf, landing, i, to, sender):
        slot = (sender - to + 3) % 4
        return pltpu.make_async_remote_copy(
            src_ref=buf.at[0, to], dst_ref=landing.at[slot], send_sem=zs.at[i, to], recv_sem=zr.at[i, slot],
            device_id={"dp": to * 2 + xh}, device_id_type=MESH,
        )

    def x_copy_of(buf, landing, i):
        half = landing.shape[0]
        return pltpu.make_async_remote_copy(
            src_ref=buf.at[0, z, pl.ds((1 - xh) * half, half)], dst_ref=landing, send_sem=xs.at[i], recv_sem=xr.at[i],
            device_id={"dp": z * 2 + 1 - xh}, device_id_type=MESH,
        )

    def x_back(done, i, which):
        half = done.shape[0] // 2
        part = done.at[pl.ds(which * half, half)]
        return pltpu.make_async_remote_copy(
            src_ref=part, dst_ref=part, send_sem=cs.at[i], recv_sem=cr.at[i],
            device_id={"dp": z * 2 + 1 - xh}, device_id_type=MESH,
        )

    def z_back(done, out, i, to, sender):
        return pltpu.make_async_remote_copy(
            src_ref=done, dst_ref=out.at[sender], send_sem=es.at[i, to], recv_sem=er.at[i, sender],
            device_id={"dp": to * 2 + xh}, device_id_type=MESH,
        )

    def sum_step_1(buf, landing, i):
        to_owner(0, buf, i).wait_recv()
        rows = buf.shape[2] // 4
        for c in (2, 1, 3, 0):
            chunk = (z + c) % 4

            def add(n, carry):
                part = pl.ds(pl.multiple_of(n * rows, rows), rows)
                buf[0, chunk, part, :] = (buf[0, chunk, part, :].astype(F32) + buf[1, chunk, part, :].astype(F32)).astype(BF16)
                return carry

            lax.fori_loop(0, 4, add, 0)
            if c:
                z_copy(buf, landing, i, chunk, z).start()

    def sum_step_2(buf, landing, over, i):
        for c in range(1, 4):
            z_copy(buf, landing, i, z, (z + c) % 4).wait_recv()
        rows = buf.shape[2] // 4

        def add(n, carry):
            part = pl.ds(pl.multiple_of(n * rows, rows), rows)
            total = buf[0, z, part, :].astype(F32)
            for s in range(3):
                total += landing[s, part, :].astype(F32)
            buf[0, z, part, :] = total.astype(BF16)
            return carry

        lax.fori_loop(0, 4, add, 0)
        x_copy_of(buf, over, i).start()

    def sum_step_3(buf, over, done, i):
        x_copy_of(buf, over, i).wait_recv()
        half = over.shape[0]
        rows = half // 2

        def add(n, carry):
            part = pl.ds(pl.multiple_of(xh * half + n * rows, 16), rows)
            here = pl.ds(pl.multiple_of(n * rows, 16), rows)
            done[part, :] = (buf[0, z, part, :].astype(F32) + over[here, :].astype(F32)).astype(BF16)
            return carry

        lax.fori_loop(0, 2, add, 0)
        x_back(done, i, xh).start()

    def sum_step_4(done, out, i):
        x_back(done, i, 1 - xh).wait_recv()
        for c in (2, 1, 3):
            z_back(done, out, i, (z + c) % 4, z).start()
        pltpu.make_async_copy(done, out.at[z], gl.at[i]).start()

    def sum_step_5(buf, landing, over, done, out, i):
        x_copy_of(buf, over, i).wait_send()
        x_back(done, i, xh).wait_send()
        pltpu.make_async_copy(done, out.at[z], gl.at[i]).wait()
        for c in range(1, 4):
            peer = (z + c) % 4
            z_copy(buf, landing, i, peer, z).wait_send()
            z_back(done, out, i, peer, z).wait_send()
            z_back(done, out, i, z, peer).wait_recv()

    def backward_layer(step, c):
        layer = 1 - step
        mine = sec * (1 - layer)

        @pl.when(layer == 0)
        def _():
            ag_start(df, 2)

            @pl.when(sec == 1)
            def _():
                sum_step_1(ga, za, 0)

            ag_wait(df, 2)

        dy = df[my_rows, :].astype(F32)
        dxb[layer] = dy

        def unit_grads(n, c):
            cols = pl.ds(pl.multiple_of(n * 256, 256), 256)
            upper = pl.ds(pl.multiple_of(n * 256 + FF, 256), 256)
            du = dot_nt(df[...], wd[layer, cols, :])
            g, up = gate_s[layer, :, cols], up_s[layer, :, cols]
            sig = jax.nn.sigmoid(g)
            dgu[:, cols] = (du * up * sig * (1.0 + g * (1.0 - sig))).astype(BF16)
            dgu[:, upper] = (du * g * sig).astype(BF16)
            return c

        lax.fori_loop(0, 2, unit_grads, 0)

        def normed_part(n, c):
            cols = pl.ds(pl.multiple_of(n * 256, 256), 256)
            rsrc[0, :, cols] = dot_nt(dgu[...], wgu[layer, cols, :]).astype(BF16)
            return c

        lax.fori_loop(0, 6, normed_part, 0)
        rs_start(0)

        @pl.when((step == 1) & (sec == 0))
        def _():
            to_owner(1, ga, 0).wait_send()
            to_owner(1, gb, 1).wait_send()

        def unit_weights(n, c):
            cols = pl.ds(pl.multiple_of(n * 384, 384), 384)
            got = dot_tn(n2[layer, :, cols], dgu[...]).astype(BF16)
            ga[mine, n, pl.ds(0, 384), :] = got[:, 0:FF]
            ga[mine, n, pl.ds(384, 384), :] = got[:, FF : 2 * FF]
            cols = pl.ds(pl.multiple_of(n * 128, 128), 128)
            got = dot_tn(u_s[layer, :, cols], df[...]).astype(BF16)
            for i in range(3):
                ga[mine, n, pl.ds(768 + 128 * i, 128), :] = got[:, 512 * i : 512 * i + 512]
            return c

        lax.fori_loop(0, 4, unit_weights, 0)

        @pl.when(layer != sec)
        def _():
            to_owner(layer, ga, 0).start()

        @pl.when((step == 1) & (sec == 1))
        def _():
            sum_step_1(gb, zb, 1)

        dn = rs_sum(0)
        h = h_own[layer]
        r = factor_of(h)
        tt = dn * gains[layer, 8:9, :]
        dh = dxb[layer] + r * tt - h * (r * r * r * jnp.mean(h * tt, axis=-1, keepdims=True))
        dgain[layer, 1:2, :] = jnp.sum(dn * h * r, axis=0, keepdims=True)
        dxb[layer] = dh
        da[my_rows, :] = dh.astype(BF16)
        ag_start(da, 3)

        @pl.when((step == 1) & (sec == 1))
        def _():
            sum_step_2(ga, za, xa, 0)

        @pl.when((step == 1) & (sec == 0))
        def _():
            sum_step_1(ga, za, 0)

        ag_wait(da, 3)
        for h in range(2):
            rows = pl.ds(h * ROWS, ROWS)
            got = dot_nt(da[...], wo[layer, pl.ds(h * HD, HD), :])
            do2[rows, :] = got.astype(BF16)
            padded = jnp.concatenate([got, jnp.zeros((ROWS, 128 - HD), F32)], axis=1)
            do2t[:, rows] = jnp.transpose(padded)[0:HD, :].astype(BF16)
        dot_rows = jnp.sum(do2[...].astype(F32) * o_f[layer], axis=-1, keepdims=True)
        s_m[...] = dot_rows
        acc[...] = jnp.zeros(acc.shape, F32)

        def dkv_copy(to, sender):
            return pltpu.make_async_remote_copy(
                src_ref=dkv_src.at[to], dst_ref=dkv_land.at[layer, sender], send_sem=dkv_s.at[to], recv_sem=dkv_r.at[layer, sender],
                device_id={"dp": to}, device_id_type=MESH,
            )

        def attend_back(j, c):
            allowed = allowed_of(j)
            dkt = jnp.zeros((HD, ROWS), F32)
            dvt = jnp.zeros((HD, ROWS), F32)
            for h in range(2):
                rows = pl.ds(h * ROWS, ROWS)
                kt = kv[layer, j, pl.ds(0, HD), :]
                s = dot(q2[layer, rows, :], kt) * SCALE
                p = jnp.exp(jnp.where(allowed, s, MASKED) - stat_m[layer, rows, :])
                dp = dot(do2[rows, :], kv[layer, j, pl.ds(HD, HD), :])
                ds = (p * (dp - s_m[rows, :])).astype(BF16)
                acc[rows, :] += dot_nt(ds, kt)
                dkt += dot(q2t[layer, :, rows], ds)
                dvt += dot(do2t[:, rows], p.astype(BF16))
            dkv_src[j, pl.ds(0, HD), :] = (dkt * SCALE).astype(BF16)
            dkv_src[j, pl.ds(HD, HD), :] = dvt.astype(BF16)

            @pl.when(j < d)
            def _():
                dkv_copy(j, d).start()

            return c

        lax.fori_loop(0, d + 1, attend_back, 0)

        def dkv_sent(k, c):
            dkv_copy(k, d).wait_send()
            return c

        def out_weights(n, c):
            cols = pl.ds(pl.multiple_of(n * 384, 384), 384)
            for h in range(2):
                got = dot_tn(o_b[layer, pl.ds(h * ROWS, ROWS), :], da[:, cols])
                gb[mine, n, pl.ds(h * HD, HD), :] = got.astype(BF16)
            return c

        lax.fori_loop(0, 4, out_weights, 0)
        lax.fori_loop(0, d, dkv_sent, 0)

        @pl.when((step == 1) & (sec == 1))
        def _():
            sum_step_2(gb, zb, xb, 1)
            sum_step_3(ga, xa, fa, 0)

        @pl.when((step == 1) & (sec == 0))
        def _():
            sum_step_2(ga, za, xa, 0)

        def dkv_sum(k, total):
            dkv_copy(d, k).wait_recv()
            return total + dkv_land[layer, k].astype(F32)

        dkv_total = lax.fori_loop(d + 1, 8, dkv_sum, dkv_src[d].astype(F32))
        dkv_t[...] = jnp.zeros(dkv_t.shape, F32)
        dkv_t[0, pl.ds(0, HD), :] = dkv_total[0:HD]
        dkv_t[1, pl.ds(0, HD), :] = dkv_total[HD : 2 * HD]
        dk_rot = jnp.transpose(dkv_t[0])
        dv = jnp.transpose(dkv_t[1])
        cosine, sine = cos_ref[...], sin_ref[...]
        dq[...] = jnp.zeros(dq.shape, F32)
        dq[:, 0:HD] = acc[...] * SCALE
        dq0, dq1 = dq[pl.ds(0, ROWS), :], dq[pl.ds(ROWS, ROWS), :]
        dq0 = dq0 * cosine - swapped(dq0) * sine
        dq1 = dq1 * cosine - swapped(dq1) * sine
        dk = dk_rot * cosine - swapped(dk_rot) * sine
        lane = lanes_of(dk)
        dqkv[:, 0:128] = jnp.where(lane < HD, dq0, pltpu.roll(dq1, 96, 1)).astype(BF16)
        dqkv[:, 128:256] = jnp.where(lane < 64, pltpu.roll(dq1, 96, 1), pltpu.roll(dk, 64, 1)).astype(BF16)
        dqkv[:, 256:384] = jnp.where(lane < 32, pltpu.roll(dk, 64, 1), pltpu.roll(dv, 32, 1)).astype(BF16)

        def input_part(n, c):
            cols = pl.ds(pl.multiple_of(n * 256, 256), 256)
            rsrc[1, :, cols] = dot_nt(dqkv[...], wqkv[layer, cols, :]).astype(BF16)
            return c

        lax.fori_loop(0, 6, input_part, 0)
        rs_start(1)

        def qkv_weights(n, c):
            cols = pl.ds(pl.multiple_of(n * 384, 384), 384)
            gb[mine, n, pl.ds(2 * HD, 384), :] = dot_tn(n1[layer, :, cols], dqkv[...]).astype(BF16)
            return c

        lax.fori_loop(0, 4, qkv_weights, 0)

        @pl.when(layer != sec)
        def _():
            to_owner(layer, gb, 1).start()

        @pl.when((step == 1) & (sec == 1))
        def _():
            sum_step_3(gb, xb, fb, 1)
            sum_step_4(fa, ga_out, 0)

        @pl.when((step == 1) & (sec == 0))
        def _():
            sum_step_3(ga, xa, fa, 0)

        dn = rs_sum(1)
        v = x_own[layer]
        r = factor_of(v)
        tt = dn * gains[layer, 0:1, :]
        dx = dxb[layer] + r * tt - v * (r * r * r * jnp.mean(v * tt, axis=-1, keepdims=True))
        dgain[layer, 0:1, :] = jnp.sum(dn * v * r, axis=0, keepdims=True)
        dxb[layer] = dx
        df[my_rows, :] = dx.astype(BF16)
        row_out(layer, dxb, dx_out, 1)
        return c

    dgain[...] = jnp.zeros(dgain.shape, F32)
    lax.fori_loop(0, 2, backward_layer, 0)

    mate = pltpu.make_async_remote_copy(
        src_ref=dgain.at[other], dst_ref=dg_peer, send_sem=ns.at[0, 0], recv_sem=nr.at[0, 0],
        device_id={"section": other}, device_id_type=MESH,
    )
    mate.start()

    @pl.when(sec == 0)
    def _():
        sum_step_4(fa, ga_out, 0)
        sum_step_1(gb, zb, 1)

    @pl.when(sec == 1)
    def _():
        sum_step_4(fb, gb_out, 1)

    def gain_copy(axis, i, buf, me, to, sender):
        return pltpu.make_async_remote_copy(
            src_ref=buf.at[me], dst_ref=buf.at[sender], send_sem=ns.at[i, to], recv_sem=nr.at[i, sender],
            device_id={axis: to}, device_id_type=MESH,
        )

    def gain_round(axis, i, buf, me):
        def send(k, c):
            gain_copy(axis, i, buf, me, (me + k) % 8, me).start()
            return c

        def take(k, total):
            p = (me + k) % 8
            gain_copy(axis, i, buf, me, p, p).wait_recv()
            return total + buf[p]

        def sent(k, c):
            gain_copy(axis, i, buf, me, (me + k) % 8, me).wait_send()
            return c

        lax.fori_loop(1, 8, send, 0)
        total = lax.fori_loop(1, 8, take, buf[me])
        lax.fori_loop(1, 8, sent, 0)
        return total

    mate.wait_recv()
    mate.wait_send()
    dg_t[t] = dgain[sec] + dg_peer[...]
    dg_d[d] = gain_round("tensor", 1, dg_t, t)

    @pl.when(sec == 0)
    def _():
        sum_step_2(gb, zb, xb, 1)

    gn_out[...] = gain_round("dp", 2, dg_d, d)

    @pl.when(sec == 0)
    def _():
        sum_step_3(gb, xb, fb, 1)
        sum_step_4(fb, gb_out, 1)

    @pl.when(sec == 1)
    def _():
        to_owner(0, ga, 0).wait_send()
        to_owner(0, gb, 1).wait_send()

    sum_step_5(ga, za, xa, fa, ga_out, 0)
    sum_step_5(gb, zb, xb, fb, gb_out, 1)
    row_out_wait(yb, y_out, 0)
    row_out_wait(dxb, dx_out, 1)
    for i in range(6):
        sent_parts[i].wait_send()


def step_call(*args):
    hbm = pl.BlockSpec(memory_space=pl.ANY)
    vmem = pl.BlockSpec(memory_space=pltpu.VMEM)
    dma = pltpu.SemaphoreType.DMA
    scratch = [
        pltpu.VMEM((2, D, 384), BF16), pltpu.VMEM((2, 192, D), BF16), pltpu.VMEM((2, D, 2 * FF), BF16),
        pltpu.VMEM((2, FF, D), BF16), pltpu.VMEM((2, 16, D), F32), pltpu.VMEM((ROWS, D), BF16), pltpu.VMEM((ROWS, D), BF16),
        pltpu.VMEM((2, ROWS, D), BF16), pltpu.VMEM((2, ROWS, D), BF16), pltpu.VMEM((2, 2 * ROWS, HD), BF16),
        pltpu.VMEM((2, HD, 2 * ROWS), BF16), pltpu.VMEM((2, 8, 2 * HD, ROWS), BF16), pltpu.VMEM((2, 2 * ROWS, HD), F32),
        pltpu.VMEM((2, 2 * ROWS, HD), BF16), pltpu.VMEM((2, 2 * ROWS, 1), F32), pltpu.VMEM((2, 2 * ROWS, 1), F32),
        pltpu.VMEM((2, ROWS, FF), F32), pltpu.VMEM((2, ROWS, FF), F32), pltpu.VMEM((2, ROWS, FF), BF16),
        pltpu.VMEM((2, OWN, D), F32), pltpu.VMEM((2, OWN, D), F32),
        pltpu.VMEM((2, ROWS, D), BF16), pltpu.VMEM((2, 8, OWN, D), BF16), pltpu.VMEM((ROWS, D), BF16),
        pltpu.VMEM((2 * ROWS, HD), BF16), pltpu.VMEM((HD, 2 * ROWS), BF16), pltpu.VMEM((ROWS, 2 * FF), BF16),
        pltpu.VMEM((2 * ROWS, 128), F32), pltpu.VMEM((ROWS, 384), BF16), pltpu.VMEM((2, 128, ROWS), F32),
        pltpu.VMEM((8, 2 * HD, ROWS), BF16), pltpu.VMEM((2, 8, 2 * HD, ROWS), BF16), pltpu.VMEM((2 * ROWS, HD), F32),
        pltpu.VMEM((2 * ROWS, 1), F32),
        pltpu.VMEM((2, 4, 1152, 512), BF16), pltpu.VMEM((2, 4, 576, 384), BF16), pltpu.VMEM((3, 1152, 512), BF16),
        pltpu.VMEM((3, 576, 384), BF16), pltpu.VMEM((576, 512), BF16), pltpu.VMEM((288, 384), BF16),
        pltpu.VMEM((1152, 512), BF16), pltpu.VMEM((576, 384), BF16),
        pltpu.VMEM((2, OWN, D), BF16), pltpu.VMEM((2, OWN, D), F32), pltpu.VMEM((2, 8, D), F32), pltpu.VMEM((8, D), F32),
        pltpu.VMEM((8, 8, D), F32), pltpu.VMEM((8, 8, D), F32),
        dma((8,)), dma((6,)), dma((6,)), dma((4, 8)), dma((4, 8)), dma((2, 8)), dma((2, 8)), dma((8,)), dma((8, 2)),
        dma((8,)), dma((2, 8)), dma((2,)), dma((2,)), dma((2,)),
        dma((2,)), dma((2,)), dma((2, 4)), dma((2, 3)), dma((2,)), dma((2,)), dma((2,)), dma((2,)), dma((2, 4)),
        dma((2, 4)), dma((2,)), dma((3, 8)), dma((3, 8)),
    ]
    return pl.pallas_call(
        kernel,
        out_shape=(
            jax.ShapeDtypeStruct((2, OWN, D), BF16),
            jax.ShapeDtypeStruct((2, OWN, D), F32),
            jax.ShapeDtypeStruct((4, 1152, 512), BF16),
            jax.ShapeDtypeStruct((4, 576, 384), BF16),
            jax.ShapeDtypeStruct((8, D), F32),
        ),
        in_specs=[hbm] * 8 + [vmem] * 3,
        out_specs=(hbm, hbm, hbm, hbm, vmem),
        scratch_shapes=scratch,
        compiler_params=pltpu.CompilerParams(
            collective_id=0, has_side_effects=True, vmem_limit_bytes=64 * 1024 * 1024 - 65536
        ),
        name="train_step",
    )(*args)


def on_device(inputs, cotangent, doc_lengths, norm_one, query_w, key_w, value_w, out_w, norm_two, gate_w, up_w, down_w):
    wqkv = jnp.concatenate([query_w[0], key_w[0], value_w[0]], axis=1)
    gains = jnp.concatenate([jnp.broadcast_to(norm_one, (8, D)), jnp.broadcast_to(norm_two, (8, D))]).astype(F32)
    lengths = lax.dynamic_index_in_dim(doc_lengths, lax.axis_index("section"), 0, keepdims=False)
    starts = jnp.cumsum(lengths) - lengths
    places = lax.axis_index("dp") * ROWS + jnp.arange(ROWS, dtype=jnp.int32)
    begins = jnp.max(jnp.where(starts[None, :] <= places[:, None], starts[None, :], 0), axis=1)
    inverse = jnp.exp(jnp.arange(HALF, dtype=F32) * (-2.0 * math.log(ROPE) / HD))
    angles = (places - begins).astype(F32)[:, None] * inverse[None, :]
    cosine, sine = jnp.cos(angles), jnp.sin(angles)
    rest = jnp.zeros((ROWS, 128 - HD), F32)
    cosine = jnp.concatenate([cosine, cosine, rest], axis=1)
    sine = jnp.concatenate([-sine, sine, rest], axis=1)
    begins = jnp.broadcast_to(begins[:, None], (ROWS, 128))
    y, dx, ga, gb, gn = step_call(
        inputs, cotangent, wqkv, out_w[0], gate_w[0], up_w[0], down_w[0], gains, cosine, sine, begins
    )
    gate = ga[:, 0:384].reshape(D, FF).astype(F32)
    up = ga[:, 384:768].reshape(D, FF).astype(F32)
    down = ga[:, 768:].reshape(4, 3, 128, 512).transpose(0, 2, 1, 3).reshape(FF, D).astype(F32)
    out = gb[:, 0:192].transpose(1, 0, 2).reshape(192, D).astype(F32)
    qkv = gb[:, 192:].reshape(D, 384)
    grads = (
        gn[0:1], qkv[:, 0:192].astype(F32), qkv[:, 192:288].astype(F32), qkv[:, 288:384].astype(F32), out, gn[1:2], gate, up, down,
    )
    return (y[None], dx[None]) + tuple(g if g.shape[0] == 1 else g[None] for g in grads)


def solution(mesh):
    in_specs = (
        P(None, "dp", None),
        P(None, "dp", None),
        P(),
        P("section", None),
        P("section", None, "tensor"),
        P("section", None, "tensor"),
        P("section", None, "tensor"),
        P("section", "tensor", None),
        P("section", None),
        P("section", None, "tensor"),
        P("section", None, "tensor"),
        P("section", "tensor", None),
    )
    out_specs = (
        P("section", None, ("dp", "tensor"), None),
        P("section", None, ("dp", "tensor"), None),
        P("section", None),
        P("section", None, "tensor"),
        P("section", None, "tensor"),
        P("section", None, "tensor"),
        P("section", "tensor", None),
        P("section", None),
        P("section", None, "tensor"),
        P("section", None, "tensor"),
        P("section", "tensor", None),
    )
    return jax.shard_map(on_device, mesh=mesh, in_specs=in_specs, out_specs=out_specs, check_vma=False)
```

```python
import math

import jax
import jax.numpy as jnp
from jax import lax
from jax.experimental import pallas as pl
from jax.experimental.pallas import tpu as pltpu
from jax.sharding import PartitionSpec as P

MESH = pl.DeviceIdType.MESH
F32 = jnp.float32
BF16 = jnp.bfloat16

HD = 96
HALF = HD // 2
D = 1536
FF = 512
ROWS = 256
OWN = 32
SCALE = 1.0 / math.sqrt(HD)
EPS = 1e-05
ROPE = 100000.0
MASKED = -1e30


def dot(a, b):
    return lax.dot_general(a, b, (((1,), (0,)), ((), ())), preferred_element_type=F32)


def dot_nt(a, b):
    return lax.dot_general(a, b, (((1,), (1,)), ((), ())), preferred_element_type=F32)


def dot_tn(a, b):
    return lax.dot_general(a, b, (((0,), (0,)), ((), ())), preferred_element_type=F32)


def lanes_of(v):
    return lax.broadcasted_iota(jnp.int32, v.shape, 1)


def swapped(v):
    return jnp.where(lanes_of(v) < HALF, pltpu.roll(v, 128 - HALF, 1), pltpu.roll(v, HALF, 1))


def factor_of(v):
    return lax.rsqrt(jnp.mean(v * v, axis=-1, keepdims=True) + EPS)


def kernel(
    x_hbm, ct_hbm, wq_hbm, wk_hbm, wv_hbm, wo_hbm, wg_hbm, wu_hbm, wd_hbm, gains_hbm, cos_ref, sin_ref, beg_ref,
    y_out, dx_out, ga_out, gb_out, gn_out,
    wqkv, wo, wgu, wd, gains, df,
    n1, n2, q2, q2t, kv, o_f, o_b, stat_m, stat_l, gate_s, up_s, u_s, x_own, h_own,
    rsrc, land, da, do2, do2t, dgu, dq, dqkv, dkv_t, dkv_src, dkv_land, acc, s_m,
    ga, gb, da_in, db_in, za, rb, xa, fa, fb, yb, dxb, dgain, dg_peer, dg_t, dg_d,
    w_l, w_s, w_r, ag_s, ag_r, rs_s, rs_r, kv_s, kv_r, dkv_s, dkv_r, out_l, out_s, out_r,
    ds_s, ds_r, z_s, z_r, x_s, x_r, a_s, a_r, a_l, f_s, f_r, b_s, b_r, e_s, e_r, e_l, ns, nr,
):
    sec = lax.axis_index("section")
    t = lax.axis_index("tensor")
    d = lax.axis_index("dp")
    other = 1 - sec
    z, xh = d // 2, d % 2

    barrier = pltpu.get_barrier_semaphore()

    def greet(axis, me, k, _):
        pl.semaphore_signal(barrier, inc=1, device_id={axis: (me + k) % 8}, device_id_type=MESH)
        return _

    pl.semaphore_signal(barrier, inc=1, device_id={"section": other}, device_id_type=MESH)
    lax.fori_loop(1, 8, lambda k, c: greet("tensor", t, k, c), 0)
    lax.fori_loop(1, 8, lambda k, c: greet("dp", d, k, c), 0)

    x_copy = pltpu.make_async_copy(x_hbm.at[sec], df, w_l.at[8])
    ct_copy = pltpu.make_async_copy(ct_hbm.at[sec], df, w_l.at[9])
    own_parts = [
        (wq_hbm, lambda i: wqkv.at[i, pl.ds(0, 2 * HD)]),
        (wk_hbm, lambda i: wqkv.at[i, pl.ds(2 * HD, HD)]),
        (wv_hbm, lambda i: wqkv.at[i, pl.ds(3 * HD, HD)]),
        (wo_hbm, lambda i: wo.at[i]),
        (wg_hbm, lambda i: wgu.at[i, :, 0:FF]),
        (wu_hbm, lambda i: wgu.at[i, :, FF : 2 * FF]),
        (wd_hbm, lambda i: wd.at[i]),
        (gains_hbm, lambda i: gains.at[i]),
    ]
    n_parts = len(own_parts)
    own_copies = [pltpu.make_async_copy(a, b(sec), w_l.at[i]) for i, (a, b) in enumerate(own_parts)]
    x_copy.start()
    own_copies[7].start()
    for i in range(7):
        own_copies[i].start()
    pl.semaphore_wait(barrier, 15)
    sent_parts = [
        pltpu.make_async_remote_copy(
            src_ref=a, dst_ref=b(sec), send_sem=w_s.at[i], recv_sem=w_r.at[i],
            device_id={"section": other}, device_id_type=MESH,
        )
        for i, (a, b) in enumerate(own_parts)
    ]
    for i in (7, 0, 1, 2, 3, 4, 5, 6):
        sent_parts[i].start()

    def weight_ready(layer, *which):
        @pl.when(layer == sec)
        def _():
            for i in which:
                own_copies[i].wait()

        @pl.when(layer != sec)
        def _():
            for i in which:
                a, b = own_parts[i]
                pltpu.make_async_remote_copy(
                    src_ref=a, dst_ref=b(other), send_sem=w_s.at[i], recv_sem=w_r.at[i],
                    device_id={"section": other}, device_id_type=MESH,
                ).wait_recv()

    def rows_of(i):
        return pl.ds(pl.multiple_of(i * OWN, OWN), OWN)

    my_rows = rows_of(t)

    def ag_start(buf, i):
        def body(k, c):
            p = (t + k) % 8
            pltpu.make_async_remote_copy(
                src_ref=buf.at[my_rows], dst_ref=buf.at[my_rows], send_sem=ag_s.at[i, p], recv_sem=ag_r.at[i, t],
                device_id={"tensor": p}, device_id_type=MESH,
            ).start()
            return c

        lax.fori_loop(1, 8, body, 0)

    def ag_wait(buf, i):
        def body(k, c):
            p = (t + k) % 8
            copy = pltpu.make_async_remote_copy(
                src_ref=buf.at[my_rows], dst_ref=buf.at[rows_of(p)], send_sem=ag_s.at[i, p], recv_sem=ag_r.at[i, p],
                device_id={"tensor": p}, device_id_type=MESH,
            )
            copy.wait_recv()
            copy.wait_send()
            return c

        lax.fori_loop(1, 8, body, 0)

    def rs_start(i):
        def body(k, c):
            p = (t + k) % 8
            pltpu.make_async_remote_copy(
                src_ref=rsrc.at[i, rows_of(p)], dst_ref=land.at[i, t], send_sem=rs_s.at[i, p], recv_sem=rs_r.at[i, t],
                device_id={"tensor": p}, device_id_type=MESH,
            ).start()
            return c

        lax.fori_loop(1, 8, body, 0)

    def rs_sum(i):
        acc_rows = rsrc[i, my_rows, :].astype(F32)

        def body(k, total):
            p = (t + k) % 8
            copy = pltpu.make_async_remote_copy(
                src_ref=rsrc.at[i, rows_of(p)], dst_ref=land.at[i, p], send_sem=rs_s.at[i, p], recv_sem=rs_r.at[i, p],
                device_id={"tensor": p}, device_id_type=MESH,
            )
            copy.wait_recv()
            copy.wait_send()
            return total + land[i, p].astype(F32)

        return lax.fori_loop(1, 8, body, acc_rows)

    def allowed_of(j):
        rows = lax.broadcasted_iota(jnp.int32, (ROWS, ROWS), 0) + d * ROWS
        cols = lax.broadcasted_iota(jnp.int32, (ROWS, ROWS), 1) + j * ROWS
        return (cols <= rows) & (cols >= beg_ref[...][:, 0:1])

    weight_ready(0, 7)
    x_copy.wait()

    def first_norm(i, c):
        rows = pl.ds(pl.multiple_of(i * OWN, OWN), OWN)
        v = df[rows, :].astype(F32)
        n1[0, rows, :] = (v * factor_of(v) * gains[0, 0:1, :]).astype(BF16)
        return c

    lax.fori_loop(0, ROWS // OWN, first_norm, 0)
    x_own[0] = df[my_rows, :].astype(F32)
    ct_copy.start()

    def forward_layer(layer, c):
        @pl.when(layer == 1)
        def _():
            weight_ready(1, 7)
            v = x_own[1]
            n1[1, my_rows, :] = (v * factor_of(v) * gains[1, 0:1, :]).astype(BF16)
            ag_start(n1.at[1], 0)
            ag_wait(n1.at[1], 0)

        weight_ready(layer, 0, 1, 2)
        raw = dot_nt(n1[layer], wqkv[layer])
        c0, c1, c2 = raw[:, 0:128], raw[:, 128:256], raw[:, 256:384]
        lane = lanes_of(c0)
        q1 = jnp.where(lane < 32, pltpu.roll(c0, 32, 1), pltpu.roll(c1, 32, 1))
        k0 = jnp.where(lane < 64, pltpu.roll(c1, 64, 1), pltpu.roll(c2, 64, 1))
        v0 = pltpu.roll(c2, 96, 1)
        cosine, sine = cos_ref[...], sin_ref[...]
        for h, part in ((0, c0), (1, q1)):
            turned = part * cosine + swapped(part) * sine
            q2[layer, pl.ds(h * ROWS, ROWS), :] = turned[:, 0:HD].astype(BF16)
            q2t[layer, :, pl.ds(h * ROWS, ROWS)] = jnp.transpose(turned)[0:HD, :].astype(BF16)
        turned = k0 * cosine + swapped(k0) * sine
        kv[layer, d, pl.ds(0, HD), :] = jnp.transpose(turned)[0:HD, :].astype(BF16)
        kv[layer, d, pl.ds(HD, HD), :] = jnp.transpose(v0)[0:HD, :].astype(BF16)

        def kv_copy(owner, to):
            return pltpu.make_async_remote_copy(
                src_ref=kv.at[layer, owner], dst_ref=kv.at[layer, owner], send_sem=kv_s.at[to], recv_sem=kv_r.at[owner, layer],
                device_id={"dp": to}, device_id_type=MESH,
            )

        def kv_send(k, c):
            kv_copy(d, k).start()
            return c

        lax.fori_loop(d + 1, 8, kv_send, 0)
        s_m[...] = jnp.full(s_m.shape, MASKED, F32)
        stat_l[layer] = jnp.zeros((2 * ROWS, 1), F32)
        acc[...] = jnp.zeros(acc.shape, F32)

        def attend(i, c):
            j = d - i

            @pl.when(i > 0)
            def _():
                kv_copy(j, d).wait_recv()

            allowed = allowed_of(j)
            for h in range(2):
                rows = pl.ds(h * ROWS, ROWS)
                s = dot(q2[layer, rows, :], kv[layer, j, pl.ds(0, HD), :]) * SCALE
                s = jnp.where(allowed, s, MASKED)
                old = s_m[rows, :]
                new = jnp.maximum(old, jnp.max(s, axis=-1, keepdims=True))
                p = jnp.exp(s - new)
                shrink = jnp.exp(old - new)
                s_m[rows, :] = new
                stat_l[layer, rows, :] = stat_l[layer, rows, :] * shrink + jnp.sum(p, axis=-1, keepdims=True)
                acc[rows, :] = acc[rows, :] * shrink + dot_nt(p.astype(BF16), kv[layer, j, pl.ds(HD, HD), :])
            return c

        lax.fori_loop(0, d + 1, attend, 0)
        total = stat_l[layer]
        mixed = acc[...] / total
        o_f[layer] = mixed
        o_b[layer] = mixed.astype(BF16)
        stat_m[layer] = s_m[...] + jnp.log(total)

        def kv_sent(k, c):
            kv_copy(d, k).wait_send()
            return c

        weight_ready(layer, 3)

        def out_part(n, c):
            cols = pl.ds(pl.multiple_of(n * 512, 512), 512)
            part = dot(o_b[layer, pl.ds(0, ROWS), :], wo[layer, pl.ds(0, HD), cols])
            part += dot(o_b[layer, pl.ds(ROWS, ROWS), :], wo[layer, pl.ds(HD, HD), cols])
            rsrc[0, :, cols] = part.astype(BF16)
            return c

        lax.fori_loop(0, 3, out_part, 0)
        rs_start(0)
        lax.fori_loop(d + 1, 8, kv_sent, 0)
        v = x_own[layer] + rs_sum(0)
        h_own[layer] = v
        n2[layer, my_rows, :] = (v * factor_of(v) * gains[layer, 8:9, :]).astype(BF16)
        ag_start(n2.at[layer], 1)
        ag_wait(n2.at[layer], 1)
        weight_ready(layer, 4, 5)

        def units(n, c):
            cols = pl.ds(pl.multiple_of(n * 256, 256), 256)
            upper = pl.ds(pl.multiple_of(n * 256 + FF, 256), 256)
            g = dot(n2[layer], wgu[layer, :, cols])
            up = dot(n2[layer], wgu[layer, :, upper])
            gate_s[layer, :, cols] = g
            up_s[layer, :, cols] = up
            u_s[layer, :, cols] = (g * jax.nn.sigmoid(g) * up).astype(BF16)
            return c

        lax.fori_loop(0, 2, units, 0)
        weight_ready(layer, 6)

        def down_part(n, c):
            cols = pl.ds(pl.multiple_of(n * 512, 512), 512)
            rsrc[1, :, cols] = dot(u_s[layer], wd[layer, :, cols]).astype(BF16)
            return c

        lax.fori_loop(0, 3, down_part, 0)
        rs_start(1)
        y = (h_own[layer] + rs_sum(1)).astype(BF16)
        yb[layer] = y

        @pl.when(layer == 0)
        def _():
            x_own[1] = y.astype(F32)

        row_out(layer, yb, y_out, 0)
        return c

    def row_out(layer, buf, out, i):
        @pl.when(layer == sec)
        def _():
            pltpu.make_async_copy(buf.at[layer], out.at[sec], out_l.at[i]).start()

        @pl.when(layer != sec)
        def _():
            pltpu.make_async_remote_copy(
                src_ref=buf.at[layer], dst_ref=out.at[sec], send_sem=out_s.at[i], recv_sem=out_r.at[i],
                device_id={"section": other}, device_id_type=MESH,
            ).start()

    def row_out_wait(buf, out, i):
        pltpu.make_async_copy(buf.at[sec], out.at[sec], out_l.at[i]).wait()
        copy = pltpu.make_async_remote_copy(
            src_ref=buf.at[other], dst_ref=out.at[other], send_sem=out_s.at[i], recv_sem=out_r.at[i],
            device_id={"section": other}, device_id_type=MESH,
        )
        copy.wait_send()
        copy.wait_recv()

    lax.fori_loop(0, 2, forward_layer, 0)

    ct_copy.wait()

    before, after = (z + 3) % 4, (z + 1) % 4
    far = (z + 2) % 4
    upper, lower = pl.ds(0, 288), pl.ds(288, 288)

    def dp_at(zz, xx):
        return zz * 2 + xx

    def swap_cores(layer, i):
        buf, landing = ((ga, da_in), (gb, db_in))[i]
        return pltpu.make_async_remote_copy(
            src_ref=buf.at[layer, other], dst_ref=landing.at[layer], send_sem=ds_s.at[i, layer], recv_sem=ds_r.at[i, layer],
            device_id={"section": other}, device_id_type=MESH,
        )

    def add_rows(target, index, rows, sources, count):
        first, size = rows

        def add(n, carry):
            here = pl.ds(pl.multiple_of(first + n * count, 16), count)
            total = target[(*index, here)].astype(F32)
            for ref, place, start in sources:
                total += ref[(*place, pl.ds(pl.multiple_of(start + n * count, 16), count))].astype(F32)
            target[(*index, here)] = total.astype(BF16)
            return carry

        lax.fori_loop(0, size // count, add, 0)

    def z_piece(layer, piece, chunk, rows, to):
        return pltpu.make_async_remote_copy(
            src_ref=ga.at[layer, sec, chunk, rows], dst_ref=za.at[layer, piece], send_sem=z_s.at[layer, piece],
            recv_sem=z_r.at[layer, piece], device_id={"dp": dp_at(to, xh)}, device_id_type=MESH,
        )

    def ffn_1(layer):
        swap_cores(layer, 0).wait_recv()
        for chunk, sends in (
            (far, ((0, upper, after), (1, lower, before))),
            (after, ((2, lower, after),)),
            (before, ((3, upper, before),)),
            (z, ()),
        ):
            add_rows(ga, (layer, sec, chunk), (0, 576), [(da_in, (layer, chunk), 0)], 96)
            for piece, rows, to in sends:
                z_piece(layer, piece, chunk, rows, to).start()

    def ffn_2(layer):
        z_piece(layer, 0, far, upper, after).wait_recv()
        add_rows(ga, (layer, sec, after), (0, 288), [(za, (layer, 0), 0)], 96)
        z_piece(layer, 4, after, upper, after).start()
        z_piece(layer, 1, far, lower, before).wait_recv()
        add_rows(ga, (layer, sec, before), (288, 288), [(za, (layer, 1), 0)], 96)
        z_piece(layer, 5, before, lower, before).start()

    def x_over(layer):
        return pltpu.make_async_remote_copy(
            src_ref=ga.at[layer, sec, z, pl.ds((1 - xh) * 288, 288)], dst_ref=xa.at[layer], send_sem=x_s.at[0, layer],
            recv_sem=x_r.at[0, layer], device_id={"dp": dp_at(z, 1 - xh)}, device_id_type=MESH,
        )

    def x_back(layer, which):
        part = fa.at[layer, pl.ds(which * 288, 288)]
        return pltpu.make_async_remote_copy(
            src_ref=part, dst_ref=part, send_sem=x_s.at[1, layer], recv_sem=x_r.at[1, layer],
            device_id={"dp": dp_at(z, 1 - xh)}, device_id_type=MESH,
        )

    def ffn_3(layer):
        for piece in (2, 3, 4, 5):
            z_piece(layer, piece, z, upper, after).wait_recv()
        add_rows(ga, (layer, sec, z), (0, 288), [(za, (layer, 3), 0), (za, (layer, 4), 0)], 96)
        add_rows(ga, (layer, sec, z), (288, 288), [(za, (layer, 2), 0), (za, (layer, 5), 0)], 96)
        x_over(layer).start()

    def ffn_4(layer):
        x_over(layer).wait_recv()

        def add(n, carry):
            here = pl.ds(pl.multiple_of(n * 96, 16), 96)
            there = pl.ds(pl.multiple_of(xh * 288 + n * 96, 16), 96)
            fa[layer, there, :] = (ga[layer, sec, z, there, :].astype(F32) + xa[layer, here, :].astype(F32)).astype(BF16)
            return carry

        lax.fori_loop(0, 3, add, 0)
        x_back(layer, xh).start()

    def spread(layer, half, chunk, to, i):
        return pltpu.make_async_remote_copy(
            src_ref=fa.at[layer], dst_ref=ga_out.at[half, chunk], send_sem=a_s.at[layer, i], recv_sem=a_r.at[half, chunk],
            device_id={"section": layer, "dp": dp_at(to, xh)}, device_id_type=MESH,
        )

    def keep(layer):
        return pltpu.make_async_copy(fa.at[layer], ga_out.at[sec, z], a_l)

    def ffn_5(layer):
        x_back(layer, 1 - xh).wait_recv()
        spread(layer, sec, z, after, 0).start()
        spread(layer, sec, z, before, 1).start()

        @pl.when(layer == sec)
        def _():
            keep(layer).start()

        @pl.when(layer != sec)
        def _():
            spread(layer, sec, z, z, 2).start()

    def pass_on(half, i, chunk, rows, to):
        part = ga_out.at[half, chunk, rows]
        return pltpu.make_async_remote_copy(
            src_ref=part, dst_ref=part, send_sem=f_s.at[half, i], recv_sem=f_r.at[half, i],
            device_id={"dp": dp_at(to, xh)}, device_id_type=MESH,
        )

    def ffn_6():
        for half in range(2):
            spread(sec, half, before, z, 0).wait_recv()
            pass_on(half, 0, before, upper, after).start()
            spread(sec, half, after, z, 0).wait_recv()
            pass_on(half, 1, after, lower, before).start()

    def ffn_7():
        keep(sec).wait()
        spread(sec, other, z, z, 2).wait_recv()
        for half in range(2):
            pass_on(half, 0, far, upper, z).wait_recv()
            pass_on(half, 1, far, lower, z).wait_recv()
            pass_on(half, 0, before, upper, after).wait_send()
            pass_on(half, 1, after, lower, before).wait_send()
        spread(other, sec, z, z, 2).wait_send()
        for layer in range(2):
            swap_cores(layer, 0).wait_send()
            for piece in range(6):
                z_piece(layer, piece, z, upper, after).wait_send()
            x_over(layer).wait_send()
            x_back(layer, xh).wait_send()
            spread(layer, sec, z, after, 0).wait_send()
            spread(layer, sec, z, before, 1).wait_send()

    def b_piece(layer, to, sender):
        return pltpu.make_async_remote_copy(
            src_ref=gb.at[layer, sec, to // 2, pl.ds((to % 2) * 144, 144)], dst_ref=rb.at[layer, sender],
            send_sem=b_s.at[layer, to], recv_sem=b_r.at[layer, sender], device_id={"dp": to}, device_id_type=MESH,
        )

    def b_spread(layer, half, to, sender):
        return pltpu.make_async_remote_copy(
            src_ref=fb.at[layer], dst_ref=gb_out.at[half, sender // 2, pl.ds((sender % 2) * 144, 144)],
            send_sem=e_s.at[layer, to], recv_sem=e_r.at[half, sender], device_id={"section": layer, "dp": to},
            device_id_type=MESH,
        )

    def b_keep(layer):
        return pltpu.make_async_copy(fb.at[layer], gb_out.at[sec, z, pl.ds(xh * 144, 144)], e_l)

    def attn_1(layer):
        swap_cores(layer, 1).wait_recv()
        for chunk in (far, after, before, z):
            add_rows(gb, (layer, sec, chunk), (0, 288), [(db_in, (layer, chunk), 0)], 144)

        def send(k, c):
            b_piece(layer, (d + k) % 8, d).start()
            return c

        lax.fori_loop(1, 8, send, 0)

    def attn_2(layer):
        def take(k, total):
            p = (d + k) % 8
            b_piece(layer, d, p).wait_recv()
            return total + rb[layer, p].astype(F32)

        mine = gb[layer, sec, z, pl.ds(pl.multiple_of(xh * 144, 16), 144), :].astype(F32)
        fb[layer] = lax.fori_loop(1, 8, take, mine).astype(BF16)

        def send(k, c):
            b_spread(layer, sec, (d + k) % 8, d).start()
            return c

        lax.fori_loop(1, 8, send, 0)

        @pl.when(layer == sec)
        def _():
            b_keep(layer).start()

        @pl.when(layer != sec)
        def _():
            b_spread(layer, sec, d, d).start()

    def attn_3():
        b_keep(sec).wait()
        b_spread(sec, other, d, d).wait_recv()
        b_spread(other, sec, d, d).wait_send()

        def finish(k, c):
            p = (d + k) % 8
            b_spread(sec, 0, d, p).wait_recv()
            b_spread(sec, 1, d, p).wait_recv()
            for layer in range(2):
                b_piece(layer, p, d).wait_send()
                b_spread(layer, sec, p, d).wait_send()
            return c

        lax.fori_loop(1, 8, finish, 0)
        for layer in range(2):
            swap_cores(layer, 1).wait_send()

    def backward_layer(step, c):
        layer = 1 - step

        @pl.when(layer == 0)
        def _():
            ag_start(df, 2)

            attn_1(1)
            ffn_4(1)
            ag_wait(df, 2)

        dy = df[my_rows, :].astype(F32)
        dxb[layer] = dy

        def unit_grads(n, c):
            cols = pl.ds(pl.multiple_of(n * 256, 256), 256)
            upper = pl.ds(pl.multiple_of(n * 256 + FF, 256), 256)
            du = dot_nt(df[...], wd[layer, cols, :])
            g, up = gate_s[layer, :, cols], up_s[layer, :, cols]
            sig = jax.nn.sigmoid(g)
            dgu[:, cols] = (du * up * sig * (1.0 + g * (1.0 - sig))).astype(BF16)
            dgu[:, upper] = (du * g * sig).astype(BF16)
            return c

        lax.fori_loop(0, 2, unit_grads, 0)

        def normed_part(n, c):
            cols = pl.ds(pl.multiple_of(n * 256, 256), 256)
            rsrc[0, :, cols] = dot_nt(dgu[...], wgu[layer, cols, :]).astype(BF16)
            return c

        lax.fori_loop(0, 6, normed_part, 0)
        rs_start(0)

        def unit_weights(n, c):
            cols = pl.ds(pl.multiple_of(n * 384, 384), 384)
            got = dot_tn(n2[layer, :, cols], dgu[...]).astype(BF16)
            for h in range(2):
                ga[layer, h, n, pl.ds(0, 192), :] = got[192 * h : 192 * h + 192, 0:FF]
                ga[layer, h, n, pl.ds(192, 192), :] = got[192 * h : 192 * h + 192, FF : 2 * FF]
            cols = pl.ds(pl.multiple_of(n * 128, 128), 128)
            got = dot_tn(u_s[layer, :, cols], df[...]).astype(BF16)
            for h in range(2):
                for i in range(3):
                    ga[layer, h, n, pl.ds(384 + 64 * i, 64), :] = got[64 * h : 64 * h + 64, 512 * i : 512 * i + 512]
            return c

        lax.fori_loop(0, 4, unit_weights, 0)
        swap_cores(layer, 0).start()

        @pl.when(step == 1)
        def _():
            ffn_5(1)
            attn_2(1)

        dn = rs_sum(0)
        h = h_own[layer]
        r = factor_of(h)
        tt = dn * gains[layer, 8:9, :]
        dh = dxb[layer] + r * tt - h * (r * r * r * jnp.mean(h * tt, axis=-1, keepdims=True))
        dgain[layer, 1:2, :] = jnp.sum(dn * h * r, axis=0, keepdims=True)
        dxb[layer] = dh
        da[my_rows, :] = dh.astype(BF16)
        ag_start(da, 3)
        ffn_1(layer)

        @pl.when((step == 1) & (sec == 1))
        def _():
            ffn_6()

        ag_wait(da, 3)
        for h in range(2):
            rows = pl.ds(h * ROWS, ROWS)
            got = dot_nt(da[...], wo[layer, pl.ds(h * HD, HD), :])
            do2[rows, :] = got.astype(BF16)
            padded = jnp.concatenate([got, jnp.zeros((ROWS, 128 - HD), F32)], axis=1)
            do2t[:, rows] = jnp.transpose(padded)[0:HD, :].astype(BF16)
        dot_rows = jnp.sum(do2[...].astype(F32) * o_f[layer], axis=-1, keepdims=True)
        s_m[...] = dot_rows
        acc[...] = jnp.zeros(acc.shape, F32)

        def dkv_copy(to, sender):
            return pltpu.make_async_remote_copy(
                src_ref=dkv_src.at[to], dst_ref=dkv_land.at[layer, sender], send_sem=dkv_s.at[to], recv_sem=dkv_r.at[layer, sender],
                device_id={"dp": to}, device_id_type=MESH,
            )

        def attend_back(j, c):
            allowed = allowed_of(j)
            dkt = jnp.zeros((HD, ROWS), F32)
            dvt = jnp.zeros((HD, ROWS), F32)
            for h in range(2):
                rows = pl.ds(h * ROWS, ROWS)
                kt = kv[layer, j, pl.ds(0, HD), :]
                s = dot(q2[layer, rows, :], kt) * SCALE
                p = jnp.exp(jnp.where(allowed, s, MASKED) - stat_m[layer, rows, :])
                dp = dot(do2[rows, :], kv[layer, j, pl.ds(HD, HD), :])
                ds = (p * (dp - s_m[rows, :])).astype(BF16)
                acc[rows, :] += dot_nt(ds, kt)
                dkt += dot(q2t[layer, :, rows], ds)
                dvt += dot(do2t[:, rows], p.astype(BF16))
            dkv_src[j, pl.ds(0, HD), :] = (dkt * SCALE).astype(BF16)
            dkv_src[j, pl.ds(HD, HD), :] = dvt.astype(BF16)

            @pl.when(j < d)
            def _():
                dkv_copy(j, d).start()

            return c

        lax.fori_loop(0, d + 1, attend_back, 0)

        def dkv_sent(k, c):
            dkv_copy(k, d).wait_send()
            return c

        def out_weights(n, c):
            cols = pl.ds(pl.multiple_of(n * 384, 384), 384)
            for h in range(2):
                got = dot_tn(o_b[layer, pl.ds(h * ROWS, ROWS), :], da[:, cols])
                gb[layer, 0, n, pl.ds(h * HD, HD), :] = got.astype(BF16)
            return c

        lax.fori_loop(0, 4, out_weights, 0)
        lax.fori_loop(0, d, dkv_sent, 0)

        ffn_2(layer)

        def dkv_sum(k, total):
            dkv_copy(d, k).wait_recv()
            return total + dkv_land[layer, k].astype(F32)

        dkv_total = lax.fori_loop(d + 1, 8, dkv_sum, dkv_src[d].astype(F32))
        dkv_t[...] = jnp.zeros(dkv_t.shape, F32)
        dkv_t[0, pl.ds(0, HD), :] = dkv_total[0:HD]
        dkv_t[1, pl.ds(0, HD), :] = dkv_total[HD : 2 * HD]
        dk_rot = jnp.transpose(dkv_t[0])
        dv = jnp.transpose(dkv_t[1])
        cosine, sine = cos_ref[...], sin_ref[...]
        dq[...] = jnp.zeros(dq.shape, F32)
        dq[:, 0:HD] = acc[...] * SCALE
        dq0, dq1 = dq[pl.ds(0, ROWS), :], dq[pl.ds(ROWS, ROWS), :]
        dq0 = dq0 * cosine - swapped(dq0) * sine
        dq1 = dq1 * cosine - swapped(dq1) * sine
        dk = dk_rot * cosine - swapped(dk_rot) * sine
        lane = lanes_of(dk)
        dqkv[:, 0:128] = jnp.where(lane < HD, dq0, pltpu.roll(dq1, 96, 1)).astype(BF16)
        dqkv[:, 128:256] = jnp.where(lane < 64, pltpu.roll(dq1, 96, 1), pltpu.roll(dk, 64, 1)).astype(BF16)
        dqkv[:, 256:384] = jnp.where(lane < 32, pltpu.roll(dk, 64, 1), pltpu.roll(dv, 32, 1)).astype(BF16)

        def input_part(n, c):
            cols = pl.ds(pl.multiple_of(n * 256, 256), 256)
            rsrc[1, :, cols] = dot(dqkv[...], wqkv[layer, :, cols]).astype(BF16)
            return c

        lax.fori_loop(0, 6, input_part, 0)
        rs_start(1)

        def qkv_weights(n, c):
            cols = pl.ds(pl.multiple_of(n * 384, 384), 384)
            got = dot_tn(dqkv[...], n1[layer, :, cols]).astype(BF16)
            gb[layer, 0, n, pl.ds(2 * HD, HD), :] = got[0:HD]
            gb[layer, 1, n] = got[HD : 4 * HD]
            return c

        lax.fori_loop(0, 4, qkv_weights, 0)
        swap_cores(layer, 1).start()
        ffn_3(layer)
        dn = rs_sum(1)
        v = x_own[layer]
        r = factor_of(v)
        tt = dn * gains[layer, 0:1, :]
        dx = dxb[layer] + r * tt - v * (r * r * r * jnp.mean(v * tt, axis=-1, keepdims=True))
        dgain[layer, 0:1, :] = jnp.sum(dn * v * r, axis=0, keepdims=True)
        dxb[layer] = dx
        df[my_rows, :] = dx.astype(BF16)
        row_out(layer, dxb, dx_out, 1)
        return c

    dgain[...] = jnp.zeros(dgain.shape, F32)
    lax.fori_loop(0, 2, backward_layer, 0)

    mate = pltpu.make_async_remote_copy(
        src_ref=dgain.at[other], dst_ref=dg_peer, send_sem=ns.at[0, 0], recv_sem=nr.at[0, 0],
        device_id={"section": other}, device_id_type=MESH,
    )
    mate.start()
    ffn_4(0)
    attn_1(0)

    def gain_copy(axis, i, buf, me, to, sender):
        return pltpu.make_async_remote_copy(
            src_ref=buf.at[me], dst_ref=buf.at[sender], send_sem=ns.at[i, to], recv_sem=nr.at[i, sender],
            device_id={axis: to}, device_id_type=MESH,
        )

    def gain_round(axis, i, buf, me):
        def send(k, c):
            gain_copy(axis, i, buf, me, (me + k) % 8, me).start()
            return c

        def take(k, total):
            p = (me + k) % 8
            gain_copy(axis, i, buf, me, p, p).wait_recv()
            return total + buf[p]

        def sent(k, c):
            gain_copy(axis, i, buf, me, (me + k) % 8, me).wait_send()
            return c

        lax.fori_loop(1, 8, send, 0)
        total = lax.fori_loop(1, 8, take, buf[me])
        lax.fori_loop(1, 8, sent, 0)
        return total

    mate.wait_recv()
    mate.wait_send()
    dg_t[t] = dgain[sec] + dg_peer[...]
    ffn_5(0)
    dg_d[d] = gain_round("tensor", 1, dg_t, t)
    attn_2(0)

    @pl.when(sec == 0)
    def _():
        ffn_6()

    gn_out[...] = gain_round("dp", 2, dg_d, d)
    attn_3()
    ffn_7()
    row_out_wait(yb, y_out, 0)
    row_out_wait(dxb, dx_out, 1)
    for i in range(n_parts):
        sent_parts[i].wait_send()


def step_call(*args):
    hbm = pl.BlockSpec(memory_space=pl.ANY)
    vmem = pl.BlockSpec(memory_space=pltpu.VMEM)
    dma = pltpu.SemaphoreType.DMA
    scratch = [
        pltpu.VMEM((2, 384, D), BF16), pltpu.VMEM((2, 192, D), BF16), pltpu.VMEM((2, D, 2 * FF), BF16),
        pltpu.VMEM((2, FF, D), BF16), pltpu.VMEM((2, 16, D), F32), pltpu.VMEM((ROWS, D), BF16),
        pltpu.VMEM((2, ROWS, D), BF16), pltpu.VMEM((2, ROWS, D), BF16), pltpu.VMEM((2, 2 * ROWS, HD), BF16),
        pltpu.VMEM((2, HD, 2 * ROWS), BF16), pltpu.VMEM((2, 8, 2 * HD, ROWS), BF16), pltpu.VMEM((2, 2 * ROWS, HD), F32),
        pltpu.VMEM((2, 2 * ROWS, HD), BF16), pltpu.VMEM((2, 2 * ROWS, 1), F32), pltpu.VMEM((2, 2 * ROWS, 1), F32),
        pltpu.VMEM((2, ROWS, FF), F32), pltpu.VMEM((2, ROWS, FF), F32), pltpu.VMEM((2, ROWS, FF), BF16),
        pltpu.VMEM((2, OWN, D), F32), pltpu.VMEM((2, OWN, D), F32),
        pltpu.VMEM((2, ROWS, D), BF16), pltpu.VMEM((2, 8, OWN, D), BF16), pltpu.VMEM((ROWS, D), BF16),
        pltpu.VMEM((2 * ROWS, HD), BF16), pltpu.VMEM((HD, 2 * ROWS), BF16), pltpu.VMEM((ROWS, 2 * FF), BF16),
        pltpu.VMEM((2 * ROWS, 128), F32), pltpu.VMEM((ROWS, 384), BF16), pltpu.VMEM((2, 128, ROWS), F32),
        pltpu.VMEM((8, 2 * HD, ROWS), BF16), pltpu.VMEM((2, 8, 2 * HD, ROWS), BF16), pltpu.VMEM((2 * ROWS, HD), F32),
        pltpu.VMEM((2 * ROWS, 1), F32),
        pltpu.VMEM((2, 2, 4, 576, 512), BF16), pltpu.VMEM((2, 2, 4, 288, 384), BF16), pltpu.VMEM((2, 4, 576, 512), BF16),
        pltpu.VMEM((2, 4, 288, 384), BF16), pltpu.VMEM((2, 6, 288, 512), BF16), pltpu.VMEM((2, 8, 144, 384), BF16),
        pltpu.VMEM((2, 288, 512), BF16), pltpu.VMEM((2, 576, 512), BF16), pltpu.VMEM((2, 144, 384), BF16),
        pltpu.VMEM((2, OWN, D), BF16), pltpu.VMEM((2, OWN, D), F32), pltpu.VMEM((2, 8, D), F32), pltpu.VMEM((8, D), F32),
        pltpu.VMEM((8, 8, D), F32), pltpu.VMEM((8, 8, D), F32),
        dma((10,)), dma((8,)), dma((8,)), dma((4, 8)), dma((4, 8)), dma((2, 8)), dma((2, 8)), dma((8,)), dma((8, 2)),
        dma((8,)), dma((2, 8)), dma((2,)), dma((2,)), dma((2,)),
        dma((2, 2)), dma((2, 2)), dma((2, 6)), dma((2, 6)), dma((2, 2)), dma((2, 2)), dma((2, 3)), dma((2, 4)), dma,
        dma((2, 2)), dma((2, 2)), dma((2, 8)), dma((2, 8)), dma((2, 8)), dma((2, 8)), dma, dma((3, 8)), dma((3, 8)),
    ]
    return pl.pallas_call(
        kernel,
        out_shape=(
            jax.ShapeDtypeStruct((2, OWN, D), BF16),
            jax.ShapeDtypeStruct((2, OWN, D), F32),
            jax.ShapeDtypeStruct((2, 4, 576, 512), BF16),
            jax.ShapeDtypeStruct((2, 4, 288, 384), BF16),
            jax.ShapeDtypeStruct((8, D), F32),
        ),
        in_specs=[hbm] * 10 + [vmem] * 3,
        out_specs=(hbm, hbm, hbm, hbm, vmem),
        scratch_shapes=scratch,
        compiler_params=pltpu.CompilerParams(
            collective_id=0, has_side_effects=True, vmem_limit_bytes=64 * 1024 * 1024 - 65536
        ),
        name="train_step",
    )(*args)


def widen(ga_ref, gb_ref, gate_ref, up_ref, down_ref, out_ref, query_ref, key_ref, value_ref):
    for h in range(2):
        rows = pl.ds(192 * h, 192)
        gate_ref[rows, :] = ga_ref[h, 0, 0:192, :].astype(F32)
        up_ref[rows, :] = ga_ref[h, 0, 192:384, :].astype(F32)
        for i in range(3):
            down_ref[pl.ds(64 * h, 64), pl.ds(512 * i, 512)] = ga_ref[h, 0, 384 + 64 * i : 448 + 64 * i, :].astype(F32)
    out_ref[...] = gb_ref[0, 0, 0:192, :].astype(F32)
    query_ref[0:HD, :] = gb_ref[0, 0, 192:288, :].astype(F32)
    query_ref[HD : 2 * HD, :] = gb_ref[1, 0, 0:HD, :].astype(F32)
    key_ref[...] = gb_ref[1, 0, HD : 2 * HD, :].astype(F32)
    value_ref[...] = gb_ref[1, 0, 2 * HD : 3 * HD, :].astype(F32)


def widened(ga, gb):
    shapes = [(D, FF), (D, FF), (FF, D), (192, D), (192, D), (HD, D), (HD, D)]
    by_row = [pl.BlockSpec((384, FF), lambda c: (c, 0)), pl.BlockSpec((384, FF), lambda c: (c, 0)), pl.BlockSpec((128, D), lambda c: (c, 0))]
    by_column = [pl.BlockSpec((rows, 384), lambda c: (0, c)) for rows in (192, 192, HD, HD)]
    return pl.pallas_call(
        widen,
        grid=(4,),
        out_shape=tuple(jax.ShapeDtypeStruct(shape, F32) for shape in shapes),
        in_specs=[pl.BlockSpec((2, 1, 576, 512), lambda c: (0, c, 0, 0)), pl.BlockSpec((2, 1, 288, 384), lambda c: (0, c, 0, 0))],
        out_specs=tuple(by_row + by_column),
        compiler_params=pltpu.CompilerParams(vmem_limit_bytes=40 * 1024 * 1024),
        name="widen",
    )(ga, gb)


def on_device(inputs, cotangent, doc_lengths, norm_one, query_w, key_w, value_w, out_w, norm_two, gate_w, up_w, down_w):
    gains = jnp.concatenate([jnp.broadcast_to(norm_one, (8, D)), jnp.broadcast_to(norm_two, (8, D))]).astype(F32)
    lengths = lax.dynamic_index_in_dim(doc_lengths, lax.axis_index("section"), 0, keepdims=False)
    starts = jnp.cumsum(lengths) - lengths
    places = lax.axis_index("dp") * ROWS + jnp.arange(ROWS, dtype=jnp.int32)
    begins = jnp.max(jnp.where(starts[None, :] <= places[:, None], starts[None, :], 0), axis=1)
    inverse = jnp.exp(jnp.arange(HALF, dtype=F32) * (-2.0 * math.log(ROPE) / HD))
    angles = (places - begins).astype(F32)[:, None] * inverse[None, :]
    cosine, sine = jnp.cos(angles), jnp.sin(angles)
    rest = jnp.zeros((ROWS, 128 - HD), F32)
    cosine = jnp.concatenate([cosine, cosine, rest], axis=1)
    sine = jnp.concatenate([-sine, sine, rest], axis=1)
    begins = jnp.broadcast_to(begins[:, None], (ROWS, 128))
    y, dx, ga, gb, gn = step_call(
        inputs, cotangent, query_w[0].T, key_w[0].T, value_w[0].T, out_w[0], gate_w[0], up_w[0], down_w[0], gains, cosine, sine, begins
    )
    gate, up, down, out, query, key, value = widened(ga, gb)
    return (
        y[None], dx[None], gn[0:1], query.T[None], key.T[None], value.T[None], out[None], gn[1:2], gate[None], up[None], down[None],
    )


def solution(mesh):
    in_specs = (
        P(None, "dp", None),
        P(None, "dp", None),
        P(),
        P("section", None),
        P("section", None, "tensor"),
        P("section", None, "tensor"),
        P("section", None, "tensor"),
        P("section", "tensor", None),
        P("section", None),
        P("section", None, "tensor"),
        P("section", None, "tensor"),
        P("section", "tensor", None),
    )
    out_specs = (
        P("section", None, ("dp", "tensor"), None),
        P("section", None, ("dp", "tensor"), None),
        P("section", None),
        P("section", None, "tensor"),
        P("section", None, "tensor"),
        P("section", None, "tensor"),
        P("section", "tensor", None),
        P("section", None),
        P("section", None, "tensor"),
        P("section", None, "tensor"),
        P("section", "tensor", None),
    )
    return jax.shard_map(on_device, mesh=mesh, in_specs=in_specs, out_specs=out_specs, check_vma=False)
```

```python
import math

import jax
import jax.numpy as jnp
from jax import lax
from jax.experimental import pallas as pl
from jax.experimental.pallas import tpu as pltpu
from jax.sharding import PartitionSpec as P

MESH = pl.DeviceIdType.MESH
F32 = jnp.float32
BF16 = jnp.bfloat16

HD = 96
HALF = HD // 2
D = 1536
FF = 512
ROWS = 256
OWN = 32
HROWS = 128
HOWN = 16
SCALE = 1.0 / math.sqrt(HD)
EPS = 1e-05
ROPE = 100000.0
MASKED = -1e30


def dot(a, b):
    return lax.dot_general(a, b, (((1,), (0,)), ((), ())), preferred_element_type=F32)


def dot_nt(a, b):
    return lax.dot_general(a, b, (((1,), (1,)), ((), ())), preferred_element_type=F32)


def dot_tn(a, b):
    return lax.dot_general(a, b, (((0,), (0,)), ((), ())), preferred_element_type=F32)


def lanes_of(v):
    return lax.broadcasted_iota(jnp.int32, v.shape, 1)


def swapped(v):
    return jnp.where(lanes_of(v) < HALF, pltpu.roll(v, 128 - HALF, 1), pltpu.roll(v, HALF, 1))


def factor_of(v):
    return lax.rsqrt(jnp.mean(v * v, axis=-1, keepdims=True) + EPS)


def kernel(
    x_hbm, ct_hbm, wq_hbm, wk_hbm, wv_hbm, wo_hbm, wg_hbm, wu_hbm, wd_hbm, gains_hbm, cos_ref, sin_ref, beg_ref,
    y_out, dx_out, ga_out, gb_out, gn_out,
    wqkv, wo, wgu, wd, gains, df,
    n1, n2, q2, q2t, kv, o_f, o_b, stat_m, stat_l, gate_s, up_s, u_s, x_own, h_own,
    rsrc, land, da, do2, do2t, dgu, dq, dqkv, dkv_t, dkv_src, dkv_land, acc, s_m,
    ga, gb, da_in, db_in, za, rb, xa, fa, fb, yb, dxb, dgain, dg_peer, dg_t, dg_d,
    w_l, w_s, w_r, ag_s, ag_r, rs_s, rs_r, kv_s, kv_r, dkv_s, dkv_r, out_l, out_s, out_r,
    ds_s, ds_r, z_s, z_r, x_s, x_r, a_s, a_r, a_l, f_s, f_r, b_s, b_r, e_s, e_r, e_l, ns, nr,
):
    sec = lax.axis_index("section")
    t = lax.axis_index("tensor")
    d = lax.axis_index("dp")
    other = 1 - sec
    z, xh = d // 2, d % 2

    barrier = pltpu.get_barrier_semaphore()

    def greet(axis, me, k, _):
        pl.semaphore_signal(barrier, inc=1, device_id={axis: (me + k) % 8}, device_id_type=MESH)
        return _

    pl.semaphore_signal(barrier, inc=1, device_id={"section": other}, device_id_type=MESH)
    lax.fori_loop(1, 8, lambda k, c: greet("tensor", t, k, c), 0)
    lax.fori_loop(1, 8, lambda k, c: greet("dp", d, k, c), 0)

    def load_rows(source, sem):
        def body(i, c):
            h, p = i // 8, i % 8
            pltpu.make_async_copy(
                source.at[sec, pl.ds(pl.multiple_of(p * OWN + h * HOWN, HOWN), HOWN)],
                df.at[pl.ds(pl.multiple_of(h * HROWS + p * HOWN, HOWN), HOWN)], sem,
            ).start()
            return c

        lax.fori_loop(0, 16, body, 0)

    def rows_loaded(source, sem):
        pltpu.make_async_copy(source.at[sec], df, sem).wait()

    own_parts = [
        (wq_hbm, lambda i: wqkv.at[i, pl.ds(0, 2 * HD)]),
        (wk_hbm, lambda i: wqkv.at[i, pl.ds(2 * HD, HD)]),
        (wv_hbm, lambda i: wqkv.at[i, pl.ds(3 * HD, HD)]),
        (wo_hbm, lambda i: wo.at[i]),
        (wg_hbm, lambda i: wgu.at[i, :, 0:FF]),
        (wu_hbm, lambda i: wgu.at[i, :, FF : 2 * FF]),
        (wd_hbm, lambda i: wd.at[i]),
        (gains_hbm, lambda i: gains.at[i]),
    ]
    n_parts = len(own_parts)
    own_copies = [pltpu.make_async_copy(a, b(sec), w_l.at[i]) for i, (a, b) in enumerate(own_parts)]
    load_rows(x_hbm, w_l.at[8])
    own_copies[7].start()
    for i in range(7):
        own_copies[i].start()
    pl.semaphore_wait(barrier, 15)
    sent_parts = [
        pltpu.make_async_remote_copy(
            src_ref=a, dst_ref=b(sec), send_sem=w_s.at[i], recv_sem=w_r.at[i],
            device_id={"section": other}, device_id_type=MESH,
        )
        for i, (a, b) in enumerate(own_parts)
    ]
    for i in (7, 0, 1, 2, 3, 4, 5, 6):
        sent_parts[i].start()

    def weight_ready(layer, *which):
        @pl.when(layer == sec)
        def _():
            for i in which:
                own_copies[i].wait()

        @pl.when(layer != sec)
        def _():
            for i in which:
                a, b = own_parts[i]
                pltpu.make_async_remote_copy(
                    src_ref=a, dst_ref=b(other), send_sem=w_s.at[i], recv_sem=w_r.at[i],
                    device_id={"section": other}, device_id_type=MESH,
                ).wait_recv()

    def half_rows(half):
        return pl.ds(pl.multiple_of(half * HROWS, HROWS), HROWS)

    def pair_rows(half):
        return pl.ds(pl.multiple_of(half * ROWS, ROWS), ROWS)

    def rows_of(half, owner):
        return pl.ds(pl.multiple_of(half * HROWS + owner * HOWN, HOWN), HOWN)

    def kept(half):
        return pl.ds(pl.multiple_of(half * HOWN, HOWN), HOWN)

    def over_peers(body):
        def step(k, c):
            body((t + k) % 8)
            return c

        lax.fori_loop(1, 8, step, 0)

    def ag_copy(buf, i, half, to, owner):
        rows = rows_of(half, owner)
        return pltpu.make_async_remote_copy(
            src_ref=buf.at[rows], dst_ref=buf.at[rows], send_sem=ag_s.at[i, half, to], recv_sem=ag_r.at[i, half, owner],
            device_id={"tensor": to}, device_id_type=MESH,
        )

    def ag_start(buf, i, half):
        over_peers(lambda p: ag_copy(buf, i, half, p, t).start())

    def ag_wait(buf, i, half):
        over_peers(lambda p: ag_copy(buf, i, half, t, p).wait_recv())

    def ag_sent(buf, i, half):
        over_peers(lambda p: ag_copy(buf, i, half, p, t).wait_send())

    def rs_copy(i, half, to, sender):
        return pltpu.make_async_remote_copy(
            src_ref=rsrc.at[i, rows_of(half, to)], dst_ref=land.at[i, half, sender], send_sem=rs_s.at[i, half, to],
            recv_sem=rs_r.at[i, half, sender], device_id={"tensor": to}, device_id_type=MESH,
        )

    def rs_start(i, half):
        over_peers(lambda p: rs_copy(i, half, p, t).start())

    def rs_sum(i, half):
        def body(k, total):
            p = (t + k) % 8
            rs_copy(i, half, t, p).wait_recv()
            return total + land[i, half, p].astype(F32)

        return lax.fori_loop(1, 8, body, rsrc[i, rows_of(half, t), :].astype(F32))

    def rs_sent(i, half):
        over_peers(lambda p: rs_copy(i, half, p, t).wait_send())

    def both(body):
        def step(half, c):
            body(half)
            return c

        lax.fori_loop(0, 2, step, 0)

    def place_of(i):
        return OWN * ((i // HOWN) % 8) + HOWN * (i // HROWS) + i % HOWN

    def allowed_of(j, half):
        rows = place_of(lax.broadcasted_iota(jnp.int32, (HROWS, 1), 0) + half * HROWS) + d * ROWS
        cols = place_of(lax.broadcasted_iota(jnp.int32, (1, ROWS), 1)) + j * ROWS
        allowed = (cols <= rows) & (cols >= beg_ref[half_rows(half), 0:1])
        return jnp.concatenate([jnp.where(allowed, 0.0, MASKED)] * 2, axis=0)

    weight_ready(0, 7)
    rows_loaded(x_hbm, w_l.at[8])

    def first_norm(i, c):
        rows = pl.ds(pl.multiple_of(i * OWN, OWN), OWN)
        v = df[rows, :].astype(F32)
        n1[0, rows, :] = (v * factor_of(v) * gains[0, 0:1, :]).astype(BF16)
        return c

    lax.fori_loop(0, ROWS // OWN, first_norm, 0)
    for half in range(2):
        x_own[0, kept(half), :] = df[rows_of(half, t), :].astype(F32)
    load_rows(ct_hbm, w_l.at[9])

    def forward_layer(layer, c):
        weight_ready(layer, 0, 1, 2)

        def kv_copy(owner, to, half):
            part = kv.at[layer, owner, :, half_rows(half)]
            return pltpu.make_async_remote_copy(
                src_ref=part, dst_ref=part, send_sem=kv_s.at[to, half], recv_sem=kv_r.at[owner, layer, half],
                device_id={"dp": to}, device_id_type=MESH,
            )

        def project(half):
            rows = half_rows(half)

            @pl.when(layer == 1)
            def _():
                ag_wait(n1.at[1], 0, half)

            raw = dot_nt(n1[layer, rows, :], wqkv[layer])
            c0, c1, c2 = raw[:, 0:128], raw[:, 128:256], raw[:, 256:384]
            lane = lanes_of(c0)
            q1 = jnp.where(lane < 32, pltpu.roll(c0, 32, 1), pltpu.roll(c1, 32, 1))
            k0 = jnp.where(lane < 64, pltpu.roll(c1, 64, 1), pltpu.roll(c2, 64, 1))
            v0 = pltpu.roll(c2, 96, 1)
            cosine, sine = cos_ref[rows, :], sin_ref[rows, :]
            turned = k0 * cosine + swapped(k0) * sine
            kv[layer, d, pl.ds(0, HD), rows] = jnp.transpose(turned)[0:HD, :].astype(BF16)
            kv[layer, d, pl.ds(HD, HD), rows] = jnp.transpose(v0)[0:HD, :].astype(BF16)

            def kv_send(k, c):
                kv_copy(d, k, half).start()
                return c

            lax.fori_loop(d + 1, 8, kv_send, 0)
            for h, part in ((0, c0), (1, q1)):
                turned = part * cosine + swapped(part) * sine
                place = pl.ds(pl.multiple_of(half * ROWS + h * HROWS, HROWS), HROWS)
                q2[layer, place, :] = turned[:, 0:HD].astype(BF16)
                q2t[layer, :, place] = jnp.transpose(turned)[0:HD, :].astype(BF16)

        both(project)

        @pl.when(layer == 1)
        def _():
            both(lambda half: ag_sent(n1.at[1], 0, half))

        weight_ready(layer, 3)

        def attend_half(half):
            rows = pair_rows(half)
            s_m[rows, :] = jnp.full((ROWS, 1), MASKED, F32)
            stat_l[layer, rows, :] = jnp.zeros((ROWS, 1), F32)
            acc[rows, :] = jnp.zeros((ROWS, HD), F32)

            def attend(i, c):
                j = d - i

                @pl.when((i > 0) & (half == 0))
                def _():
                    kv_copy(j, d, 0).wait_recv()
                    kv_copy(j, d, 1).wait_recv()

                s = dot(q2[layer, rows, :], kv[layer, j, pl.ds(0, HD), :]) * SCALE + allowed_of(j, half)
                old = s_m[rows, :]
                new = jnp.maximum(old, jnp.max(s, axis=-1, keepdims=True))
                p = jnp.exp(s - new)
                shrink = jnp.exp(old - new)
                s_m[rows, :] = new
                stat_l[layer, rows, :] = stat_l[layer, rows, :] * shrink + jnp.sum(p, axis=-1, keepdims=True)
                acc[rows, :] = acc[rows, :] * shrink + dot_nt(p.astype(BF16), kv[layer, j, pl.ds(HD, HD), :])
                return c

            lax.fori_loop(0, d + 1, attend, 0)
            total = stat_l[layer, rows, :]
            mixed = acc[rows, :] / total
            o_f[layer, rows, :] = mixed
            o_b[layer, rows, :] = mixed.astype(BF16)
            stat_m[layer, rows, :] = s_m[rows, :] + jnp.log(total)
            first = pl.ds(pl.multiple_of(half * ROWS, HROWS), HROWS)
            second = pl.ds(pl.multiple_of(half * ROWS + HROWS, HROWS), HROWS)

            def out_part(n, c):
                cols = pl.ds(pl.multiple_of(n * 512, 512), 512)
                part = dot(o_b[layer, first, :], wo[layer, pl.ds(0, HD), cols])
                part += dot(o_b[layer, second, :], wo[layer, pl.ds(HD, HD), cols])
                rsrc[0, half_rows(half), cols] = part.astype(BF16)
                return c

            lax.fori_loop(0, 3, out_part, 0)
            rs_start(0, half)

        both(attend_half)

        def kv_sent(k, c):
            kv_copy(d, k, 0).wait_send()
            kv_copy(d, k, 1).wait_send()
            return c

        lax.fori_loop(d + 1, 8, kv_sent, 0)

        def middle(half):
            v = x_own[layer, kept(half), :] + rs_sum(0, half)
            h_own[layer, kept(half), :] = v
            n2[layer, rows_of(half, t), :] = (v * factor_of(v) * gains[layer, 8:9, :]).astype(BF16)
            ag_start(n2.at[layer], 1, half)
            rs_sent(0, half)

        both(middle)
        weight_ready(layer, 4, 5)
        weight_ready(layer, 6)

        def feed(half):
            rows = half_rows(half)
            ag_wait(n2.at[layer], 1, half)

            def units(n, c):
                cols = pl.ds(pl.multiple_of(n * 256, 256), 256)
                above = pl.ds(pl.multiple_of(n * 256 + FF, 256), 256)
                g = dot(n2[layer, rows, :], wgu[layer, :, cols])
                up = dot(n2[layer, rows, :], wgu[layer, :, above])
                gate_s[layer, rows, cols] = g
                up_s[layer, rows, cols] = up
                u_s[layer, rows, cols] = (g * jax.nn.sigmoid(g) * up).astype(BF16)
                return c

            lax.fori_loop(0, 2, units, 0)

            def down_part(n, c):
                cols = pl.ds(pl.multiple_of(n * 512, 512), 512)
                rsrc[1, rows, cols] = dot(u_s[layer, rows, :], wd[layer, :, cols]).astype(BF16)
                return c

            lax.fori_loop(0, 3, down_part, 0)
            rs_start(1, half)
            ag_sent(n2.at[layer], 1, half)

        both(feed)

        @pl.when(layer == 0)
        def _():
            weight_ready(1, 7)

        def result(half):
            y = (h_own[layer, kept(half), :] + rs_sum(1, half)).astype(BF16)
            yb[layer, kept(half), :] = y

            @pl.when(layer == 0)
            def _():
                v = y.astype(F32)
                x_own[1, kept(half), :] = v
                n1[1, rows_of(half, t), :] = (v * factor_of(v) * gains[1, 0:1, :]).astype(BF16)
                ag_start(n1.at[1], 0, half)

            rs_sent(1, half)

        both(result)
        row_out(layer, yb, y_out, 0)
        return c

    def row_out(layer, buf, out, i):
        @pl.when(layer == sec)
        def _():
            pltpu.make_async_copy(buf.at[layer], out.at[sec], out_l.at[i]).start()

        @pl.when(layer != sec)
        def _():
            pltpu.make_async_remote_copy(
                src_ref=buf.at[layer], dst_ref=out.at[sec], send_sem=out_s.at[i], recv_sem=out_r.at[i],
                device_id={"section": other}, device_id_type=MESH,
            ).start()

    def row_out_wait(buf, out, i):
        pltpu.make_async_copy(buf.at[sec], out.at[sec], out_l.at[i]).wait()
        copy = pltpu.make_async_remote_copy(
            src_ref=buf.at[other], dst_ref=out.at[other], send_sem=out_s.at[i], recv_sem=out_r.at[i],
            device_id={"section": other}, device_id_type=MESH,
        )
        copy.wait_send()
        copy.wait_recv()

    lax.fori_loop(0, 2, forward_layer, 0)

    rows_loaded(ct_hbm, w_l.at[9])

    before, after = (z + 3) % 4, (z + 1) % 4
    far = (z + 2) % 4
    upper, lower = pl.ds(0, 288), pl.ds(288, 288)

    def dp_at(zz, xx):
        return zz * 2 + xx

    def swap_cores(layer, i):
        buf, landing = ((ga, da_in), (gb, db_in))[i]
        return pltpu.make_async_remote_copy(
            src_ref=buf.at[layer, other], dst_ref=landing.at[layer], send_sem=ds_s.at[i, layer], recv_sem=ds_r.at[i, layer],
            device_id={"section": other}, device_id_type=MESH,
        )

    def add_rows(target, index, rows, sources, count):
        first, size = rows

        def add(n, carry):
            here = pl.ds(pl.multiple_of(first + n * count, 16), count)
            total = target[(*index, here)].astype(F32)
            for ref, place, start in sources:
                total += ref[(*place, pl.ds(pl.multiple_of(start + n * count, 16), count))].astype(F32)
            target[(*index, here)] = total.astype(BF16)
            return carry

        lax.fori_loop(0, size // count, add, 0)

    def z_piece(layer, piece, chunk, rows, to):
        return pltpu.make_async_remote_copy(
            src_ref=ga.at[layer, sec, chunk, rows], dst_ref=za.at[layer, piece], send_sem=z_s.at[layer, piece],
            recv_sem=z_r.at[layer, piece], device_id={"dp": dp_at(to, xh)}, device_id_type=MESH,
        )

    def ffn_1(layer):
        swap_cores(layer, 0).wait_recv()
        for chunk, sends in (
            (far, ((0, upper, after), (1, lower, before))),
            (after, ((2, lower, after),)),
            (before, ((3, upper, before),)),
            (z, ()),
        ):
            add_rows(ga, (layer, sec, chunk), (0, 576), [(da_in, (layer, chunk), 0)], 96)
            for piece, rows, to in sends:
                z_piece(layer, piece, chunk, rows, to).start()

    def ffn_2(layer):
        z_piece(layer, 0, far, upper, after).wait_recv()
        add_rows(ga, (layer, sec, after), (0, 288), [(za, (layer, 0), 0)], 96)
        z_piece(layer, 4, after, upper, after).start()
        z_piece(layer, 1, far, lower, before).wait_recv()
        add_rows(ga, (layer, sec, before), (288, 288), [(za, (layer, 1), 0)], 96)
        z_piece(layer, 5, before, lower, before).start()

    def x_over(layer):
        return pltpu.make_async_remote_copy(
            src_ref=ga.at[layer, sec, z, pl.ds((1 - xh) * 288, 288)], dst_ref=xa.at[layer], send_sem=x_s.at[0, layer],
            recv_sem=x_r.at[0, layer], device_id={"dp": dp_at(z, 1 - xh)}, device_id_type=MESH,
        )

    def x_back(layer, which):
        part = fa.at[layer, pl.ds(which * 288, 288)]
        return pltpu.make_async_remote_copy(
            src_ref=part, dst_ref=part, send_sem=x_s.at[1, layer], recv_sem=x_r.at[1, layer],
            device_id={"dp": dp_at(z, 1 - xh)}, device_id_type=MESH,
        )

    def ffn_3(layer):
        for piece in (2, 3, 4, 5):
            z_piece(layer, piece, z, upper, after).wait_recv()
        add_rows(ga, (layer, sec, z), (0, 288), [(za, (layer, 3), 0), (za, (layer, 4), 0)], 96)
        add_rows(ga, (layer, sec, z), (288, 288), [(za, (layer, 2), 0), (za, (layer, 5), 0)], 96)
        x_over(layer).start()

    def ffn_4(layer):
        x_over(layer).wait_recv()

        def add(n, carry):
            here = pl.ds(pl.multiple_of(n * 96, 16), 96)
            there = pl.ds(pl.multiple_of(xh * 288 + n * 96, 16), 96)
            fa[layer, there, :] = (ga[layer, sec, z, there, :].astype(F32) + xa[layer, here, :].astype(F32)).astype(BF16)
            return carry

        lax.fori_loop(0, 3, add, 0)
        x_back(layer, xh).start()

    def spread(layer, half, chunk, to, i):
        return pltpu.make_async_remote_copy(
            src_ref=fa.at[layer], dst_ref=ga_out.at[half, chunk], send_sem=a_s.at[layer, i], recv_sem=a_r.at[half, chunk],
            device_id={"section": layer, "dp": dp_at(to, xh)}, device_id_type=MESH,
        )

    def keep(layer):
        return pltpu.make_async_copy(fa.at[layer], ga_out.at[sec, z], a_l)

    def ffn_5(layer):
        x_back(layer, 1 - xh).wait_recv()
        spread(layer, sec, z, after, 0).start()
        spread(layer, sec, z, before, 1).start()

        @pl.when(layer == sec)
        def _():
            keep(layer).start()

        @pl.when(layer != sec)
        def _():
            spread(layer, sec, z, z, 2).start()

    def pass_on(half, i, chunk, rows, to):
        part = ga_out.at[half, chunk, rows]
        return pltpu.make_async_remote_copy(
            src_ref=part, dst_ref=part, send_sem=f_s.at[half, i], recv_sem=f_r.at[half, i],
            device_id={"dp": dp_at(to, xh)}, device_id_type=MESH,
        )

    def ffn_6():
        for half in range(2):
            spread(sec, half, before, z, 0).wait_recv()
            pass_on(half, 0, before, upper, after).start()
            spread(sec, half, after, z, 0).wait_recv()
            pass_on(half, 1, after, lower, before).start()

    def ffn_7():
        keep(sec).wait()
        spread(sec, other, z, z, 2).wait_recv()
        for half in range(2):
            pass_on(half, 0, far, upper, z).wait_recv()
            pass_on(half, 1, far, lower, z).wait_recv()
            pass_on(half, 0, before, upper, after).wait_send()
            pass_on(half, 1, after, lower, before).wait_send()
        spread(other, sec, z, z, 2).wait_send()
        for layer in range(2):
            swap_cores(layer, 0).wait_send()
            for piece in range(6):
                z_piece(layer, piece, z, upper, after).wait_send()
            x_over(layer).wait_send()
            x_back(layer, xh).wait_send()
            spread(layer, sec, z, after, 0).wait_send()
            spread(layer, sec, z, before, 1).wait_send()

    def b_piece(layer, to, sender):
        return pltpu.make_async_remote_copy(
            src_ref=gb.at[layer, sec, to // 2, pl.ds((to % 2) * 144, 144)], dst_ref=rb.at[layer, sender],
            send_sem=b_s.at[layer, to], recv_sem=b_r.at[layer, sender], device_id={"dp": to}, device_id_type=MESH,
        )

    def b_spread(layer, half, to, sender):
        return pltpu.make_async_remote_copy(
            src_ref=fb.at[layer], dst_ref=gb_out.at[half, sender // 2, pl.ds((sender % 2) * 144, 144)],
            send_sem=e_s.at[layer, to], recv_sem=e_r.at[half, sender], device_id={"section": layer, "dp": to},
            device_id_type=MESH,
        )

    def b_keep(layer):
        return pltpu.make_async_copy(fb.at[layer], gb_out.at[sec, z, pl.ds(xh * 144, 144)], e_l)

    def attn_1(layer):
        swap_cores(layer, 1).wait_recv()
        for chunk in (far, after, before, z):
            add_rows(gb, (layer, sec, chunk), (0, 288), [(db_in, (layer, chunk), 0)], 144)

        def send(k, c):
            b_piece(layer, (d + k) % 8, d).start()
            return c

        lax.fori_loop(1, 8, send, 0)

    def attn_2(layer):
        def take(k, total):
            p = (d + k) % 8
            b_piece(layer, d, p).wait_recv()
            return total + rb[layer, p].astype(F32)

        mine = gb[layer, sec, z, pl.ds(pl.multiple_of(xh * 144, 16), 144), :].astype(F32)
        fb[layer] = lax.fori_loop(1, 8, take, mine).astype(BF16)

        def send(k, c):
            b_spread(layer, sec, (d + k) % 8, d).start()
            return c

        lax.fori_loop(1, 8, send, 0)

        @pl.when(layer == sec)
        def _():
            b_keep(layer).start()

        @pl.when(layer != sec)
        def _():
            b_spread(layer, sec, d, d).start()

    def attn_3():
        b_keep(sec).wait()
        b_spread(sec, other, d, d).wait_recv()
        b_spread(other, sec, d, d).wait_send()

        def finish(k, c):
            p = (d + k) % 8
            b_spread(sec, 0, d, p).wait_recv()
            b_spread(sec, 1, d, p).wait_recv()
            for layer in range(2):
                b_piece(layer, p, d).wait_send()
                b_spread(layer, sec, p, d).wait_send()
            return c

        lax.fori_loop(1, 8, finish, 0)
        for layer in range(2):
            swap_cores(layer, 1).wait_send()

    def backward_layer(step, c):
        layer = 1 - step

        @pl.when(step == 1)
        def _():
            attn_1(1)
            ffn_4(1)

        def feed_back(half):
            rows = half_rows(half)

            @pl.when(step == 1)
            def _():
                ag_wait(df, 2, half)

            dxb[layer, kept(half), :] = df[rows_of(half, t), :].astype(F32)

            def unit_grads(n, c):
                cols = pl.ds(pl.multiple_of(n * 256, 256), 256)
                above = pl.ds(pl.multiple_of(n * 256 + FF, 256), 256)
                du = dot_nt(df[rows, :], wd[layer, cols, :])
                g, up = gate_s[layer, rows, cols], up_s[layer, rows, cols]
                sig = jax.nn.sigmoid(g)
                dgu[rows, cols] = (du * up * sig * (1.0 + g * (1.0 - sig))).astype(BF16)
                dgu[rows, above] = (du * g * sig).astype(BF16)
                return c

            lax.fori_loop(0, 2, unit_grads, 0)

            def normed_part(n, c):
                cols = pl.ds(pl.multiple_of(n * 256, 256), 256)
                rsrc[0, rows, cols] = dot_nt(dgu[rows, :], wgu[layer, cols, :]).astype(BF16)
                return c

            lax.fori_loop(0, 6, normed_part, 0)
            rs_start(0, half)

        both(feed_back)

        @pl.when(step == 1)
        def _():
            both(lambda half: ag_sent(df, 2, half))

        def unit_weights(n, c):
            cols = pl.ds(pl.multiple_of(n * 384, 384), 384)
            got = dot_tn(n2[layer, :, cols], dgu[...]).astype(BF16)
            for h in range(2):
                ga[layer, h, n, pl.ds(0, 192), :] = got[192 * h : 192 * h + 192, 0:FF]
                ga[layer, h, n, pl.ds(192, 192), :] = got[192 * h : 192 * h + 192, FF : 2 * FF]
            cols = pl.ds(pl.multiple_of(n * 128, 128), 128)
            got = dot_tn(u_s[layer, :, cols], df[...]).astype(BF16)
            for h in range(2):
                for i in range(3):
                    ga[layer, h, n, pl.ds(384 + 64 * i, 64), :] = got[64 * h : 64 * h + 64, 512 * i : 512 * i + 512]
            return c

        lax.fori_loop(0, 4, unit_weights, 0)
        swap_cores(layer, 0).start()

        @pl.when(step == 1)
        def _():
            ffn_5(1)
            attn_2(1)

        def hidden_grads(half):
            dn = rs_sum(0, half)
            h = h_own[layer, kept(half), :]
            r = factor_of(h)
            tt = dn * gains[layer, 8:9, :]
            dh = dxb[layer, kept(half), :] + r * tt - h * (r * r * r * jnp.mean(h * tt, axis=-1, keepdims=True))
            dgain[layer, 1:2, :] += jnp.sum(dn * h * r, axis=0, keepdims=True)
            dxb[layer, kept(half), :] = dh
            da[rows_of(half, t), :] = dh.astype(BF16)
            ag_start(da, 3, half)
            rs_sent(0, half)

        both(hidden_grads)
        ffn_1(layer)

        @pl.when((step == 1) & (sec == 1))
        def _():
            ffn_6()

        def mixed_grads(half):
            ag_wait(da, 3, half)
            for h in range(2):
                place = pl.ds(pl.multiple_of(half * ROWS + h * HROWS, HROWS), HROWS)
                got = dot_nt(da[half_rows(half), :], wo[layer, pl.ds(h * HD, HD), :])
                do2[place, :] = got.astype(BF16)
                padded = jnp.concatenate([got, jnp.zeros((HROWS, 128 - HD), F32)], axis=1)
                do2t[:, place] = jnp.transpose(padded)[0:HD, :].astype(BF16)

        both(mixed_grads)
        both(lambda half: ag_sent(da, 3, half))
        dot_rows = jnp.sum(do2[...].astype(F32) * o_f[layer], axis=-1, keepdims=True)
        s_m[...] = dot_rows
        acc[...] = jnp.zeros(acc.shape, F32)

        def dkv_copy(to, sender):
            return pltpu.make_async_remote_copy(
                src_ref=dkv_src.at[to], dst_ref=dkv_land.at[layer, sender], send_sem=dkv_s.at[to], recv_sem=dkv_r.at[layer, sender],
                device_id={"dp": to}, device_id_type=MESH,
            )

        def attend_back(j, c):
            dkt = jnp.zeros((HD, ROWS), F32)
            dvt = jnp.zeros((HD, ROWS), F32)
            for half in range(2):
                rows = pair_rows(half)
                kt = kv[layer, j, pl.ds(0, HD), :]
                s = dot(q2[layer, rows, :], kt) * SCALE + allowed_of(j, half)
                p = jnp.exp(s - stat_m[layer, rows, :])
                dp = dot(do2[rows, :], kv[layer, j, pl.ds(HD, HD), :])
                ds = (p * (dp - s_m[rows, :])).astype(BF16)
                acc[rows, :] += dot_nt(ds, kt)
                dkt += dot(q2t[layer, :, rows], ds)
                dvt += dot(do2t[:, rows], p.astype(BF16))
            dkv_src[j, pl.ds(0, HD), :] = (dkt * SCALE).astype(BF16)
            dkv_src[j, pl.ds(HD, HD), :] = dvt.astype(BF16)

            @pl.when(j < d)
            def _():
                dkv_copy(j, d).start()

            return c

        lax.fori_loop(0, d + 1, attend_back, 0)

        def dkv_sent(k, c):
            dkv_copy(k, d).wait_send()
            return c

        def out_weights(n, c):
            cols = pl.ds(pl.multiple_of(n * 384, 384), 384)
            for h in range(2):
                mixed = [o_b[layer, pl.ds(half * ROWS + h * HROWS, HROWS), :] for half in range(2)]
                got = dot_tn(jnp.concatenate(mixed, axis=0), da[:, cols])
                gb[layer, 0, n, pl.ds(h * HD, HD), :] = got.astype(BF16)
            return c

        lax.fori_loop(0, 4, out_weights, 0)
        lax.fori_loop(0, d, dkv_sent, 0)

        ffn_2(layer)

        def dkv_sum(k, total):
            dkv_copy(d, k).wait_recv()
            return total + dkv_land[layer, k].astype(F32)

        dkv_total = lax.fori_loop(d + 1, 8, dkv_sum, dkv_src[d].astype(F32))
        dkv_t[...] = jnp.zeros(dkv_t.shape, F32)
        dkv_t[0, pl.ds(0, HD), :] = dkv_total[0:HD]
        dkv_t[1, pl.ds(0, HD), :] = dkv_total[HD : 2 * HD]
        dk_rot = jnp.transpose(dkv_t[0])
        dv = jnp.transpose(dkv_t[1])
        cosine, sine = cos_ref[...], sin_ref[...]
        dq[...] = jnp.zeros(dq.shape, F32)
        dq[:, 0:HD] = acc[...] * SCALE
        dq0, dq1 = (
            jnp.concatenate([dq[pl.ds(half * ROWS + h * HROWS, HROWS), :] for half in range(2)], axis=0) for h in range(2)
        )
        dq0 = dq0 * cosine - swapped(dq0) * sine
        dq1 = dq1 * cosine - swapped(dq1) * sine
        dk = dk_rot * cosine - swapped(dk_rot) * sine
        lane = lanes_of(dk)
        dqkv[:, 0:128] = jnp.where(lane < HD, dq0, pltpu.roll(dq1, 96, 1)).astype(BF16)
        dqkv[:, 128:256] = jnp.where(lane < 64, pltpu.roll(dq1, 96, 1), pltpu.roll(dk, 64, 1)).astype(BF16)
        dqkv[:, 256:384] = jnp.where(lane < 32, pltpu.roll(dk, 64, 1), pltpu.roll(dv, 32, 1)).astype(BF16)

        def project_back(half):
            rows = half_rows(half)

            def input_part(n, c):
                cols = pl.ds(pl.multiple_of(n * 512, 512), 512)
                rsrc[1, rows, cols] = dot(dqkv[rows, :], wqkv[layer, :, cols]).astype(BF16)
                return c

            lax.fori_loop(0, 3, input_part, 0)
            rs_start(1, half)

        both(project_back)

        def qkv_weights(n, c):
            cols = pl.ds(pl.multiple_of(n * 384, 384), 384)
            got = dot_tn(dqkv[...], n1[layer, :, cols]).astype(BF16)
            gb[layer, 0, n, pl.ds(2 * HD, HD), :] = got[0:HD]
            gb[layer, 1, n] = got[HD : 4 * HD]
            return c

        lax.fori_loop(0, 4, qkv_weights, 0)
        swap_cores(layer, 1).start()
        ffn_3(layer)
        def input_grads(half):
            dn = rs_sum(1, half)
            v = x_own[layer, kept(half), :]
            r = factor_of(v)
            tt = dn * gains[layer, 0:1, :]
            dx = dxb[layer, kept(half), :] + r * tt - v * (r * r * r * jnp.mean(v * tt, axis=-1, keepdims=True))
            dgain[layer, 0:1, :] += jnp.sum(dn * v * r, axis=0, keepdims=True)
            dxb[layer, kept(half), :] = dx

            @pl.when(step == 0)
            def _():
                df[rows_of(half, t), :] = dx.astype(BF16)
                ag_start(df, 2, half)

            rs_sent(1, half)

        both(input_grads)
        row_out(layer, dxb, dx_out, 1)
        return c

    dgain[...] = jnp.zeros(dgain.shape, F32)
    lax.fori_loop(0, 2, backward_layer, 0)

    mate = pltpu.make_async_remote_copy(
        src_ref=dgain.at[other], dst_ref=dg_peer, send_sem=ns.at[0, 0], recv_sem=nr.at[0, 0],
        device_id={"section": other}, device_id_type=MESH,
    )
    mate.start()
    ffn_4(0)
    attn_1(0)

    def gain_copy(axis, i, buf, me, to, sender):
        return pltpu.make_async_remote_copy(
            src_ref=buf.at[me], dst_ref=buf.at[sender], send_sem=ns.at[i, to], recv_sem=nr.at[i, sender],
            device_id={axis: to}, device_id_type=MESH,
        )

    def gain_send(axis, i, buf, me):
        def send(k, c):
            gain_copy(axis, i, buf, me, (me + k) % 8, me).start()
            return c

        lax.fori_loop(1, 8, send, 0)

    def gain_sum(axis, i, buf, me):
        def take(k, total):
            p = (me + k) % 8
            gain_copy(axis, i, buf, me, p, p).wait_recv()
            return total + buf[p]

        def sent(k, c):
            gain_copy(axis, i, buf, me, (me + k) % 8, me).wait_send()
            return c

        total = lax.fori_loop(1, 8, take, buf[me])
        lax.fori_loop(1, 8, sent, 0)
        return total

    mate.wait_recv()
    mate.wait_send()
    dg_t[t] = dgain[sec] + dg_peer[...]
    gain_send("tensor", 1, dg_t, t)
    ffn_5(0)
    dg_d[d] = gain_sum("tensor", 1, dg_t, t)
    gain_send("dp", 2, dg_d, d)
    attn_2(0)

    @pl.when(sec == 0)
    def _():
        ffn_6()

    gn_out[...] = gain_sum("dp", 2, dg_d, d)
    attn_3()
    ffn_7()
    row_out_wait(yb, y_out, 0)
    row_out_wait(dxb, dx_out, 1)
    for i in range(n_parts):
        sent_parts[i].wait_send()


def step_call(*args):
    hbm = pl.BlockSpec(memory_space=pl.ANY)
    vmem = pl.BlockSpec(memory_space=pltpu.VMEM)
    dma = pltpu.SemaphoreType.DMA
    scratch = [
        pltpu.VMEM((2, 384, D), BF16), pltpu.VMEM((2, 192, D), BF16), pltpu.VMEM((2, D, 2 * FF), BF16),
        pltpu.VMEM((2, FF, D), BF16), pltpu.VMEM((2, 16, D), F32), pltpu.VMEM((ROWS, D), BF16),
        pltpu.VMEM((2, ROWS, D), BF16), pltpu.VMEM((2, ROWS, D), BF16), pltpu.VMEM((2, 2 * ROWS, HD), BF16),
        pltpu.VMEM((2, HD, 2 * ROWS), BF16), pltpu.VMEM((2, 8, 2 * HD, ROWS), BF16), pltpu.VMEM((2, 2 * ROWS, HD), F32),
        pltpu.VMEM((2, 2 * ROWS, HD), BF16), pltpu.VMEM((2, 2 * ROWS, 1), F32), pltpu.VMEM((2, 2 * ROWS, 1), F32),
        pltpu.VMEM((2, ROWS, FF), F32), pltpu.VMEM((2, ROWS, FF), F32), pltpu.VMEM((2, ROWS, FF), BF16),
        pltpu.VMEM((2, OWN, D), F32), pltpu.VMEM((2, OWN, D), F32),
        pltpu.VMEM((2, ROWS, D), BF16), pltpu.VMEM((2, 2, 8, HOWN, D), BF16), pltpu.VMEM((ROWS, D), BF16),
        pltpu.VMEM((2 * ROWS, HD), BF16), pltpu.VMEM((HD, 2 * ROWS), BF16), pltpu.VMEM((ROWS, 2 * FF), BF16),
        pltpu.VMEM((2 * ROWS, 128), F32), pltpu.VMEM((ROWS, 384), BF16), pltpu.VMEM((2, 128, ROWS), F32),
        pltpu.VMEM((8, 2 * HD, ROWS), BF16), pltpu.VMEM((2, 8, 2 * HD, ROWS), BF16), pltpu.VMEM((2 * ROWS, HD), F32),
        pltpu.VMEM((2 * ROWS, 1), F32),
        pltpu.VMEM((2, 2, 4, 576, 512), BF16), pltpu.VMEM((2, 2, 4, 288, 384), BF16), pltpu.VMEM((2, 4, 576, 512), BF16),
        pltpu.VMEM((2, 4, 288, 384), BF16), pltpu.VMEM((2, 6, 288, 512), BF16), pltpu.VMEM((2, 8, 144, 384), BF16),
        pltpu.VMEM((2, 288, 512), BF16), pltpu.VMEM((2, 576, 512), BF16), pltpu.VMEM((2, 144, 384), BF16),
        pltpu.VMEM((2, OWN, D), BF16), pltpu.VMEM((2, OWN, D), F32), pltpu.VMEM((2, 8, D), F32), pltpu.VMEM((8, D), F32),
        pltpu.VMEM((8, 8, D), F32), pltpu.VMEM((8, 8, D), F32),
        dma((10,)), dma((8,)), dma((8,)), dma((4, 2, 8)), dma((4, 2, 8)), dma((2, 2, 8)), dma((2, 2, 8)), dma((8, 2)), dma((8, 2, 2)),
        dma((8,)), dma((2, 8)), dma((2,)), dma((2,)), dma((2,)),
        dma((2, 2)), dma((2, 2)), dma((2, 6)), dma((2, 6)), dma((2, 2)), dma((2, 2)), dma((2, 3)), dma((2, 4)), dma,
        dma((2, 2)), dma((2, 2)), dma((2, 8)), dma((2, 8)), dma((2, 8)), dma((2, 8)), dma, dma((3, 8)), dma((3, 8)),
    ]
    return pl.pallas_call(
        kernel,
        out_shape=(
            jax.ShapeDtypeStruct((2, OWN, D), BF16),
            jax.ShapeDtypeStruct((2, OWN, D), F32),
            jax.ShapeDtypeStruct((2, 4, 576, 512), BF16),
            jax.ShapeDtypeStruct((2, 4, 288, 384), BF16),
            jax.ShapeDtypeStruct((8, D), F32),
        ),
        in_specs=[hbm] * 10 + [vmem] * 3,
        out_specs=(hbm, hbm, hbm, hbm, vmem),
        scratch_shapes=scratch,
        compiler_params=pltpu.CompilerParams(
            collective_id=0, has_side_effects=True, vmem_limit_bytes=64 * 1024 * 1024 - 65536
        ),
        name="train_step",
    )(*args)


def widen(ga_ref, gb_ref, gate_ref, up_ref, down_ref, out_ref, query_ref, key_ref, value_ref):
    for h in range(2):
        rows = pl.ds(192 * h, 192)
        gate_ref[rows, :] = ga_ref[h, 0, 0:192, :].astype(F32)
        up_ref[rows, :] = ga_ref[h, 0, 192:384, :].astype(F32)
        for i in range(3):
            down_ref[pl.ds(64 * h, 64), pl.ds(512 * i, 512)] = ga_ref[h, 0, 384 + 64 * i : 448 + 64 * i, :].astype(F32)
    out_ref[...] = gb_ref[0, 0, 0:192, :].astype(F32)
    query_ref[0:HD, :] = gb_ref[0, 0, 192:288, :].astype(F32)
    query_ref[HD : 2 * HD, :] = gb_ref[1, 0, 0:HD, :].astype(F32)
    key_ref[...] = gb_ref[1, 0, HD : 2 * HD, :].astype(F32)
    value_ref[...] = gb_ref[1, 0, 2 * HD : 3 * HD, :].astype(F32)


def widened(ga, gb):
    shapes = [(D, FF), (D, FF), (FF, D), (192, D), (192, D), (HD, D), (HD, D)]
    by_row = [pl.BlockSpec((384, FF), lambda c: (c, 0)), pl.BlockSpec((384, FF), lambda c: (c, 0)), pl.BlockSpec((128, D), lambda c: (c, 0))]
    by_column = [pl.BlockSpec((rows, 384), lambda c: (0, c)) for rows in (192, 192, HD, HD)]
    return pl.pallas_call(
        widen,
        grid=(4,),
        out_shape=tuple(jax.ShapeDtypeStruct(shape, F32) for shape in shapes),
        in_specs=[pl.BlockSpec((2, 1, 576, 512), lambda c: (0, c, 0, 0)), pl.BlockSpec((2, 1, 288, 384), lambda c: (0, c, 0, 0))],
        out_specs=tuple(by_row + by_column),
        compiler_params=pltpu.CompilerParams(vmem_limit_bytes=40 * 1024 * 1024),
        name="widen",
    )(ga, gb)


def on_device(inputs, cotangent, doc_lengths, norm_one, query_w, key_w, value_w, out_w, norm_two, gate_w, up_w, down_w):
    gains = jnp.concatenate([jnp.broadcast_to(norm_one, (8, D)), jnp.broadcast_to(norm_two, (8, D))]).astype(F32)
    lengths = lax.dynamic_index_in_dim(doc_lengths, lax.axis_index("section"), 0, keepdims=False)
    starts = jnp.cumsum(lengths) - lengths
    i = jnp.arange(ROWS, dtype=jnp.int32)
    places = lax.axis_index("dp") * ROWS + OWN * ((i // HOWN) % 8) + HOWN * (i // HROWS) + i % HOWN
    begins = jnp.max(jnp.where(starts[None, :] <= places[:, None], starts[None, :], 0), axis=1)
    inverse = jnp.exp(jnp.arange(HALF, dtype=F32) * (-2.0 * math.log(ROPE) / HD))
    angles = (places - begins).astype(F32)[:, None] * inverse[None, :]
    cosine, sine = jnp.cos(angles), jnp.sin(angles)
    rest = jnp.zeros((ROWS, 128 - HD), F32)
    cosine = jnp.concatenate([cosine, cosine, rest], axis=1)
    sine = jnp.concatenate([-sine, sine, rest], axis=1)
    begins = jnp.broadcast_to(begins[:, None], (ROWS, 128))
    y, dx, ga, gb, gn = step_call(
        inputs, cotangent, query_w[0].T, key_w[0].T, value_w[0].T, out_w[0], gate_w[0], up_w[0], down_w[0], gains, cosine, sine, begins
    )
    gate, up, down, out, query, key, value = widened(ga, gb)
    return (
        y[None], dx[None], gn[0:1], query.T[None], key.T[None], value.T[None], out[None], gn[1:2], gate[None], up[None], down[None],
    )


def solution(mesh):
    in_specs = (
        P(None, "dp", None),
        P(None, "dp", None),
        P(),
        P("section", None),
        P("section", None, "tensor"),
        P("section", None, "tensor"),
        P("section", None, "tensor"),
        P("section", "tensor", None),
        P("section", None),
        P("section", None, "tensor"),
        P("section", None, "tensor"),
        P("section", "tensor", None),
    )
    out_specs = (
        P("section", None, ("dp", "tensor"), None),
        P("section", None, ("dp", "tensor"), None),
        P("section", None),
        P("section", None, "tensor"),
        P("section", None, "tensor"),
        P("section", None, "tensor"),
        P("section", "tensor", None),
        P("section", None),
        P("section", None, "tensor"),
        P("section", None, "tensor"),
        P("section", "tensor", None),
    )
    return jax.shard_map(on_device, mesh=mesh, in_specs=in_specs, out_specs=out_specs, check_vma=False)
```

```python
import math

import jax
import jax.numpy as jnp
from jax import lax
from jax.experimental import pallas as pl
from jax.experimental.pallas import tpu as pltpu
from jax.sharding import PartitionSpec as P

MESH = pl.DeviceIdType.MESH
F32 = jnp.float32
BF16 = jnp.bfloat16

HD = 96
HALF = HD // 2
D = 1536
FF = 512
ROWS = 256
OWN = 32
HROWS = 128
HOWN = 16
SCALE = 1.0 / math.sqrt(HD)
EPS = 1e-05
ROPE = 100000.0
MASKED = -1e30


def dot(a, b):
    return lax.dot_general(a, b, (((1,), (0,)), ((), ())), preferred_element_type=F32)


def dot_nt(a, b):
    return lax.dot_general(a, b, (((1,), (1,)), ((), ())), preferred_element_type=F32)


def dot_tn(a, b):
    return lax.dot_general(a, b, (((0,), (0,)), ((), ())), preferred_element_type=F32)


def lanes_of(v):
    return lax.broadcasted_iota(jnp.int32, v.shape, 1)


def swapped(v):
    return jnp.where(lanes_of(v) < HALF, pltpu.roll(v, 128 - HALF, 1), pltpu.roll(v, HALF, 1))


def factor_of(v):
    return lax.rsqrt(jnp.mean(v * v, axis=-1, keepdims=True) + EPS)


def kernel(
    x_hbm, ct_hbm, wq_hbm, wk_hbm, wv_hbm, wo_hbm, wg_hbm, wu_hbm, wd_hbm, gains_hbm, cos_ref, sin_ref, beg_ref,
    y_out, dx_out, ga_out, gb_out, gn_out,
    wqkv, wo, wgu, wd, gains, df,
    n1, n2, q2, q2t, kv, o_f, o_b, stat_m, stat_l, gate_s, up_s, u_s, x_own, h_own,
    rsrc, land, da, do2, do2t, dgu, dq, dqkv, dkv_t, dkv_src, dkv_land, acc, s_m,
    ga, gb, da_in, db_in, za, zb, xa, xb, fa, fb, yb, dxb, dgain, dg_peer, dg_t, dg_d,
    w_l, w_s, w_r, ag_s, ag_r, rs_s, rs_r, kv_s, kv_r, dkv_s, dkv_r, out_l, out_s, out_r,
    ds_s, ds_r, z_s, z_r, x_s, x_r, a_s, a_r, a_l, f_s, f_r, ns, nr,
):
    sec = lax.axis_index("section")
    t = lax.axis_index("tensor")
    d = lax.axis_index("dp")
    other = 1 - sec
    z, xh = d // 2, d % 2

    barrier = pltpu.get_barrier_semaphore()

    def greet(axis, me, k, _):
        pl.semaphore_signal(barrier, inc=1, device_id={axis: (me + k) % 8}, device_id_type=MESH)
        return _

    pl.semaphore_signal(barrier, inc=1, device_id={"section": other}, device_id_type=MESH)
    lax.fori_loop(1, 8, lambda k, c: greet("tensor", t, k, c), 0)
    lax.fori_loop(1, 8, lambda k, c: greet("dp", d, k, c), 0)

    def load_rows(source, sem):
        def body(i, c):
            h, p = i // 8, i % 8
            pltpu.make_async_copy(
                source.at[sec, pl.ds(pl.multiple_of(p * OWN + h * HOWN, HOWN), HOWN)],
                df.at[pl.ds(pl.multiple_of(h * HROWS + p * HOWN, HOWN), HOWN)], sem,
            ).start()
            return c

        lax.fori_loop(0, 16, body, 0)

    def rows_loaded(source, sem):
        pltpu.make_async_copy(source.at[sec], df, sem).wait()

    own_parts = [
        (wq_hbm, lambda i: wqkv.at[i, pl.ds(0, 2 * HD)]),
        (wk_hbm, lambda i: wqkv.at[i, pl.ds(2 * HD, HD)]),
        (wv_hbm, lambda i: wqkv.at[i, pl.ds(3 * HD, HD)]),
        (wo_hbm, lambda i: wo.at[i]),
        (wg_hbm, lambda i: wgu.at[i, :, 0:FF]),
        (wu_hbm, lambda i: wgu.at[i, :, FF : 2 * FF]),
        (wd_hbm, lambda i: wd.at[i]),
        (gains_hbm, lambda i: gains.at[i]),
    ]
    n_parts = len(own_parts)
    own_copies = [pltpu.make_async_copy(a, b(sec), w_l.at[i]) for i, (a, b) in enumerate(own_parts)]
    load_rows(x_hbm, w_l.at[8])
    own_copies[7].start()
    for i in range(7):
        own_copies[i].start()
    pl.semaphore_wait(barrier, 15)
    sent_parts = [
        pltpu.make_async_remote_copy(
            src_ref=a, dst_ref=b(sec), send_sem=w_s.at[i], recv_sem=w_r.at[i],
            device_id={"section": other}, device_id_type=MESH,
        )
        for i, (a, b) in enumerate(own_parts)
    ]
    for i in (7, 0, 1, 2, 3, 4, 5, 6):
        sent_parts[i].start()

    def weight_ready(layer, *which):
        @pl.when(layer == sec)
        def _():
            for i in which:
                own_copies[i].wait()

        @pl.when(layer != sec)
        def _():
            for i in which:
                a, b = own_parts[i]
                pltpu.make_async_remote_copy(
                    src_ref=a, dst_ref=b(other), send_sem=w_s.at[i], recv_sem=w_r.at[i],
                    device_id={"section": other}, device_id_type=MESH,
                ).wait_recv()

    def half_rows(half):
        return pl.ds(pl.multiple_of(half * HROWS, HROWS), HROWS)

    def pair_rows(half):
        return pl.ds(pl.multiple_of(half * ROWS, ROWS), ROWS)

    def rows_of(half, owner):
        return pl.ds(pl.multiple_of(half * HROWS + owner * HOWN, HOWN), HOWN)

    def kept(half):
        return pl.ds(pl.multiple_of(half * HOWN, HOWN), HOWN)

    def over_peers(body):
        def step(k, c):
            body((t + k) % 8)
            return c

        lax.fori_loop(1, 8, step, 0)

    def ag_copy(buf, i, half, to, owner):
        rows = rows_of(half, owner)
        return pltpu.make_async_remote_copy(
            src_ref=buf.at[rows], dst_ref=buf.at[rows], send_sem=ag_s.at[i, half, to], recv_sem=ag_r.at[i, half, owner],
            device_id={"tensor": to}, device_id_type=MESH,
        )

    def ag_start(buf, i, half):
        over_peers(lambda p: ag_copy(buf, i, half, p, t).start())

    def ag_wait(buf, i, half):
        over_peers(lambda p: ag_copy(buf, i, half, t, p).wait_recv())

    def ag_sent(buf, i, half):
        over_peers(lambda p: ag_copy(buf, i, half, p, t).wait_send())

    def rs_copy(i, half, to, sender):
        return pltpu.make_async_remote_copy(
            src_ref=rsrc.at[i, rows_of(half, to)], dst_ref=land.at[i, half, sender], send_sem=rs_s.at[i, half, to],
            recv_sem=rs_r.at[i, half, sender], device_id={"tensor": to}, device_id_type=MESH,
        )

    def rs_start(i, half):
        over_peers(lambda p: rs_copy(i, half, p, t).start())

    def rs_sum(i, half):
        def body(k, total):
            p = (t + k) % 8
            rs_copy(i, half, t, p).wait_recv()
            return total + land[i, half, p].astype(F32)

        return lax.fori_loop(1, 8, body, rsrc[i, rows_of(half, t), :].astype(F32))

    def rs_sent(i, half):
        over_peers(lambda p: rs_copy(i, half, p, t).wait_send())

    def both(body):
        def step(half, c):
            body(half)
            return c

        lax.fori_loop(0, 2, step, 0)

    def place_of(i):
        return OWN * ((i // HOWN) % 8) + HOWN * (i // HROWS) + i % HOWN

    def allowed_of(j, half):
        rows = place_of(lax.broadcasted_iota(jnp.int32, (HROWS, 1), 0) + half * HROWS) + d * ROWS
        cols = place_of(lax.broadcasted_iota(jnp.int32, (1, ROWS), 1)) + j * ROWS
        allowed = (cols <= rows) & (cols >= beg_ref[half_rows(half), 0:1])
        return jnp.concatenate([jnp.where(allowed, 0.0, MASKED)] * 2, axis=0)

    weight_ready(0, 7)
    rows_loaded(x_hbm, w_l.at[8])

    def first_norm(i, c):
        rows = pl.ds(pl.multiple_of(i * OWN, OWN), OWN)
        v = df[rows, :].astype(F32)
        n1[0, rows, :] = (v * factor_of(v) * gains[0, 0:1, :]).astype(BF16)
        return c

    lax.fori_loop(0, ROWS // OWN, first_norm, 0)
    for half in range(2):
        x_own[0, kept(half), :] = df[rows_of(half, t), :].astype(F32)
    load_rows(ct_hbm, w_l.at[9])

    def forward_layer(layer, c):
        weight_ready(layer, 0, 1, 2)

        def kv_copy(owner, to, half):
            part = kv.at[layer, owner, :, half_rows(half)]
            return pltpu.make_async_remote_copy(
                src_ref=part, dst_ref=part, send_sem=kv_s.at[to, half], recv_sem=kv_r.at[owner, layer, half],
                device_id={"dp": to}, device_id_type=MESH,
            )

        def project(half):
            rows = half_rows(half)

            @pl.when(layer == 1)
            def _():
                ag_wait(n1.at[1], 0, half)

            raw = dot_nt(n1[layer, rows, :], wqkv[layer])
            c0, c1, c2 = raw[:, 0:128], raw[:, 128:256], raw[:, 256:384]
            lane = lanes_of(c0)
            q1 = jnp.where(lane < 32, pltpu.roll(c0, 32, 1), pltpu.roll(c1, 32, 1))
            k0 = jnp.where(lane < 64, pltpu.roll(c1, 64, 1), pltpu.roll(c2, 64, 1))
            v0 = pltpu.roll(c2, 96, 1)
            cosine, sine = cos_ref[rows, :], sin_ref[rows, :]
            turned = k0 * cosine + swapped(k0) * sine
            kv[layer, d, pl.ds(0, HD), rows] = jnp.transpose(turned)[0:HD, :].astype(BF16)
            kv[layer, d, pl.ds(HD, HD), rows] = jnp.transpose(v0)[0:HD, :].astype(BF16)

            def kv_send(k, c):
                kv_copy(d, k, half).start()
                return c

            lax.fori_loop(d + 1, 8, kv_send, 0)
            for h, part in ((0, c0), (1, q1)):
                turned = part * cosine + swapped(part) * sine
                place = pl.ds(pl.multiple_of(half * ROWS + h * HROWS, HROWS), HROWS)
                q2[layer, place, :] = turned[:, 0:HD].astype(BF16)
                q2t[layer, :, place] = jnp.transpose(turned)[0:HD, :].astype(BF16)

        both(project)

        @pl.when(layer == 1)
        def _():
            both(lambda half: ag_sent(n1.at[1], 0, half))

        weight_ready(layer, 3)

        def attend_half(half):
            rows = pair_rows(half)
            s_m[rows, :] = jnp.full((ROWS, 1), MASKED, F32)
            stat_l[layer, rows, :] = jnp.zeros((ROWS, 1), F32)
            acc[rows, :] = jnp.zeros((ROWS, HD), F32)

            def attend(i, c):
                j = d - i

                @pl.when((i > 0) & (half == 0))
                def _():
                    kv_copy(j, d, 0).wait_recv()
                    kv_copy(j, d, 1).wait_recv()

                s = dot(q2[layer, rows, :], kv[layer, j, pl.ds(0, HD), :]) * SCALE + allowed_of(j, half)
                old = s_m[rows, :]
                new = jnp.maximum(old, jnp.max(s, axis=-1, keepdims=True))
                p = jnp.exp(s - new)
                shrink = jnp.exp(old - new)
                s_m[rows, :] = new
                stat_l[layer, rows, :] = stat_l[layer, rows, :] * shrink + jnp.sum(p, axis=-1, keepdims=True)
                acc[rows, :] = acc[rows, :] * shrink + dot_nt(p.astype(BF16), kv[layer, j, pl.ds(HD, HD), :])
                return c

            lax.fori_loop(0, d + 1, attend, 0)
            total = stat_l[layer, rows, :]
            mixed = acc[rows, :] / total
            o_f[layer, rows, :] = mixed
            o_b[layer, rows, :] = mixed.astype(BF16)
            stat_m[layer, rows, :] = s_m[rows, :] + jnp.log(total)
            first = pl.ds(pl.multiple_of(half * ROWS, HROWS), HROWS)
            second = pl.ds(pl.multiple_of(half * ROWS + HROWS, HROWS), HROWS)

            def out_part(n, c):
                cols = pl.ds(pl.multiple_of(n * 512, 512), 512)
                part = dot(o_b[layer, first, :], wo[layer, pl.ds(0, HD), cols])
                part += dot(o_b[layer, second, :], wo[layer, pl.ds(HD, HD), cols])
                rsrc[0, half_rows(half), cols] = part.astype(BF16)
                return c

            lax.fori_loop(0, 3, out_part, 0)
            rs_start(0, half)

        both(attend_half)

        def kv_sent(k, c):
            kv_copy(d, k, 0).wait_send()
            kv_copy(d, k, 1).wait_send()
            return c

        lax.fori_loop(d + 1, 8, kv_sent, 0)

        def middle(half):
            v = x_own[layer, kept(half), :] + rs_sum(0, half)
            h_own[layer, kept(half), :] = v
            n2[layer, rows_of(half, t), :] = (v * factor_of(v) * gains[layer, 8:9, :]).astype(BF16)
            ag_start(n2.at[layer], 1, half)
            rs_sent(0, half)

        both(middle)
        weight_ready(layer, 4, 5)
        weight_ready(layer, 6)

        def feed(half):
            rows = half_rows(half)
            ag_wait(n2.at[layer], 1, half)

            def units(n, c):
                cols = pl.ds(pl.multiple_of(n * 256, 256), 256)
                above = pl.ds(pl.multiple_of(n * 256 + FF, 256), 256)
                g = dot(n2[layer, rows, :], wgu[layer, :, cols])
                up = dot(n2[layer, rows, :], wgu[layer, :, above])
                gate_s[layer, rows, cols] = g
                up_s[layer, rows, cols] = up
                u_s[layer, rows, cols] = (g * jax.nn.sigmoid(g) * up).astype(BF16)
                return c

            lax.fori_loop(0, 2, units, 0)

            def down_part(n, c):
                cols = pl.ds(pl.multiple_of(n * 512, 512), 512)
                rsrc[1, rows, cols] = dot(u_s[layer, rows, :], wd[layer, :, cols]).astype(BF16)
                return c

            lax.fori_loop(0, 3, down_part, 0)
            rs_start(1, half)
            ag_sent(n2.at[layer], 1, half)

        both(feed)

        @pl.when(layer == 0)
        def _():
            weight_ready(1, 7)

        def result(half):
            y = (h_own[layer, kept(half), :] + rs_sum(1, half)).astype(BF16)
            yb[layer, kept(half), :] = y

            @pl.when(layer == 0)
            def _():
                v = y.astype(F32)
                x_own[1, kept(half), :] = v
                n1[1, rows_of(half, t), :] = (v * factor_of(v) * gains[1, 0:1, :]).astype(BF16)
                ag_start(n1.at[1], 0, half)

            rs_sent(1, half)

        both(result)
        row_out(layer, yb, y_out, 0)
        return c

    def row_out(layer, buf, out, i):
        @pl.when(layer == sec)
        def _():
            pltpu.make_async_copy(buf.at[layer], out.at[sec], out_l.at[i]).start()

        @pl.when(layer != sec)
        def _():
            pltpu.make_async_remote_copy(
                src_ref=buf.at[layer], dst_ref=out.at[sec], send_sem=out_s.at[i], recv_sem=out_r.at[i],
                device_id={"section": other}, device_id_type=MESH,
            ).start()

    def row_out_wait(buf, out, i):
        pltpu.make_async_copy(buf.at[sec], out.at[sec], out_l.at[i]).wait()
        copy = pltpu.make_async_remote_copy(
            src_ref=buf.at[other], dst_ref=out.at[other], send_sem=out_s.at[i], recv_sem=out_r.at[i],
            device_id={"section": other}, device_id_type=MESH,
        )
        copy.wait_send()
        copy.wait_recv()

    lax.fori_loop(0, 2, forward_layer, 0)

    rows_loaded(ct_hbm, w_l.at[9])

    sets = ((ga, da_in, za, xa, fa, ga_out), (gb, db_in, zb, xb, fb, gb_out))
    before, after = (z + 3) % 4, (z + 1) % 4
    far = (z + 2) % 4

    def dp_at(zz, xx):
        return zz * 2 + xx

    def quarter(i, which):
        size = (288, 144)[i]
        return pl.ds(pl.multiple_of(which * size, 16), size)

    def swap_cores(layer, i):
        return pltpu.make_async_remote_copy(
            src_ref=sets[i][0].at[layer, other], dst_ref=sets[i][1].at[layer], send_sem=ds_s.at[i, layer],
            recv_sem=ds_r.at[i, layer], device_id={"section": other}, device_id_type=MESH,
        )

    def add_rows(target, index, first, size, sources):
        count = 96 if size % 96 == 0 else 48

        def add(n, carry):
            here = pl.ds(pl.multiple_of(first + n * count, 16), count)
            total = target[(*index, here)].astype(F32)
            for ref, place, start in sources:
                total += ref[(*place, pl.ds(pl.multiple_of(start + n * count, 16), count))].astype(F32)
            target[(*index, here)] = total.astype(BF16)
            return carry

        lax.fori_loop(0, size // count, add, 0)

    def z_piece(layer, i, piece, chunk, which, to):
        return pltpu.make_async_remote_copy(
            src_ref=sets[i][0].at[layer, sec, chunk, quarter(i, which)], dst_ref=sets[i][2].at[layer, piece],
            send_sem=z_s.at[i, layer, piece], recv_sem=z_r.at[i, layer, piece], device_id={"dp": dp_at(to, xh)},
            device_id_type=MESH,
        )

    def sum_1(layer, i):
        g, arrived = sets[i][0:2]
        swap_cores(layer, i).wait_recv()
        for chunk, sends in (
            (far, ((0, 0, after), (1, 1, before))),
            (after, ((2, 1, after),)),
            (before, ((3, 0, before),)),
            (z, ()),
        ):
            add_rows(g, (layer, sec, chunk), 0, g.shape[3], [(arrived, (layer, chunk), 0)])
            for piece, which, to in sends:
                z_piece(layer, i, piece, chunk, which, to).start()

    def sum_2(layer, i):
        g, landed = sets[i][0], sets[i][2]
        size = landed.shape[2]
        z_piece(layer, i, 0, far, 0, after).wait_recv()
        add_rows(g, (layer, sec, after), 0, size, [(landed, (layer, 0), 0)])
        z_piece(layer, i, 4, after, 0, after).start()
        z_piece(layer, i, 1, far, 1, before).wait_recv()
        add_rows(g, (layer, sec, before), size, size, [(landed, (layer, 1), 0)])
        z_piece(layer, i, 5, before, 1, before).start()

    def x_over(layer, i):
        return pltpu.make_async_remote_copy(
            src_ref=sets[i][0].at[layer, sec, z, quarter(i, 1 - xh)], dst_ref=sets[i][3].at[layer],
            send_sem=x_s.at[i, 0, layer], recv_sem=x_r.at[i, 0, layer], device_id={"dp": dp_at(z, 1 - xh)},
            device_id_type=MESH,
        )

    def x_back(layer, i, which):
        part = sets[i][4].at[layer, quarter(i, which)]
        return pltpu.make_async_remote_copy(
            src_ref=part, dst_ref=part, send_sem=x_s.at[i, 1, layer], recv_sem=x_r.at[i, 1, layer],
            device_id={"dp": dp_at(z, 1 - xh)}, device_id_type=MESH,
        )

    def sum_3(layer, i):
        g, landed = sets[i][0], sets[i][2]
        size = landed.shape[2]
        for piece in (2, 3, 4, 5):
            z_piece(layer, i, piece, z, 0, after).wait_recv()
        add_rows(g, (layer, sec, z), 0, size, [(landed, (layer, 3), 0), (landed, (layer, 4), 0)])
        add_rows(g, (layer, sec, z), size, size, [(landed, (layer, 2), 0), (landed, (layer, 5), 0)])
        x_over(layer, i).start()

    def spread(layer, i, half, chunk, which, to, k):
        rows = quarter(i, which)
        return pltpu.make_async_remote_copy(
            src_ref=sets[i][4].at[layer, rows], dst_ref=sets[i][5].at[half, chunk, rows], send_sem=a_s.at[i, layer, which, k],
            recv_sem=a_r.at[i, half, chunk, which], device_id={"section": layer, "dp": dp_at(to, xh)}, device_id_type=MESH,
        )

    def keep(layer, i, which):
        rows = quarter(i, which)
        return pltpu.make_async_copy(sets[i][4].at[layer, rows], sets[i][5].at[sec, z, rows], a_l.at[i, which])

    def spread_all(layer, i, which):
        spread(layer, i, sec, z, which, after, 0).start()
        spread(layer, i, sec, z, which, before, 1).start()

        @pl.when(layer == sec)
        def _():
            keep(layer, i, which).start()

        @pl.when(layer != sec)
        def _():
            spread(layer, i, sec, z, which, z, 2).start()

    def sum_4(layer, i):
        g, over, done = sets[i][0], sets[i][3], sets[i][4]
        size = over.shape[1]
        x_over(layer, i).wait_recv()

        def add(n, carry):
            here = pl.ds(pl.multiple_of(n * 48, 16), 48)
            there = pl.ds(pl.multiple_of(xh * size + n * 48, 16), 48)
            done[layer, there, :] = (g[layer, sec, z, there, :].astype(F32) + over[layer, here, :].astype(F32)).astype(BF16)
            return carry

        lax.fori_loop(0, size // 48, add, 0)
        x_back(layer, i, xh).start()
        spread_all(layer, i, xh)

    def sum_5(layer, i):
        x_back(layer, i, 1 - xh).wait_recv()
        spread_all(layer, i, 1 - xh)

    def pass_on(i, half, chunk, which, to):
        part = sets[i][5].at[half, chunk, quarter(i, which)]
        return pltpu.make_async_remote_copy(
            src_ref=part, dst_ref=part, send_sem=f_s.at[i, half, which], recv_sem=f_r.at[i, half, which],
            device_id={"dp": dp_at(to, xh)}, device_id_type=MESH,
        )

    def sum_6(i):
        for half in range(2):
            spread(sec, i, half, before, 0, z, 0).wait_recv()
            pass_on(i, half, before, 0, after).start()
            spread(sec, i, half, after, 1, z, 0).wait_recv()
            pass_on(i, half, after, 1, before).start()

    def sum_7(i):
        for which in range(2):
            keep(sec, i, which).wait()
            spread(sec, i, other, z, which, z, 2).wait_recv()
            spread(other, i, sec, z, which, z, 2).wait_send()
            for half in range(2):
                spread(sec, i, half, (after, before)[which], which, z, 0).wait_recv()
                pass_on(i, half, far, which, z).wait_recv()
                pass_on(i, half, z, which, after).wait_send()
        for layer in range(2):
            swap_cores(layer, i).wait_send()
            for piece in range(6):
                z_piece(layer, i, piece, z, 0, after).wait_send()
            x_over(layer, i).wait_send()
            x_back(layer, i, xh).wait_send()
            for which in range(2):
                spread(layer, i, sec, z, which, after, 0).wait_send()
                spread(layer, i, sec, z, which, before, 1).wait_send()

    def backward_layer(step, c):
        layer = 1 - step

        @pl.when(step == 1)
        def _():
            sum_1(1, 1)

        def feed_back(half):
            rows = half_rows(half)

            @pl.when(step == 1)
            def _():
                ag_wait(df, 2, half)

            dxb[layer, kept(half), :] = df[rows_of(half, t), :].astype(F32)

            def unit_grads(n, c):
                cols = pl.ds(pl.multiple_of(n * 256, 256), 256)
                above = pl.ds(pl.multiple_of(n * 256 + FF, 256), 256)
                du = dot_nt(df[rows, :], wd[layer, cols, :])
                g, up = gate_s[layer, rows, cols], up_s[layer, rows, cols]
                sig = jax.nn.sigmoid(g)
                dgu[rows, cols] = (du * up * sig * (1.0 + g * (1.0 - sig))).astype(BF16)
                dgu[rows, above] = (du * g * sig).astype(BF16)
                return c

            lax.fori_loop(0, 2, unit_grads, 0)

            def normed_part(n, c):
                cols = pl.ds(pl.multiple_of(n * 256, 256), 256)
                rsrc[0, rows, cols] = dot_nt(dgu[rows, :], wgu[layer, cols, :]).astype(BF16)
                return c

            lax.fori_loop(0, 6, normed_part, 0)
            rs_start(0, half)

        both(feed_back)

        @pl.when(step == 1)
        def _():
            both(lambda half: ag_sent(df, 2, half))

        def unit_weights(n, c):
            cols = pl.ds(pl.multiple_of(n * 384, 384), 384)
            got = dot_tn(n2[layer, :, cols], dgu[...]).astype(BF16)
            for h in range(2):
                ga[layer, h, n, pl.ds(0, 192), :] = got[192 * h : 192 * h + 192, 0:FF]
                ga[layer, h, n, pl.ds(192, 192), :] = got[192 * h : 192 * h + 192, FF : 2 * FF]
            cols = pl.ds(pl.multiple_of(n * 128, 128), 128)
            got = dot_tn(u_s[layer, :, cols], df[...]).astype(BF16)
            for h in range(2):
                for i in range(3):
                    ga[layer, h, n, pl.ds(384 + 64 * i, 64), :] = got[64 * h : 64 * h + 64, 512 * i : 512 * i + 512]
            return c

        lax.fori_loop(0, 4, unit_weights, 0)
        swap_cores(layer, 0).start()

        @pl.when(step == 1)
        def _():
            sum_4(1, 0)
            sum_2(1, 1)

        def hidden_grads(half):
            dn = rs_sum(0, half)
            h = h_own[layer, kept(half), :]
            r = factor_of(h)
            tt = dn * gains[layer, 8:9, :]
            dh = dxb[layer, kept(half), :] + r * tt - h * (r * r * r * jnp.mean(h * tt, axis=-1, keepdims=True))
            dgain[layer, 1:2, :] += jnp.sum(dn * h * r, axis=0, keepdims=True)
            dxb[layer, kept(half), :] = dh
            da[rows_of(half, t), :] = dh.astype(BF16)
            ag_start(da, 3, half)
            rs_sent(0, half)

        both(hidden_grads)
        sum_1(layer, 0)

        @pl.when(step == 1)
        def _():
            sum_5(1, 0)
            sum_3(1, 1)

        def mixed_grads(half):
            ag_wait(da, 3, half)
            for h in range(2):
                place = pl.ds(pl.multiple_of(half * ROWS + h * HROWS, HROWS), HROWS)
                got = dot_nt(da[half_rows(half), :], wo[layer, pl.ds(h * HD, HD), :])
                do2[place, :] = got.astype(BF16)
                padded = jnp.concatenate([got, jnp.zeros((HROWS, 128 - HD), F32)], axis=1)
                do2t[:, place] = jnp.transpose(padded)[0:HD, :].astype(BF16)

        both(mixed_grads)
        both(lambda half: ag_sent(da, 3, half))
        dot_rows = jnp.sum(do2[...].astype(F32) * o_f[layer], axis=-1, keepdims=True)
        s_m[...] = dot_rows
        acc[...] = jnp.zeros(acc.shape, F32)

        def dkv_copy(to, sender):
            return pltpu.make_async_remote_copy(
                src_ref=dkv_src.at[to], dst_ref=dkv_land.at[layer, sender], send_sem=dkv_s.at[to], recv_sem=dkv_r.at[layer, sender],
                device_id={"dp": to}, device_id_type=MESH,
            )

        def attend_back(j, c):
            dkt = jnp.zeros((HD, ROWS), F32)
            dvt = jnp.zeros((HD, ROWS), F32)
            for half in range(2):
                rows = pair_rows(half)
                kt = kv[layer, j, pl.ds(0, HD), :]
                s = dot(q2[layer, rows, :], kt) * SCALE + allowed_of(j, half)
                p = jnp.exp(s - stat_m[layer, rows, :])
                dp = dot(do2[rows, :], kv[layer, j, pl.ds(HD, HD), :])
                ds = (p * (dp - s_m[rows, :])).astype(BF16)
                acc[rows, :] += dot_nt(ds, kt)
                dkt += dot(q2t[layer, :, rows], ds)
                dvt += dot(do2t[:, rows], p.astype(BF16))
            dkv_src[j, pl.ds(0, HD), :] = (dkt * SCALE).astype(BF16)
            dkv_src[j, pl.ds(HD, HD), :] = dvt.astype(BF16)

            @pl.when(j < d)
            def _():
                dkv_copy(j, d).start()

            return c

        lax.fori_loop(0, d + 1, attend_back, 0)

        def dkv_sent(k, c):
            dkv_copy(k, d).wait_send()
            return c

        def out_weights(n, c):
            cols = pl.ds(pl.multiple_of(n * 384, 384), 384)
            for h in range(2):
                mixed = [o_b[layer, pl.ds(half * ROWS + h * HROWS, HROWS), :] for half in range(2)]
                got = dot_tn(jnp.concatenate(mixed, axis=0), da[:, cols])
                gb[layer, 0, n, pl.ds(h * HD, HD), :] = got.astype(BF16)
            return c

        lax.fori_loop(0, 4, out_weights, 0)
        lax.fori_loop(0, d, dkv_sent, 0)

        sum_2(layer, 0)

        @pl.when(step == 1)
        def _():
            sum_4(1, 1)

        def dkv_sum(k, total):
            dkv_copy(d, k).wait_recv()
            return total + dkv_land[layer, k].astype(F32)

        dkv_total = lax.fori_loop(d + 1, 8, dkv_sum, dkv_src[d].astype(F32))
        dkv_t[...] = jnp.zeros(dkv_t.shape, F32)
        dkv_t[0, pl.ds(0, HD), :] = dkv_total[0:HD]
        dkv_t[1, pl.ds(0, HD), :] = dkv_total[HD : 2 * HD]
        dk_rot = jnp.transpose(dkv_t[0])
        dv = jnp.transpose(dkv_t[1])
        cosine, sine = cos_ref[...], sin_ref[...]
        dq[...] = jnp.zeros(dq.shape, F32)
        dq[:, 0:HD] = acc[...] * SCALE
        dq0, dq1 = (
            jnp.concatenate([dq[pl.ds(half * ROWS + h * HROWS, HROWS), :] for half in range(2)], axis=0) for h in range(2)
        )
        dq0 = dq0 * cosine - swapped(dq0) * sine
        dq1 = dq1 * cosine - swapped(dq1) * sine
        dk = dk_rot * cosine - swapped(dk_rot) * sine
        lane = lanes_of(dk)
        dqkv[:, 0:128] = jnp.where(lane < HD, dq0, pltpu.roll(dq1, 96, 1)).astype(BF16)
        dqkv[:, 128:256] = jnp.where(lane < 64, pltpu.roll(dq1, 96, 1), pltpu.roll(dk, 64, 1)).astype(BF16)
        dqkv[:, 256:384] = jnp.where(lane < 32, pltpu.roll(dk, 64, 1), pltpu.roll(dv, 32, 1)).astype(BF16)

        def project_back(half):
            rows = half_rows(half)

            def input_part(n, c):
                cols = pl.ds(pl.multiple_of(n * 512, 512), 512)
                rsrc[1, rows, cols] = dot(dqkv[rows, :], wqkv[layer, :, cols]).astype(BF16)
                return c

            lax.fori_loop(0, 3, input_part, 0)
            rs_start(1, half)

        both(project_back)

        def qkv_weights(n, c):
            cols = pl.ds(pl.multiple_of(n * 384, 384), 384)
            got = dot_tn(dqkv[...], n1[layer, :, cols]).astype(BF16)
            gb[layer, 0, n, pl.ds(2 * HD, HD), :] = got[0:HD]
            gb[layer, 1, n] = got[HD : 4 * HD]
            return c

        lax.fori_loop(0, 4, qkv_weights, 0)
        swap_cores(layer, 1).start()
        sum_3(layer, 0)

        @pl.when(step == 1)
        def _():
            sum_5(1, 1)

            @pl.when(sec == 1)
            def _():
                sum_6(0)

        def input_grads(half):
            dn = rs_sum(1, half)
            v = x_own[layer, kept(half), :]
            r = factor_of(v)
            tt = dn * gains[layer, 0:1, :]
            dx = dxb[layer, kept(half), :] + r * tt - v * (r * r * r * jnp.mean(v * tt, axis=-1, keepdims=True))
            dgain[layer, 0:1, :] += jnp.sum(dn * v * r, axis=0, keepdims=True)
            dxb[layer, kept(half), :] = dx

            @pl.when(step == 0)
            def _():
                df[rows_of(half, t), :] = dx.astype(BF16)
                ag_start(df, 2, half)

            rs_sent(1, half)

        both(input_grads)
        row_out(layer, dxb, dx_out, 1)
        return c

    dgain[...] = jnp.zeros(dgain.shape, F32)
    lax.fori_loop(0, 2, backward_layer, 0)

    mate = pltpu.make_async_remote_copy(
        src_ref=dgain.at[other], dst_ref=dg_peer, send_sem=ns.at[0, 0], recv_sem=nr.at[0, 0],
        device_id={"section": other}, device_id_type=MESH,
    )
    mate.start()
    sum_4(0, 0)
    sum_1(0, 1)

    @pl.when(sec == 1)
    def _():
        sum_6(1)


    def gain_copy(axis, i, buf, me, to, sender):
        return pltpu.make_async_remote_copy(
            src_ref=buf.at[me], dst_ref=buf.at[sender], send_sem=ns.at[i, to], recv_sem=nr.at[i, sender],
            device_id={axis: to}, device_id_type=MESH,
        )

    def gain_send(axis, i, buf, me):
        def send(k, c):
            gain_copy(axis, i, buf, me, (me + k) % 8, me).start()
            return c

        lax.fori_loop(1, 8, send, 0)

    def gain_sum(axis, i, buf, me):
        def take(k, total):
            p = (me + k) % 8
            gain_copy(axis, i, buf, me, p, p).wait_recv()
            return total + buf[p]

        def sent(k, c):
            gain_copy(axis, i, buf, me, (me + k) % 8, me).wait_send()
            return c

        total = lax.fori_loop(1, 8, take, buf[me])
        lax.fori_loop(1, 8, sent, 0)
        return total

    mate.wait_recv()
    mate.wait_send()
    dg_t[t] = dgain[sec] + dg_peer[...]
    gain_send("tensor", 1, dg_t, t)
    sum_5(0, 0)
    sum_2(0, 1)
    dg_d[d] = gain_sum("tensor", 1, dg_t, t)
    gain_send("dp", 2, dg_d, d)
    sum_3(0, 1)

    @pl.when(sec == 0)
    def _():
        sum_6(0)

    sum_4(0, 1)
    sum_5(0, 1)

    @pl.when(sec == 0)
    def _():
        sum_6(1)

    gn_out[...] = gain_sum("dp", 2, dg_d, d)
    sum_7(0)
    sum_7(1)
    row_out_wait(yb, y_out, 0)
    row_out_wait(dxb, dx_out, 1)
    for i in range(n_parts):
        sent_parts[i].wait_send()


def step_call(*args):
    hbm = pl.BlockSpec(memory_space=pl.ANY)
    vmem = pl.BlockSpec(memory_space=pltpu.VMEM)
    dma = pltpu.SemaphoreType.DMA
    scratch = [
        pltpu.VMEM((2, 384, D), BF16), pltpu.VMEM((2, 192, D), BF16), pltpu.VMEM((2, D, 2 * FF), BF16),
        pltpu.VMEM((2, FF, D), BF16), pltpu.VMEM((2, 16, D), F32), pltpu.VMEM((ROWS, D), BF16),
        pltpu.VMEM((2, ROWS, D), BF16), pltpu.VMEM((2, ROWS, D), BF16), pltpu.VMEM((2, 2 * ROWS, HD), BF16),
        pltpu.VMEM((2, HD, 2 * ROWS), BF16), pltpu.VMEM((2, 8, 2 * HD, ROWS), BF16), pltpu.VMEM((2, 2 * ROWS, HD), F32),
        pltpu.VMEM((2, 2 * ROWS, HD), BF16), pltpu.VMEM((2, 2 * ROWS, 1), F32), pltpu.VMEM((2, 2 * ROWS, 1), F32),
        pltpu.VMEM((2, ROWS, FF), F32), pltpu.VMEM((2, ROWS, FF), F32), pltpu.VMEM((2, ROWS, FF), BF16),
        pltpu.VMEM((2, OWN, D), F32), pltpu.VMEM((2, OWN, D), F32),
        pltpu.VMEM((2, ROWS, D), BF16), pltpu.VMEM((2, 2, 8, HOWN, D), BF16), pltpu.VMEM((ROWS, D), BF16),
        pltpu.VMEM((2 * ROWS, HD), BF16), pltpu.VMEM((HD, 2 * ROWS), BF16), pltpu.VMEM((ROWS, 2 * FF), BF16),
        pltpu.VMEM((2 * ROWS, 128), F32), pltpu.VMEM((ROWS, 384), BF16), pltpu.VMEM((2, 128, ROWS), F32),
        pltpu.VMEM((8, 2 * HD, ROWS), BF16), pltpu.VMEM((2, 8, 2 * HD, ROWS), BF16), pltpu.VMEM((2 * ROWS, HD), F32),
        pltpu.VMEM((2 * ROWS, 1), F32),
        pltpu.VMEM((2, 2, 4, 576, 512), BF16), pltpu.VMEM((2, 2, 4, 288, 384), BF16), pltpu.VMEM((2, 4, 576, 512), BF16),
        pltpu.VMEM((2, 4, 288, 384), BF16), pltpu.VMEM((2, 6, 288, 512), BF16), pltpu.VMEM((2, 6, 144, 384), BF16),
        pltpu.VMEM((2, 288, 512), BF16), pltpu.VMEM((2, 144, 384), BF16), pltpu.VMEM((2, 576, 512), BF16),
        pltpu.VMEM((2, 288, 384), BF16),
        pltpu.VMEM((2, OWN, D), BF16), pltpu.VMEM((2, OWN, D), F32), pltpu.VMEM((2, 8, D), F32), pltpu.VMEM((8, D), F32),
        pltpu.VMEM((8, 8, D), F32), pltpu.VMEM((8, 8, D), F32),
        dma((10,)), dma((8,)), dma((8,)), dma((4, 2, 8)), dma((4, 2, 8)), dma((2, 2, 8)), dma((2, 2, 8)), dma((8, 2)), dma((8, 2, 2)),
        dma((8,)), dma((2, 8)), dma((2,)), dma((2,)), dma((2,)),
        dma((2, 2)), dma((2, 2)), dma((2, 2, 6)), dma((2, 2, 6)), dma((2, 2, 2)), dma((2, 2, 2)), dma((2, 2, 2, 3)),
        dma((2, 2, 4, 2)), dma((2, 2)), dma((2, 2, 2)), dma((2, 2, 2)), dma((3, 8)), dma((3, 8)),
    ]
    return pl.pallas_call(
        kernel,
        out_shape=(
            jax.ShapeDtypeStruct((2, OWN, D), BF16),
            jax.ShapeDtypeStruct((2, OWN, D), F32),
            jax.ShapeDtypeStruct((2, 4, 576, 512), BF16),
            jax.ShapeDtypeStruct((2, 4, 288, 384), BF16),
            jax.ShapeDtypeStruct((8, D), F32),
        ),
        in_specs=[hbm] * 10 + [vmem] * 3,
        out_specs=(hbm, hbm, hbm, hbm, vmem),
        scratch_shapes=scratch,
        compiler_params=pltpu.CompilerParams(
            collective_id=0, has_side_effects=True, vmem_limit_bytes=64 * 1024 * 1024 - 65536
        ),
        name="train_step",
    )(*args)


def widen(ga_ref, gb_ref, gate_ref, up_ref, down_ref, out_ref, query_ref, key_ref, value_ref):
    for h in range(2):
        rows = pl.ds(192 * h, 192)
        gate_ref[rows, :] = ga_ref[h, 0, 0:192, :].astype(F32)
        up_ref[rows, :] = ga_ref[h, 0, 192:384, :].astype(F32)
        for i in range(3):
            down_ref[pl.ds(64 * h, 64), pl.ds(512 * i, 512)] = ga_ref[h, 0, 384 + 64 * i : 448 + 64 * i, :].astype(F32)
    out_ref[...] = gb_ref[0, 0, 0:192, :].astype(F32)
    query_ref[0:HD, :] = gb_ref[0, 0, 192:288, :].astype(F32)
    query_ref[HD : 2 * HD, :] = gb_ref[1, 0, 0:HD, :].astype(F32)
    key_ref[...] = gb_ref[1, 0, HD : 2 * HD, :].astype(F32)
    value_ref[...] = gb_ref[1, 0, 2 * HD : 3 * HD, :].astype(F32)


def widened(ga, gb):
    shapes = [(D, FF), (D, FF), (FF, D), (192, D), (192, D), (HD, D), (HD, D)]
    by_row = [pl.BlockSpec((384, FF), lambda c: (c, 0)), pl.BlockSpec((384, FF), lambda c: (c, 0)), pl.BlockSpec((128, D), lambda c: (c, 0))]
    by_column = [pl.BlockSpec((rows, 384), lambda c: (0, c)) for rows in (192, 192, HD, HD)]
    return pl.pallas_call(
        widen,
        grid=(4,),
        out_shape=tuple(jax.ShapeDtypeStruct(shape, F32) for shape in shapes),
        in_specs=[pl.BlockSpec((2, 1, 576, 512), lambda c: (0, c, 0, 0)), pl.BlockSpec((2, 1, 288, 384), lambda c: (0, c, 0, 0))],
        out_specs=tuple(by_row + by_column),
        compiler_params=pltpu.CompilerParams(vmem_limit_bytes=40 * 1024 * 1024),
        name="widen",
    )(ga, gb)


def on_device(inputs, cotangent, doc_lengths, norm_one, query_w, key_w, value_w, out_w, norm_two, gate_w, up_w, down_w):
    gains = jnp.concatenate([jnp.broadcast_to(norm_one, (8, D)), jnp.broadcast_to(norm_two, (8, D))]).astype(F32)
    lengths = lax.dynamic_index_in_dim(doc_lengths, lax.axis_index("section"), 0, keepdims=False)
    starts = jnp.cumsum(lengths) - lengths
    i = jnp.arange(ROWS, dtype=jnp.int32)
    places = lax.axis_index("dp") * ROWS + OWN * ((i // HOWN) % 8) + HOWN * (i // HROWS) + i % HOWN
    begins = jnp.max(jnp.where(starts[None, :] <= places[:, None], starts[None, :], 0), axis=1)
    inverse = jnp.exp(jnp.arange(HALF, dtype=F32) * (-2.0 * math.log(ROPE) / HD))
    angles = (places - begins).astype(F32)[:, None] * inverse[None, :]
    cosine, sine = jnp.cos(angles), jnp.sin(angles)
    rest = jnp.zeros((ROWS, 128 - HD), F32)
    cosine = jnp.concatenate([cosine, cosine, rest], axis=1)
    sine = jnp.concatenate([-sine, sine, rest], axis=1)
    begins = jnp.broadcast_to(begins[:, None], (ROWS, 128))
    y, dx, ga, gb, gn = step_call(
        inputs, cotangent, query_w[0].T, key_w[0].T, value_w[0].T, out_w[0], gate_w[0], up_w[0], down_w[0], gains, cosine, sine, begins
    )
    gate, up, down, out, query, key, value = widened(ga, gb)
    return (
        y[None], dx[None], gn[0:1], query.T[None], key.T[None], value.T[None], out[None], gn[1:2], gate[None], up[None], down[None],
    )


def solution(mesh):
    in_specs = (
        P(None, "dp", None),
        P(None, "dp", None),
        P(),
        P("section", None),
        P("section", None, "tensor"),
        P("section", None, "tensor"),
        P("section", None, "tensor"),
        P("section", "tensor", None),
        P("section", None),
        P("section", None, "tensor"),
        P("section", None, "tensor"),
        P("section", "tensor", None),
    )
    out_specs = (
        P("section", None, ("dp", "tensor"), None),
        P("section", None, ("dp", "tensor"), None),
        P("section", None),
        P("section", None, "tensor"),
        P("section", None, "tensor"),
        P("section", None, "tensor"),
        P("section", "tensor", None),
        P("section", None),
        P("section", None, "tensor"),
        P("section", None, "tensor"),
        P("section", "tensor", None),
    )
    return jax.shard_map(on_device, mesh=mesh, in_specs=in_specs, out_specs=out_specs, check_vma=False)
```

```python
import math

import jax
import jax.numpy as jnp
from jax import lax
from jax.experimental import pallas as pl
from jax.experimental.pallas import tpu as pltpu
from jax.sharding import PartitionSpec as P

MESH = pl.DeviceIdType.MESH
F32 = jnp.float32
BF16 = jnp.bfloat16

HD = 96
HALF = HD // 2
D = 1536
FF = 512
ROWS = 256
OWN = 32
HROWS = 128
HOWN = 16
SCALE = 1.0 / math.sqrt(HD)
EPS = 1e-05
ROPE = 100000.0
MASKED = -1e30


def dot(a, b):
    return lax.dot_general(a, b, (((1,), (0,)), ((), ())), preferred_element_type=F32)


def dot_nt(a, b):
    return lax.dot_general(a, b, (((1,), (1,)), ((), ())), preferred_element_type=F32)


def dot_tn(a, b):
    return lax.dot_general(a, b, (((0,), (0,)), ((), ())), preferred_element_type=F32)


def lanes_of(v):
    return lax.broadcasted_iota(jnp.int32, v.shape, 1)


def swapped(v):
    return jnp.where(lanes_of(v) < HALF, pltpu.roll(v, 128 - HALF, 1), pltpu.roll(v, HALF, 1))


def factor_of(v):
    return lax.rsqrt(jnp.mean(v * v, axis=-1, keepdims=True) + EPS)


def kernel(
    x_hbm, ct_hbm, wq_hbm, wk_hbm, wv_hbm, wo_hbm, wg_hbm, wu_hbm, wd_hbm, gains_hbm, cos_ref, sin_ref, beg_ref,
    y_out, dx_out, ga_out, gb_out, gn_out,
    wqkv, wo, wgu, wd, gains, df,
    n1, n2, q2, q2t, kv, o_f, o_b, stat_m, stat_l, gate_s, up_s, u_s, x_own, h_own,
    rsrc, land, da, do2, do2t, dgu, dq, dqkv, dkv_t, dkv_src, dkv_land, acc, s_m,
    ga, gb, da_in, db_in, za, zb, xa, xb, fa, fb, yb, dxb, dgain, dg_peer, dg_t, dg_d,
    w_l, w_s, w_r, ag_s, ag_r, rs_s, rs_r, kv_s, kv_r, dkv_s, dkv_r, out_l, out_s, out_r,
    ds_s, ds_r, z_s, z_r, x_s, x_r, a_s, a_r, a_l, f_s, f_r, ns, nr,
):
    sec = lax.axis_index("section")
    t = lax.axis_index("tensor")
    d = lax.axis_index("dp")
    other = 1 - sec
    z, xh = d // 2, d % 2

    barrier = pltpu.get_barrier_semaphore()

    def greet(axis, me, k, _):
        pl.semaphore_signal(barrier, inc=1, device_id={axis: (me + k) % 8}, device_id_type=MESH)
        return _

    pl.semaphore_signal(barrier, inc=1, device_id={"section": other}, device_id_type=MESH)
    lax.fori_loop(1, 8, lambda k, c: greet("tensor", t, k, c), 0)
    lax.fori_loop(1, 8, lambda k, c: greet("dp", d, k, c), 0)

    def load_rows(source, sem):
        def body(i, c):
            h, p = i // 8, i % 8
            pltpu.make_async_copy(
                source.at[sec, pl.ds(pl.multiple_of(p * OWN + h * HOWN, HOWN), HOWN)],
                df.at[pl.ds(pl.multiple_of(h * HROWS + p * HOWN, HOWN), HOWN)], sem,
            ).start()
            return c

        lax.fori_loop(0, 16, body, 0)

    def rows_loaded(source, sem):
        pltpu.make_async_copy(source.at[sec], df, sem).wait()

    own_parts = [
        (wq_hbm, lambda i: wqkv.at[i, pl.ds(0, 2 * HD)]),
        (wk_hbm, lambda i: wqkv.at[i, pl.ds(2 * HD, HD)]),
        (wv_hbm, lambda i: wqkv.at[i, pl.ds(3 * HD, HD)]),
        (wo_hbm, lambda i: wo.at[i]),
        (wg_hbm, lambda i: wgu.at[i, :, 0:FF]),
        (wu_hbm, lambda i: wgu.at[i, :, FF : 2 * FF]),
        (wd_hbm, lambda i: wd.at[i]),
        (gains_hbm, lambda i: gains.at[i]),
    ]
    n_parts = len(own_parts)
    own_copies = [pltpu.make_async_copy(a, b(sec), w_l.at[i]) for i, (a, b) in enumerate(own_parts)]
    load_rows(x_hbm, w_l.at[8])
    own_copies[7].start()
    for i in range(7):
        own_copies[i].start()
    pl.semaphore_wait(barrier, 15)
    sent_parts = [
        pltpu.make_async_remote_copy(
            src_ref=a, dst_ref=b(sec), send_sem=w_s.at[i], recv_sem=w_r.at[i],
            device_id={"section": other}, device_id_type=MESH,
        )
        for i, (a, b) in enumerate(own_parts)
    ]
    for i in (7, 0, 1, 2, 3, 4, 5, 6):
        sent_parts[i].start()

    def weight_ready(layer, *which):
        @pl.when(layer == sec)
        def _():
            for i in which:
                own_copies[i].wait()

        @pl.when(layer != sec)
        def _():
            for i in which:
                a, b = own_parts[i]
                pltpu.make_async_remote_copy(
                    src_ref=a, dst_ref=b(other), send_sem=w_s.at[i], recv_sem=w_r.at[i],
                    device_id={"section": other}, device_id_type=MESH,
                ).wait_recv()

    def half_rows(half):
        return pl.ds(pl.multiple_of(half * HROWS, HROWS), HROWS)

    def pair_rows(half):
        return pl.ds(pl.multiple_of(half * ROWS, ROWS), ROWS)

    def rows_of(half, owner):
        return pl.ds(pl.multiple_of(half * HROWS + owner * HOWN, HOWN), HOWN)

    def kept(half):
        return pl.ds(pl.multiple_of(half * HOWN, HOWN), HOWN)

    def over_peers(body):
        def step(k, c):
            body((t + k) % 8)
            return c

        lax.fori_loop(1, 8, step, 0)

    def ag_copy(buf, i, half, to, owner):
        rows = rows_of(half, owner)
        return pltpu.make_async_remote_copy(
            src_ref=buf.at[rows], dst_ref=buf.at[rows], send_sem=ag_s.at[i, half, to], recv_sem=ag_r.at[i, half, owner],
            device_id={"tensor": to}, device_id_type=MESH,
        )

    def ag_start(buf, i, half):
        over_peers(lambda p: ag_copy(buf, i, half, p, t).start())

    def ag_wait(buf, i, half):
        over_peers(lambda p: ag_copy(buf, i, half, t, p).wait_recv())

    def ag_sent(buf, i, half):
        over_peers(lambda p: ag_copy(buf, i, half, p, t).wait_send())

    def rs_copy(i, half, to, sender):
        return pltpu.make_async_remote_copy(
            src_ref=rsrc.at[i, rows_of(half, to)], dst_ref=land.at[i, half, sender], send_sem=rs_s.at[i, half, to],
            recv_sem=rs_r.at[i, half, sender], device_id={"tensor": to}, device_id_type=MESH,
        )

    def rs_start(i, half):
        over_peers(lambda p: rs_copy(i, half, p, t).start())

    def rs_sum(i, half):
        def body(k, total):
            p = (t + k) % 8
            rs_copy(i, half, t, p).wait_recv()
            return total + land[i, half, p].astype(F32)

        return lax.fori_loop(1, 8, body, rsrc[i, rows_of(half, t), :].astype(F32))

    def rs_sent(i, half):
        over_peers(lambda p: rs_copy(i, half, p, t).wait_send())

    def both(body):
        def step(half, c):
            body(half)
            return c

        lax.fori_loop(0, 2, step, 0)

    def place_of(i):
        return OWN * ((i // HOWN) % 8) + HOWN * (i // HROWS) + i % HOWN

    def allowed_of(j, half):
        rows = place_of(lax.broadcasted_iota(jnp.int32, (HROWS, 1), 0) + half * HROWS) + d * ROWS
        cols = place_of(lax.broadcasted_iota(jnp.int32, (1, ROWS), 1)) + j * ROWS
        allowed = (cols <= rows) & (cols >= beg_ref[half_rows(half), 0:1])
        return jnp.concatenate([jnp.where(allowed, 0.0, MASKED)] * 2, axis=0)

    weight_ready(0, 7)
    rows_loaded(x_hbm, w_l.at[8])

    def first_norm(i, c):
        rows = pl.ds(pl.multiple_of(i * OWN, OWN), OWN)
        v = df[rows, :].astype(F32)
        n1[0, rows, :] = (v * factor_of(v) * gains[0, 0:1, :]).astype(BF16)
        return c

    lax.fori_loop(0, ROWS // OWN, first_norm, 0)
    for half in range(2):
        x_own[0, kept(half), :] = df[rows_of(half, t), :].astype(F32)
    load_rows(ct_hbm, w_l.at[9])

    def forward_layer(layer, c):
        weight_ready(layer, 0, 1, 2)

        def kv_copy(owner, to, half):
            part = kv.at[layer, owner, :, half_rows(half)]
            return pltpu.make_async_remote_copy(
                src_ref=part, dst_ref=part, send_sem=kv_s.at[to, half], recv_sem=kv_r.at[owner, layer, half],
                device_id={"dp": to}, device_id_type=MESH,
            )

        def project(half):
            rows = half_rows(half)

            @pl.when(layer == 1)
            def _():
                ag_wait(n1.at[1], 0, half)

            raw = dot_nt(n1[layer, rows, :], wqkv[layer])
            c0, c1, c2 = raw[:, 0:128], raw[:, 128:256], raw[:, 256:384]
            lane = lanes_of(c0)
            q1 = jnp.where(lane < 32, pltpu.roll(c0, 32, 1), pltpu.roll(c1, 32, 1))
            k0 = jnp.where(lane < 64, pltpu.roll(c1, 64, 1), pltpu.roll(c2, 64, 1))
            v0 = pltpu.roll(c2, 96, 1)
            cosine, sine = cos_ref[rows, :], sin_ref[rows, :]
            turned = k0 * cosine + swapped(k0) * sine
            kv[layer, d, pl.ds(0, HD), rows] = jnp.transpose(turned)[0:HD, :].astype(BF16)
            kv[layer, d, pl.ds(HD, HD), rows] = jnp.transpose(v0)[0:HD, :].astype(BF16)

            def kv_send(k, c):
                kv_copy(d, k, half).start()
                return c

            lax.fori_loop(d + 1, 8, kv_send, 0)
            for h, part in ((0, c0), (1, q1)):
                turned = part * cosine + swapped(part) * sine
                place = pl.ds(pl.multiple_of(half * ROWS + h * HROWS, HROWS), HROWS)
                q2[layer, place, :] = turned[:, 0:HD].astype(BF16)
                q2t[layer, :, place] = jnp.transpose(turned)[0:HD, :].astype(BF16)

        both(project)

        @pl.when(layer == 1)
        def _():
            both(lambda half: ag_sent(n1.at[1], 0, half))

        weight_ready(layer, 3)

        def attend_half(half):
            rows = pair_rows(half)
            s_m[rows, :] = jnp.full((ROWS, 1), MASKED, F32)
            stat_l[layer, rows, :] = jnp.zeros((ROWS, 1), F32)
            acc[rows, :] = jnp.zeros((ROWS, HD), F32)

            def attend(i, c):
                j = d - i

                @pl.when((i > 0) & (half == 0))
                def _():
                    kv_copy(j, d, 0).wait_recv()
                    kv_copy(j, d, 1).wait_recv()

                s = dot(q2[layer, rows, :], kv[layer, j, pl.ds(0, HD), :]) * SCALE + allowed_of(j, half)
                old = s_m[rows, :]
                new = jnp.maximum(old, jnp.max(s, axis=-1, keepdims=True))
                p = jnp.exp(s - new)
                shrink = jnp.exp(old - new)
                s_m[rows, :] = new
                stat_l[layer, rows, :] = stat_l[layer, rows, :] * shrink + jnp.sum(p, axis=-1, keepdims=True)
                acc[rows, :] = acc[rows, :] * shrink + dot_nt(p.astype(BF16), kv[layer, j, pl.ds(HD, HD), :])
                return c

            lax.fori_loop(0, d + 1, attend, 0)
            total = stat_l[layer, rows, :]
            mixed = acc[rows, :] / total
            o_f[layer, rows, :] = mixed
            o_b[layer, rows, :] = mixed.astype(BF16)
            stat_m[layer, rows, :] = s_m[rows, :] + jnp.log(total)
            first = pl.ds(pl.multiple_of(half * ROWS, HROWS), HROWS)
            second = pl.ds(pl.multiple_of(half * ROWS + HROWS, HROWS), HROWS)

            def out_part(n, c):
                cols = pl.ds(pl.multiple_of(n * 512, 512), 512)
                part = dot(o_b[layer, first, :], wo[layer, pl.ds(0, HD), cols])
                part += dot(o_b[layer, second, :], wo[layer, pl.ds(HD, HD), cols])
                rsrc[0, half_rows(half), cols] = part.astype(BF16)
                return c

            lax.fori_loop(0, 3, out_part, 0)
            rs_start(0, half)

        both(attend_half)

        def kv_sent(k, c):
            kv_copy(d, k, 0).wait_send()
            kv_copy(d, k, 1).wait_send()
            return c

        lax.fori_loop(d + 1, 8, kv_sent, 0)

        def middle(half):
            v = x_own[layer, kept(half), :] + rs_sum(0, half)
            h_own[layer, kept(half), :] = v
            n2[layer, rows_of(half, t), :] = (v * factor_of(v) * gains[layer, 8:9, :]).astype(BF16)
            ag_start(n2.at[layer], 1, half)
            rs_sent(0, half)

        both(middle)
        weight_ready(layer, 4, 5)
        weight_ready(layer, 6)

        def feed(half):
            rows = half_rows(half)
            ag_wait(n2.at[layer], 1, half)

            def units(n, c):
                cols = pl.ds(pl.multiple_of(n * 256, 256), 256)
                above = pl.ds(pl.multiple_of(n * 256 + FF, 256), 256)
                g = dot(n2[layer, rows, :], wgu[layer, :, cols])
                up = dot(n2[layer, rows, :], wgu[layer, :, above])
                gate_s[layer, rows, cols] = g
                up_s[layer, rows, cols] = up
                u_s[layer, rows, cols] = (g * jax.nn.sigmoid(g) * up).astype(BF16)
                return c

            lax.fori_loop(0, 2, units, 0)

            def down_part(n, c):
                cols = pl.ds(pl.multiple_of(n * 512, 512), 512)
                rsrc[1, rows, cols] = dot(u_s[layer, rows, :], wd[layer, :, cols]).astype(BF16)
                return c

            lax.fori_loop(0, 3, down_part, 0)
            rs_start(1, half)
            ag_sent(n2.at[layer], 1, half)

        both(feed)

        @pl.when(layer == 0)
        def _():
            weight_ready(1, 7)

        def result(half):
            y = (h_own[layer, kept(half), :] + rs_sum(1, half)).astype(BF16)
            yb[layer, kept(half), :] = y

            @pl.when(layer == 0)
            def _():
                v = y.astype(F32)
                x_own[1, kept(half), :] = v
                n1[1, rows_of(half, t), :] = (v * factor_of(v) * gains[1, 0:1, :]).astype(BF16)
                ag_start(n1.at[1], 0, half)

            rs_sent(1, half)

        both(result)
        row_out(layer, yb, y_out, 0)
        return c

    def row_out(layer, buf, out, i):
        @pl.when(layer == sec)
        def _():
            pltpu.make_async_copy(buf.at[layer], out.at[sec], out_l.at[i]).start()

        @pl.when(layer != sec)
        def _():
            pltpu.make_async_remote_copy(
                src_ref=buf.at[layer], dst_ref=out.at[sec], send_sem=out_s.at[i], recv_sem=out_r.at[i],
                device_id={"section": other}, device_id_type=MESH,
            ).start()

    def row_out_wait(buf, out, i):
        pltpu.make_async_copy(buf.at[sec], out.at[sec], out_l.at[i]).wait()
        copy = pltpu.make_async_remote_copy(
            src_ref=buf.at[other], dst_ref=out.at[other], send_sem=out_s.at[i], recv_sem=out_r.at[i],
            device_id={"section": other}, device_id_type=MESH,
        )
        copy.wait_send()
        copy.wait_recv()

    lax.fori_loop(0, 2, forward_layer, 0)

    rows_loaded(ct_hbm, w_l.at[9])

    sets = ((ga, da_in, za, xa, fa, ga_out), (gb, db_in, zb, xb, fb, gb_out))
    before, after = (z + 3) % 4, (z + 1) % 4
    far = (z + 2) % 4

    def dp_at(zz, xx):
        return zz * 2 + xx

    def quarter(i, which):
        size = (288, 144)[i]
        return pl.ds(pl.multiple_of(which * size, 16), size)

    def swap_cores(layer, i):
        return pltpu.make_async_remote_copy(
            src_ref=sets[i][0].at[layer, other], dst_ref=sets[i][1].at[layer], send_sem=ds_s.at[i, layer],
            recv_sem=ds_r.at[i, layer], device_id={"section": other}, device_id_type=MESH,
        )

    def add_rows(target, index, first, size, sources):
        count = 96 if size % 96 == 0 else 48

        def add(n, carry):
            here = pl.ds(pl.multiple_of(first + n * count, 16), count)
            total = target[(*index, here)].astype(F32)
            for ref, place, start in sources:
                total += ref[(*place, pl.ds(pl.multiple_of(start + n * count, 16), count))].astype(F32)
            target[(*index, here)] = total.astype(BF16)
            return carry

        lax.fori_loop(0, size // count, add, 0)

    def z_piece(layer, i, piece, chunk, which, to):
        return pltpu.make_async_remote_copy(
            src_ref=sets[i][0].at[layer, sec, chunk, quarter(i, which)], dst_ref=sets[i][2].at[layer, piece],
            send_sem=z_s.at[i, layer, piece], recv_sem=z_r.at[i, layer, piece], device_id={"dp": dp_at(to, xh)},
            device_id_type=MESH,
        )

    def sum_1(layer, i):
        g, arrived = sets[i][0:2]
        swap_cores(layer, i).wait_recv()
        for chunk, sends in (
            (far, ((0, 0, after), (1, 1, before))),
            (after, ((2, 1, after),)),
            (before, ((3, 0, before),)),
            (z, ()),
        ):
            add_rows(g, (layer, sec, chunk), 0, g.shape[3], [(arrived, (layer, chunk), 0)])
            for piece, which, to in sends:
                z_piece(layer, i, piece, chunk, which, to).start()

    def sum_2(layer, i):
        g, landed = sets[i][0], sets[i][2]
        size = landed.shape[2]
        z_piece(layer, i, 0, far, 0, after).wait_recv()
        add_rows(g, (layer, sec, after), 0, size, [(landed, (layer, 0), 0)])
        z_piece(layer, i, 4, after, 0, after).start()
        z_piece(layer, i, 1, far, 1, before).wait_recv()
        add_rows(g, (layer, sec, before), size, size, [(landed, (layer, 1), 0)])
        z_piece(layer, i, 5, before, 1, before).start()

    def x_over(layer, i):
        return pltpu.make_async_remote_copy(
            src_ref=sets[i][0].at[layer, sec, z, quarter(i, 1 - xh)], dst_ref=sets[i][3].at[layer],
            send_sem=x_s.at[i, 0, layer], recv_sem=x_r.at[i, 0, layer], device_id={"dp": dp_at(z, 1 - xh)},
            device_id_type=MESH,
        )

    def x_back(layer, i, which):
        part = sets[i][4].at[layer, quarter(i, which)]
        return pltpu.make_async_remote_copy(
            src_ref=part, dst_ref=part, send_sem=x_s.at[i, 1, layer], recv_sem=x_r.at[i, 1, layer],
            device_id={"dp": dp_at(z, 1 - xh)}, device_id_type=MESH,
        )

    def sum_3(layer, i):
        g, landed = sets[i][0], sets[i][2]
        size = landed.shape[2]
        for piece in (2, 3, 4, 5):
            z_piece(layer, i, piece, z, 0, after).wait_recv()
        add_rows(g, (layer, sec, z), 0, size, [(landed, (layer, 3), 0), (landed, (layer, 4), 0)])
        add_rows(g, (layer, sec, z), size, size, [(landed, (layer, 2), 0), (landed, (layer, 5), 0)])
        x_over(layer, i).start()

    def spread(layer, i, half, chunk, which, to, k):
        rows = quarter(i, which)
        return pltpu.make_async_remote_copy(
            src_ref=sets[i][4].at[layer, rows], dst_ref=sets[i][5].at[half, chunk, rows], send_sem=a_s.at[i, layer, which, k],
            recv_sem=a_r.at[i, half, chunk, which], device_id={"section": layer, "dp": dp_at(to, xh)}, device_id_type=MESH,
        )

    def keep(layer, i, which):
        rows = quarter(i, which)
        return pltpu.make_async_copy(sets[i][4].at[layer, rows], sets[i][5].at[sec, z, rows], a_l.at[i, which])

    def spread_all(layer, i, which):
        spread(layer, i, sec, z, which, after, 0).start()
        spread(layer, i, sec, z, which, before, 1).start()

        @pl.when(layer == sec)
        def _():
            keep(layer, i, which).start()

        @pl.when(layer != sec)
        def _():
            spread(layer, i, sec, z, which, z, 2).start()

    def sum_4(layer, i):
        g, over, done = sets[i][0], sets[i][3], sets[i][4]
        size = over.shape[1]
        x_over(layer, i).wait_recv()

        def add(n, carry):
            here = pl.ds(pl.multiple_of(n * 48, 16), 48)
            there = pl.ds(pl.multiple_of(xh * size + n * 48, 16), 48)
            done[layer, there, :] = (g[layer, sec, z, there, :].astype(F32) + over[layer, here, :].astype(F32)).astype(BF16)
            return carry

        lax.fori_loop(0, size // 48, add, 0)
        x_back(layer, i, xh).start()
        spread_all(layer, i, xh)

    def sum_5(layer, i):
        x_back(layer, i, 1 - xh).wait_recv()
        spread_all(layer, i, 1 - xh)

    def pass_on(i, half, chunk, which, to):
        part = sets[i][5].at[half, chunk, quarter(i, which)]
        return pltpu.make_async_remote_copy(
            src_ref=part, dst_ref=part, send_sem=f_s.at[i, half, which], recv_sem=f_r.at[i, half, which],
            device_id={"dp": dp_at(to, xh)}, device_id_type=MESH,
        )

    def sum_6(i):
        for half in range(2):
            spread(sec, i, half, before, 0, z, 0).wait_recv()
            pass_on(i, half, before, 0, after).start()
            spread(sec, i, half, after, 1, z, 0).wait_recv()
            pass_on(i, half, after, 1, before).start()

    def sum_7(i):
        for which in range(2):
            keep(sec, i, which).wait()
            spread(sec, i, other, z, which, z, 2).wait_recv()
            spread(other, i, sec, z, which, z, 2).wait_send()
            for half in range(2):
                spread(sec, i, half, (after, before)[which], which, z, 0).wait_recv()
                pass_on(i, half, far, which, z).wait_recv()
                pass_on(i, half, z, which, after).wait_send()
        for layer in range(2):
            swap_cores(layer, i).wait_send()
            for piece in range(6):
                z_piece(layer, i, piece, z, 0, after).wait_send()
            x_over(layer, i).wait_send()
            x_back(layer, i, xh).wait_send()
            for which in range(2):
                spread(layer, i, sec, z, which, after, 0).wait_send()
                spread(layer, i, sec, z, which, before, 1).wait_send()

    def backward_layer(step, c):
        layer = 1 - step

        @pl.when(step == 1)
        def _():
            sum_1(1, 1)
            sum_4(1, 0)

        def feed_back(half):
            rows = half_rows(half)

            @pl.when(step == 1)
            def _():
                ag_wait(df, 2, half)

            dxb[layer, kept(half), :] = df[rows_of(half, t), :].astype(F32)

            def unit_grads(n, c):
                cols = pl.ds(pl.multiple_of(n * 256, 256), 256)
                above = pl.ds(pl.multiple_of(n * 256 + FF, 256), 256)
                du = dot_nt(df[rows, :], wd[layer, cols, :])
                g, up = gate_s[layer, rows, cols], up_s[layer, rows, cols]
                sig = jax.nn.sigmoid(g)
                dgu[rows, cols] = (du * up * sig * (1.0 + g * (1.0 - sig))).astype(BF16)
                dgu[rows, above] = (du * g * sig).astype(BF16)
                return c

            lax.fori_loop(0, 2, unit_grads, 0)

            def normed_part(n, c):
                cols = pl.ds(pl.multiple_of(n * 256, 256), 256)
                rsrc[0, rows, cols] = dot_nt(dgu[rows, :], wgu[layer, cols, :]).astype(BF16)
                return c

            lax.fori_loop(0, 6, normed_part, 0)
            rs_start(0, half)

        both(feed_back)

        @pl.when(step == 1)
        def _():
            both(lambda half: ag_sent(df, 2, half))

        def unit_weights(n, c):
            cols = pl.ds(pl.multiple_of(n * 384, 384), 384)
            got = dot_tn(n2[layer, :, cols], dgu[...]).astype(BF16)
            for h in range(2):
                ga[layer, h, n, pl.ds(0, 192), :] = got[192 * h : 192 * h + 192, 0:FF]
                ga[layer, h, n, pl.ds(192, 192), :] = got[192 * h : 192 * h + 192, FF : 2 * FF]
            cols = pl.ds(pl.multiple_of(n * 128, 128), 128)
            got = dot_tn(u_s[layer, :, cols], df[...]).astype(BF16)
            for h in range(2):
                for i in range(3):
                    ga[layer, h, n, pl.ds(384 + 64 * i, 64), :] = got[64 * h : 64 * h + 64, 512 * i : 512 * i + 512]
            return c

        lax.fori_loop(0, 4, unit_weights, 0)
        swap_cores(layer, 0).start()

        @pl.when(step == 1)
        def _():
            sum_5(1, 0)
            sum_2(1, 1)

        def hidden_grads(half):
            dn = rs_sum(0, half)
            h = h_own[layer, kept(half), :]
            r = factor_of(h)
            tt = dn * gains[layer, 8:9, :]
            dh = dxb[layer, kept(half), :] + r * tt - h * (r * r * r * jnp.mean(h * tt, axis=-1, keepdims=True))
            dgain[layer, 1:2, :] += jnp.sum(dn * h * r, axis=0, keepdims=True)
            dxb[layer, kept(half), :] = dh
            da[rows_of(half, t), :] = dh.astype(BF16)
            ag_start(da, 3, half)
            rs_sent(0, half)

        both(hidden_grads)
        sum_1(layer, 0)

        @pl.when(step == 1)
        def _():
            sum_3(1, 1)

        def mixed_grads(half):
            ag_wait(da, 3, half)
            for h in range(2):
                place = pl.ds(pl.multiple_of(half * ROWS + h * HROWS, HROWS), HROWS)
                got = dot_nt(da[half_rows(half), :], wo[layer, pl.ds(h * HD, HD), :])
                do2[place, :] = got.astype(BF16)
                padded = jnp.concatenate([got, jnp.zeros((HROWS, 128 - HD), F32)], axis=1)
                do2t[:, place] = jnp.transpose(padded)[0:HD, :].astype(BF16)

        both(mixed_grads)
        both(lambda half: ag_sent(da, 3, half))
        dot_rows = jnp.sum(do2[...].astype(F32) * o_f[layer], axis=-1, keepdims=True)
        s_m[...] = dot_rows
        acc[...] = jnp.zeros(acc.shape, F32)

        def dkv_copy(to, sender):
            return pltpu.make_async_remote_copy(
                src_ref=dkv_src.at[to], dst_ref=dkv_land.at[layer, sender], send_sem=dkv_s.at[to], recv_sem=dkv_r.at[layer, sender],
                device_id={"dp": to}, device_id_type=MESH,
            )

        def attend_back(j, c):
            dkt = jnp.zeros((HD, ROWS), F32)
            dvt = jnp.zeros((HD, ROWS), F32)
            for half in range(2):
                rows = pair_rows(half)
                kt = kv[layer, j, pl.ds(0, HD), :]
                s = dot(q2[layer, rows, :], kt) * SCALE + allowed_of(j, half)
                p = jnp.exp(s - stat_m[layer, rows, :])
                dp = dot(do2[rows, :], kv[layer, j, pl.ds(HD, HD), :])
                ds = (p * (dp - s_m[rows, :])).astype(BF16)
                acc[rows, :] += dot_nt(ds, kt)
                dkt += dot(q2t[layer, :, rows], ds)
                dvt += dot(do2t[:, rows], p.astype(BF16))
            dkv_src[j, pl.ds(0, HD), :] = (dkt * SCALE).astype(BF16)
            dkv_src[j, pl.ds(HD, HD), :] = dvt.astype(BF16)

            @pl.when(j < d)
            def _():
                dkv_copy(j, d).start()

            return c

        lax.fori_loop(0, d + 1, attend_back, 0)

        def dkv_sent(k, c):
            dkv_copy(k, d).wait_send()
            return c

        def out_weights(n, c):
            cols = pl.ds(pl.multiple_of(n * 384, 384), 384)
            for h in range(2):
                mixed = [o_b[layer, pl.ds(half * ROWS + h * HROWS, HROWS), :] for half in range(2)]
                got = dot_tn(jnp.concatenate(mixed, axis=0), da[:, cols])
                gb[layer, 0, n, pl.ds(h * HD, HD), :] = got.astype(BF16)
            return c

        lax.fori_loop(0, 4, out_weights, 0)
        lax.fori_loop(0, d, dkv_sent, 0)

        sum_2(layer, 0)

        @pl.when(step == 1)
        def _():
            sum_4(1, 1)

        def dkv_sum(k, total):
            dkv_copy(d, k).wait_recv()
            return total + dkv_land[layer, k].astype(F32)

        dkv_total = lax.fori_loop(d + 1, 8, dkv_sum, dkv_src[d].astype(F32))
        dkv_t[...] = jnp.zeros(dkv_t.shape, F32)
        dkv_t[0, pl.ds(0, HD), :] = dkv_total[0:HD]
        dkv_t[1, pl.ds(0, HD), :] = dkv_total[HD : 2 * HD]
        dk_rot = jnp.transpose(dkv_t[0])
        dv = jnp.transpose(dkv_t[1])
        cosine, sine = cos_ref[...], sin_ref[...]
        dq[...] = jnp.zeros(dq.shape, F32)
        dq[:, 0:HD] = acc[...] * SCALE
        dq0, dq1 = (
            jnp.concatenate([dq[pl.ds(half * ROWS + h * HROWS, HROWS), :] for half in range(2)], axis=0) for h in range(2)
        )
        dq0 = dq0 * cosine - swapped(dq0) * sine
        dq1 = dq1 * cosine - swapped(dq1) * sine
        dk = dk_rot * cosine - swapped(dk_rot) * sine
        lane = lanes_of(dk)
        dqkv[:, 0:128] = jnp.where(lane < HD, dq0, pltpu.roll(dq1, 96, 1)).astype(BF16)
        dqkv[:, 128:256] = jnp.where(lane < 64, pltpu.roll(dq1, 96, 1), pltpu.roll(dk, 64, 1)).astype(BF16)
        dqkv[:, 256:384] = jnp.where(lane < 32, pltpu.roll(dk, 64, 1), pltpu.roll(dv, 32, 1)).astype(BF16)

        def project_back(half):
            rows = half_rows(half)

            def input_part(n, c):
                cols = pl.ds(pl.multiple_of(n * 512, 512), 512)
                rsrc[1, rows, cols] = dot(dqkv[rows, :], wqkv[layer, :, cols]).astype(BF16)
                return c

            lax.fori_loop(0, 3, input_part, 0)
            rs_start(1, half)

        both(project_back)

        def qkv_weights(n, c):
            cols = pl.ds(pl.multiple_of(n * 384, 384), 384)
            got = dot_tn(dqkv[...], n1[layer, :, cols]).astype(BF16)
            gb[layer, 0, n, pl.ds(2 * HD, HD), :] = got[0:HD]
            gb[layer, 1, n] = got[HD : 4 * HD]
            return c

        lax.fori_loop(0, 4, qkv_weights, 0)
        swap_cores(layer, 1).start()
        sum_3(layer, 0)

        @pl.when(step == 1)
        def _():
            sum_5(1, 1)

            @pl.when(sec == 1)
            def _():
                sum_6(0)

        def input_grads(half):
            dn = rs_sum(1, half)
            v = x_own[layer, kept(half), :]
            r = factor_of(v)
            tt = dn * gains[layer, 0:1, :]
            dx = dxb[layer, kept(half), :] + r * tt - v * (r * r * r * jnp.mean(v * tt, axis=-1, keepdims=True))
            dgain[layer, 0:1, :] += jnp.sum(dn * v * r, axis=0, keepdims=True)
            dxb[layer, kept(half), :] = dx

            @pl.when(step == 0)
            def _():
                df[rows_of(half, t), :] = dx.astype(BF16)
                ag_start(df, 2, half)

            rs_sent(1, half)

        both(input_grads)
        row_out(layer, dxb, dx_out, 1)
        return c

    dgain[...] = jnp.zeros(dgain.shape, F32)
    lax.fori_loop(0, 2, backward_layer, 0)

    mate = pltpu.make_async_remote_copy(
        src_ref=dgain.at[other], dst_ref=dg_peer, send_sem=ns.at[0, 0], recv_sem=nr.at[0, 0],
        device_id={"section": other}, device_id_type=MESH,
    )
    mate.start()
    sum_4(0, 0)
    sum_1(0, 1)

    @pl.when(sec == 1)
    def _():
        sum_6(1)


    def gain_copy(axis, i, buf, me, to, sender):
        return pltpu.make_async_remote_copy(
            src_ref=buf.at[me], dst_ref=buf.at[sender], send_sem=ns.at[i, to], recv_sem=nr.at[i, sender],
            device_id={axis: to}, device_id_type=MESH,
        )

    def gain_send(axis, i, buf, me):
        def send(k, c):
            gain_copy(axis, i, buf, me, (me + k) % 8, me).start()
            return c

        lax.fori_loop(1, 8, send, 0)

    def gain_sum(axis, i, buf, me):
        def take(k, total):
            p = (me + k) % 8
            gain_copy(axis, i, buf, me, p, p).wait_recv()
            return total + buf[p]

        def sent(k, c):
            gain_copy(axis, i, buf, me, (me + k) % 8, me).wait_send()
            return c

        total = lax.fori_loop(1, 8, take, buf[me])
        lax.fori_loop(1, 8, sent, 0)
        return total

    mate.wait_recv()
    mate.wait_send()
    dg_t[t] = dgain[sec] + dg_peer[...]
    gain_send("tensor", 1, dg_t, t)
    sum_5(0, 0)
    sum_2(0, 1)
    dg_d[d] = gain_sum("tensor", 1, dg_t, t)
    gain_send("dp", 2, dg_d, d)
    sum_3(0, 1)

    @pl.when(sec == 0)
    def _():
        sum_6(0)

    sum_4(0, 1)
    sum_5(0, 1)

    @pl.when(sec == 0)
    def _():
        sum_6(1)

    gn_out[...] = gain_sum("dp", 2, dg_d, d)
    sum_7(0)
    sum_7(1)
    row_out_wait(yb, y_out, 0)
    row_out_wait(dxb, dx_out, 1)
    for i in range(n_parts):
        sent_parts[i].wait_send()


def step_call(*args):
    hbm = pl.BlockSpec(memory_space=pl.ANY)
    vmem = pl.BlockSpec(memory_space=pltpu.VMEM)
    dma = pltpu.SemaphoreType.DMA
    scratch = [
        pltpu.VMEM((2, 384, D), BF16), pltpu.VMEM((2, 192, D), BF16), pltpu.VMEM((2, D, 2 * FF), BF16),
        pltpu.VMEM((2, FF, D), BF16), pltpu.VMEM((2, 16, D), F32), pltpu.VMEM((ROWS, D), BF16),
        pltpu.VMEM((2, ROWS, D), BF16), pltpu.VMEM((2, ROWS, D), BF16), pltpu.VMEM((2, 2 * ROWS, HD), BF16),
        pltpu.VMEM((2, HD, 2 * ROWS), BF16), pltpu.VMEM((2, 8, 2 * HD, ROWS), BF16), pltpu.VMEM((2, 2 * ROWS, HD), F32),
        pltpu.VMEM((2, 2 * ROWS, HD), BF16), pltpu.VMEM((2, 2 * ROWS, 1), F32), pltpu.VMEM((2, 2 * ROWS, 1), F32),
        pltpu.VMEM((2, ROWS, FF), F32), pltpu.VMEM((2, ROWS, FF), F32), pltpu.VMEM((2, ROWS, FF), BF16),
        pltpu.VMEM((2, OWN, D), F32), pltpu.VMEM((2, OWN, D), F32),
        pltpu.VMEM((2, ROWS, D), BF16), pltpu.VMEM((2, 2, 8, HOWN, D), BF16), pltpu.VMEM((ROWS, D), BF16),
        pltpu.VMEM((2 * ROWS, HD), BF16), pltpu.VMEM((HD, 2 * ROWS), BF16), pltpu.VMEM((ROWS, 2 * FF), BF16),
        pltpu.VMEM((2 * ROWS, 128), F32), pltpu.VMEM((ROWS, 384), BF16), pltpu.VMEM((2, 128, ROWS), F32),
        pltpu.VMEM((8, 2 * HD, ROWS), BF16), pltpu.VMEM((2, 8, 2 * HD, ROWS), BF16), pltpu.VMEM((2 * ROWS, HD), F32),
        pltpu.VMEM((2 * ROWS, 1), F32),
        pltpu.VMEM((2, 2, 4, 576, 512), BF16), pltpu.VMEM((2, 2, 4, 288, 384), BF16), pltpu.VMEM((2, 4, 576, 512), BF16),
        pltpu.VMEM((2, 4, 288, 384), BF16), pltpu.VMEM((2, 6, 288, 512), BF16), pltpu.VMEM((2, 6, 144, 384), BF16),
        pltpu.VMEM((2, 288, 512), BF16), pltpu.VMEM((2, 144, 384), BF16), pltpu.VMEM((2, 576, 512), BF16),
        pltpu.VMEM((2, 288, 384), BF16),
        pltpu.VMEM((2, OWN, D), BF16), pltpu.VMEM((2, OWN, D), F32), pltpu.VMEM((2, 8, D), F32), pltpu.VMEM((8, D), F32),
        pltpu.VMEM((8, 8, D), F32), pltpu.VMEM((8, 8, D), F32),
        dma((10,)), dma((8,)), dma((8,)), dma((4, 2, 8)), dma((4, 2, 8)), dma((2, 2, 8)), dma((2, 2, 8)), dma((8, 2)), dma((8, 2, 2)),
        dma((8,)), dma((2, 8)), dma((2,)), dma((2,)), dma((2,)),
        dma((2, 2)), dma((2, 2)), dma((2, 2, 6)), dma((2, 2, 6)), dma((2, 2, 2)), dma((2, 2, 2)), dma((2, 2, 2, 3)),
        dma((2, 2, 4, 2)), dma((2, 2)), dma((2, 2, 2)), dma((2, 2, 2)), dma((3, 8)), dma((3, 8)),
    ]
    return pl.pallas_call(
        kernel,
        out_shape=(
            jax.ShapeDtypeStruct((2, OWN, D), BF16),
            jax.ShapeDtypeStruct((2, OWN, D), F32),
            jax.ShapeDtypeStruct((2, 4, 576, 512), BF16),
            jax.ShapeDtypeStruct((2, 4, 288, 384), BF16),
            jax.ShapeDtypeStruct((8, D), F32),
        ),
        in_specs=[hbm] * 10 + [vmem] * 3,
        out_specs=(hbm, hbm, hbm, hbm, vmem),
        scratch_shapes=scratch,
        compiler_params=pltpu.CompilerParams(
            collective_id=0, has_side_effects=True, vmem_limit_bytes=64 * 1024 * 1024 - 65536
        ),
        name="train_step",
    )(*args)


def widen(ga_ref, gb_ref, gate_ref, up_ref, down_ref, out_ref, query_ref, key_ref, value_ref):
    for h in range(2):
        rows = pl.ds(192 * h, 192)
        gate_ref[rows, :] = ga_ref[h, 0, 0:192, :].astype(F32)
        up_ref[rows, :] = ga_ref[h, 0, 192:384, :].astype(F32)
        for i in range(3):
            down_ref[pl.ds(64 * h, 64), pl.ds(512 * i, 512)] = ga_ref[h, 0, 384 + 64 * i : 448 + 64 * i, :].astype(F32)
    out_ref[...] = gb_ref[0, 0, 0:192, :].astype(F32)
    query_ref[0:HD, :] = gb_ref[0, 0, 192:288, :].astype(F32)
    query_ref[HD : 2 * HD, :] = gb_ref[1, 0, 0:HD, :].astype(F32)
    key_ref[...] = gb_ref[1, 0, HD : 2 * HD, :].astype(F32)
    value_ref[...] = gb_ref[1, 0, 2 * HD : 3 * HD, :].astype(F32)


def widened(ga, gb):
    shapes = [(D, FF), (D, FF), (FF, D), (192, D), (192, D), (HD, D), (HD, D)]
    by_row = [pl.BlockSpec((384, FF), lambda c: (c, 0)), pl.BlockSpec((384, FF), lambda c: (c, 0)), pl.BlockSpec((128, D), lambda c: (c, 0))]
    by_column = [pl.BlockSpec((rows, 384), lambda c: (0, c)) for rows in (192, 192, HD, HD)]
    return pl.pallas_call(
        widen,
        grid=(4,),
        out_shape=tuple(jax.ShapeDtypeStruct(shape, F32) for shape in shapes),
        in_specs=[pl.BlockSpec((2, 1, 576, 512), lambda c: (0, c, 0, 0)), pl.BlockSpec((2, 1, 288, 384), lambda c: (0, c, 0, 0))],
        out_specs=tuple(by_row + by_column),
        compiler_params=pltpu.CompilerParams(vmem_limit_bytes=63 * 1024 * 1024),
        name="widen",
    )(ga, gb)


def on_device(inputs, cotangent, doc_lengths, norm_one, query_w, key_w, value_w, out_w, norm_two, gate_w, up_w, down_w):
    gains = jnp.concatenate([jnp.broadcast_to(norm_one, (8, D)), jnp.broadcast_to(norm_two, (8, D))]).astype(F32)
    lengths = lax.dynamic_index_in_dim(doc_lengths, lax.axis_index("section"), 0, keepdims=False)
    starts = jnp.cumsum(lengths) - lengths
    i = jnp.arange(ROWS, dtype=jnp.int32)
    places = lax.axis_index("dp") * ROWS + OWN * ((i // HOWN) % 8) + HOWN * (i // HROWS) + i % HOWN
    begins = jnp.max(jnp.where(starts[None, :] <= places[:, None], starts[None, :], 0), axis=1)
    inverse = jnp.exp(jnp.arange(HALF, dtype=F32) * (-2.0 * math.log(ROPE) / HD))
    angles = (places - begins).astype(F32)[:, None] * inverse[None, :]
    cosine, sine = jnp.cos(angles), jnp.sin(angles)
    rest = jnp.zeros((ROWS, 128 - HD), F32)
    cosine = jnp.concatenate([cosine, cosine, rest], axis=1)
    sine = jnp.concatenate([-sine, sine, rest], axis=1)
    begins = jnp.broadcast_to(begins[:, None], (ROWS, 128))
    y, dx, ga, gb, gn = step_call(
        inputs, cotangent, query_w[0].T, key_w[0].T, value_w[0].T, out_w[0], gate_w[0], up_w[0], down_w[0], gains, cosine, sine, begins
    )
    gate, up, down, out, query, key, value = widened(ga, gb)
    return (
        y[None], dx[None], gn[0:1], query.T[None], key.T[None], value.T[None], out[None], gn[1:2], gate[None], up[None], down[None],
    )


def solution(mesh):
    in_specs = (
        P(None, "dp", None),
        P(None, "dp", None),
        P(),
        P("section", None),
        P("section", None, "tensor"),
        P("section", None, "tensor"),
        P("section", None, "tensor"),
        P("section", "tensor", None),
        P("section", None),
        P("section", None, "tensor"),
        P("section", None, "tensor"),
        P("section", "tensor", None),
    )
    out_specs = (
        P("section", None, ("dp", "tensor"), None),
        P("section", None, ("dp", "tensor"), None),
        P("section", None),
        P("section", None, "tensor"),
        P("section", None, "tensor"),
        P("section", None, "tensor"),
        P("section", "tensor", None),
        P("section", None),
        P("section", None, "tensor"),
        P("section", None, "tensor"),
        P("section", "tensor", None),
    )
    return jax.shard_map(on_device, mesh=mesh, in_specs=in_specs, out_specs=out_specs, check_vma=False)
```

```python
import math

import jax
import jax.numpy as jnp
import numpy as np
from jax import lax
from jax.experimental import pallas as pl
from jax.experimental.pallas import tpu as pltpu
from jax.sharding import PartitionSpec as P

MESH = pl.DeviceIdType.MESH
F32 = jnp.float32
BF16 = jnp.bfloat16

HD = 96
HALF = HD // 2
D = 1536
FF = 512
ROWS = 256
OWN = 32
HROWS = 128
HOWN = 16
SCALE = 1.0 / math.sqrt(HD)
EPS = 1e-05
ROPE = 100000.0
MASKED = -1e30


def dot(a, b):
    return lax.dot_general(a, b, (((1,), (0,)), ((), ())), preferred_element_type=F32)


def dot_nt(a, b):
    return lax.dot_general(a, b, (((1,), (1,)), ((), ())), preferred_element_type=F32)


def dot_tn(a, b):
    return lax.dot_general(a, b, (((0,), (0,)), ((), ())), preferred_element_type=F32)


def lanes_of(v):
    return lax.broadcasted_iota(jnp.int32, v.shape, 1)


def swapped(v):
    return jnp.where(lanes_of(v) < HALF, pltpu.roll(v, 128 - HALF, 1), pltpu.roll(v, HALF, 1))


def place_of(i):
    return OWN * ((i // HOWN) % 8) + HOWN * (i // HROWS) + i % HOWN


def factor_of(v):
    return lax.rsqrt(jnp.mean(v * v, axis=-1, keepdims=True) + EPS)


def kernel(
    x_hbm, ct_hbm, wq_hbm, wk_hbm, wv_hbm, wo_hbm, wg_hbm, wu_hbm, wd_hbm, one_ref, two_ref, lengths_ref, speed_ref,
    y_out, dx_out, ga_out, gb_out, gn_out,
    wqkv, wo, wgu, wd, gains, gains_own, gains_in, cos_ref, sin_ref, beg_ref, df,
    n1, n2, q2, q2t, kv, o_f, o_b, stat_m, stat_l, gate_s, up_s, u_s, x_own, h_own,
    rsrc, land, da, do2, do2t, dgu, dq, dqkv, dkv_t, dkv_src, dkv_land, acc, s_m,
    ga, gb, da_in, db_in, za, zb, xa, xb, fa, fb, yb, dxb, dgain, dg_peer, dg_t, dg_d,
    w_l, w_s, w_r, ag_s, ag_r, rs_s, rs_r, kv_s, kv_r, dkv_s, dkv_r, out_l, out_s, out_r,
    ds_s, ds_r, z_s, z_r, x_s, x_r, a_s, a_r, a_l, f_s, f_r, ns, nr,
):
    sec = lax.axis_index("section")
    t = lax.axis_index("tensor")
    d = lax.axis_index("dp")
    other = 1 - sec
    z, xh = d // 2, d % 2

    barrier = pltpu.get_barrier_semaphore()

    def greet(axis, me, k, _):
        pl.semaphore_signal(barrier, inc=1, device_id={axis: (me + k) % 8}, device_id_type=MESH)
        return _

    pl.semaphore_signal(barrier, inc=1, device_id={"section": other}, device_id_type=MESH)
    lax.fori_loop(1, 8, lambda k, c: greet("tensor", t, k, c), 0)
    lax.fori_loop(1, 8, lambda k, c: greet("dp", d, k, c), 0)

    def load_rows(source, sem):
        def body(i, c):
            h, p = i // 8, i % 8
            pltpu.make_async_copy(
                source.at[sec, pl.ds(pl.multiple_of(p * OWN + h * HOWN, HOWN), HOWN)],
                df.at[pl.ds(pl.multiple_of(h * HROWS + p * HOWN, HOWN), HOWN)], sem,
            ).start()
            return c

        lax.fori_loop(0, 16, body, 0)

    def rows_loaded(source, sem):
        pltpu.make_async_copy(source.at[sec], df, sem).wait()

    own_parts = [
        (wq_hbm, lambda i: wqkv.at[i, pl.ds(0, 2 * HD)]),
        (wk_hbm, lambda i: wqkv.at[i, pl.ds(2 * HD, HD)]),
        (wv_hbm, lambda i: wqkv.at[i, pl.ds(3 * HD, HD)]),
        (wo_hbm, lambda i: wo.at[i]),
        (wg_hbm, lambda i: wgu.at[i, :, 0:FF]),
        (wu_hbm, lambda i: wgu.at[i, :, FF : 2 * FF]),
        (wd_hbm, lambda i: wd.at[i]),
    ]
    n_parts = len(own_parts)
    own_copies = [pltpu.make_async_copy(a, b(sec), w_l.at[i]) for i, (a, b) in enumerate(own_parts)]
    load_rows(x_hbm, w_l.at[8])
    for i in range(n_parts):
        own_copies[i].start()
    gains_own[0:8, :] = jnp.broadcast_to(one_ref[...].astype(F32), (8, D))
    gains_own[8:16, :] = jnp.broadcast_to(two_ref[...].astype(F32), (8, D))
    gains[sec] = gains_own[...]

    places = place_of(lax.broadcasted_iota(jnp.int32, (ROWS, 128), 0)) + d * ROWS

    lengths = jnp.where(sec == 0, lengths_ref[0:1, :], lengths_ref[1:2, :])
    start, begins = jnp.zeros((1, 1), jnp.int32), jnp.zeros((ROWS, 128), jnp.int32)
    for n in range(lengths.shape[1]):
        begins = jnp.maximum(begins, jnp.where(start <= places, start, 0))
        start = start + lengths[:, n : n + 1]
    beg_ref[...] = begins
    angles = (places - begins).astype(F32) * speed_ref[0:1, :]
    lane = lanes_of(angles)
    cos_ref[...] = jnp.where(lane < HD, jnp.cos(angles), 0.0)
    sine = jnp.sin(angles)
    sin_ref[...] = jnp.where(lane < HALF, -sine, jnp.where(lane < HD, sine, 0.0))
    pl.semaphore_wait(barrier, 15)
    sent_parts = [
        pltpu.make_async_remote_copy(
            src_ref=a, dst_ref=b(sec), send_sem=w_s.at[i], recv_sem=w_r.at[i],
            device_id={"section": other}, device_id_type=MESH,
        )
        for i, (a, b) in enumerate(own_parts)
    ]
    gains_sent = pltpu.make_async_remote_copy(
        src_ref=gains_own, dst_ref=gains_in, send_sem=w_s.at[n_parts], recv_sem=w_r.at[n_parts],
        device_id={"section": other}, device_id_type=MESH,
    )
    gains_sent.start()
    for i in range(n_parts):
        sent_parts[i].start()

    def gains_arrived():
        pltpu.make_async_remote_copy(
            src_ref=gains_own, dst_ref=gains_in, send_sem=w_s.at[n_parts], recv_sem=w_r.at[n_parts],
            device_id={"section": other}, device_id_type=MESH,
        ).wait_recv()
        gains[other] = gains_in[...]

    def weight_ready(layer, *which):
        @pl.when(layer == sec)
        def _():
            for i in which:
                own_copies[i].wait()

        @pl.when(layer != sec)
        def _():
            for i in which:
                a, b = own_parts[i]
                pltpu.make_async_remote_copy(
                    src_ref=a, dst_ref=b(other), send_sem=w_s.at[i], recv_sem=w_r.at[i],
                    device_id={"section": other}, device_id_type=MESH,
                ).wait_recv()

    def half_rows(half):
        return pl.ds(pl.multiple_of(half * HROWS, HROWS), HROWS)

    def pair_rows(half):
        return pl.ds(pl.multiple_of(half * ROWS, ROWS), ROWS)

    def rows_of(half, owner):
        return pl.ds(pl.multiple_of(half * HROWS + owner * HOWN, HOWN), HOWN)

    def kept(half):
        return pl.ds(pl.multiple_of(half * HOWN, HOWN), HOWN)

    def over_peers(body):
        def step(k, c):
            body((t + k) % 8)
            return c

        lax.fori_loop(1, 8, step, 0)

    def ag_copy(buf, i, half, to, owner):
        rows = rows_of(half, owner)
        return pltpu.make_async_remote_copy(
            src_ref=buf.at[rows], dst_ref=buf.at[rows], send_sem=ag_s.at[i, half, to], recv_sem=ag_r.at[i, half, owner],
            device_id={"tensor": to}, device_id_type=MESH,
        )

    def ag_start(buf, i, half):
        over_peers(lambda p: ag_copy(buf, i, half, p, t).start())

    def ag_wait(buf, i, half):
        over_peers(lambda p: ag_copy(buf, i, half, t, p).wait_recv())

    def ag_sent(buf, i, half):
        over_peers(lambda p: ag_copy(buf, i, half, p, t).wait_send())

    def rs_copy(i, half, to, sender):
        return pltpu.make_async_remote_copy(
            src_ref=rsrc.at[i, rows_of(half, to)], dst_ref=land.at[i, half, sender], send_sem=rs_s.at[i, half, to],
            recv_sem=rs_r.at[i, half, sender], device_id={"tensor": to}, device_id_type=MESH,
        )

    def rs_start(i, half):
        over_peers(lambda p: rs_copy(i, half, p, t).start())

    def rs_sum(i, half):
        def body(k, total):
            p = (t + k) % 8
            rs_copy(i, half, t, p).wait_recv()
            return total + land[i, half, p].astype(F32)

        return lax.fori_loop(1, 8, body, rsrc[i, rows_of(half, t), :].astype(F32))

    def rs_sent(i, half):
        over_peers(lambda p: rs_copy(i, half, p, t).wait_send())

    def both(body):
        def step(half, c):
            body(half)
            return c

        lax.fori_loop(0, 2, step, 0)

    def allowed_of(j, half):
        rows = place_of(lax.broadcasted_iota(jnp.int32, (HROWS, 1), 0) + half * HROWS) + d * ROWS
        cols = place_of(lax.broadcasted_iota(jnp.int32, (1, ROWS), 1)) + j * ROWS
        allowed = (cols <= rows) & (cols >= beg_ref[half_rows(half), 0:1])
        return jnp.concatenate([jnp.where(allowed, 0.0, MASKED)] * 2, axis=0)

    pl.when(sec == 1)(gains_arrived)
    rows_loaded(x_hbm, w_l.at[8])

    def first_norm(i, c):
        rows = pl.ds(pl.multiple_of(i * OWN, OWN), OWN)
        v = df[rows, :].astype(F32)
        n1[0, rows, :] = (v * factor_of(v) * gains[0, 0:1, :]).astype(BF16)
        return c

    lax.fori_loop(0, ROWS // OWN, first_norm, 0)
    for half in range(2):
        x_own[0, kept(half), :] = df[rows_of(half, t), :].astype(F32)
    load_rows(ct_hbm, w_l.at[9])

    def forward_layer(layer, c):
        weight_ready(layer, 0, 1, 2)

        def kv_copy(owner, to, half):
            part = kv.at[layer, owner, :, half_rows(half)]
            return pltpu.make_async_remote_copy(
                src_ref=part, dst_ref=part, send_sem=kv_s.at[to, half], recv_sem=kv_r.at[owner, layer, half],
                device_id={"dp": to}, device_id_type=MESH,
            )

        def project(half):
            rows = half_rows(half)

            @pl.when(layer == 1)
            def _():
                ag_wait(n1.at[1], 0, half)

            raw = dot_nt(n1[layer, rows, :], wqkv[layer])
            c0, c1, c2 = raw[:, 0:128], raw[:, 128:256], raw[:, 256:384]
            lane = lanes_of(c0)
            q1 = jnp.where(lane < 32, pltpu.roll(c0, 32, 1), pltpu.roll(c1, 32, 1))
            k0 = jnp.where(lane < 64, pltpu.roll(c1, 64, 1), pltpu.roll(c2, 64, 1))
            v0 = pltpu.roll(c2, 96, 1)
            cosine, sine = cos_ref[rows, :], sin_ref[rows, :]
            turned = k0 * cosine + swapped(k0) * sine
            kv[layer, d, pl.ds(0, HD), rows] = jnp.transpose(turned)[0:HD, :].astype(BF16)
            kv[layer, d, pl.ds(HD, HD), rows] = jnp.transpose(v0)[0:HD, :].astype(BF16)

            def kv_send(k, c):
                kv_copy(d, k, half).start()
                return c

            lax.fori_loop(d + 1, 8, kv_send, 0)
            for h, part in ((0, c0), (1, q1)):
                turned = part * cosine + swapped(part) * sine
                place = pl.ds(pl.multiple_of(half * ROWS + h * HROWS, HROWS), HROWS)
                q2[layer, place, :] = turned[:, 0:HD].astype(BF16)
                q2t[layer, :, place] = jnp.transpose(turned)[0:HD, :].astype(BF16)

        both(project)

        @pl.when(layer == 1)
        def _():
            both(lambda half: ag_sent(n1.at[1], 0, half))

        weight_ready(layer, 3)

        def attend_half(half):
            rows = pair_rows(half)
            s_m[rows, :] = jnp.full((ROWS, 1), MASKED, F32)
            stat_l[layer, rows, :] = jnp.zeros((ROWS, 1), F32)
            acc[rows, :] = jnp.zeros((ROWS, HD), F32)

            def attend(i, c):
                j = d - i

                @pl.when((i > 0) & (half == 0))
                def _():
                    kv_copy(j, d, 0).wait_recv()
                    kv_copy(j, d, 1).wait_recv()

                s = dot(q2[layer, rows, :], kv[layer, j, pl.ds(0, HD), :]) * SCALE + allowed_of(j, half)
                old = s_m[rows, :]
                new = jnp.maximum(old, jnp.max(s, axis=-1, keepdims=True))
                p = jnp.exp(s - new)
                shrink = jnp.exp(old - new)
                s_m[rows, :] = new
                stat_l[layer, rows, :] = stat_l[layer, rows, :] * shrink + jnp.sum(p, axis=-1, keepdims=True)
                acc[rows, :] = acc[rows, :] * shrink + dot_nt(p.astype(BF16), kv[layer, j, pl.ds(HD, HD), :])
                return c

            lax.fori_loop(0, d + 1, attend, 0)
            total = stat_l[layer, rows, :]
            mixed = acc[rows, :] / total
            o_f[layer, rows, :] = mixed
            o_b[layer, rows, :] = mixed.astype(BF16)
            stat_m[layer, rows, :] = s_m[rows, :] + jnp.log(total)
            first = pl.ds(pl.multiple_of(half * ROWS, HROWS), HROWS)
            second = pl.ds(pl.multiple_of(half * ROWS + HROWS, HROWS), HROWS)

            def out_part(n, c):
                cols = pl.ds(pl.multiple_of(n * 512, 512), 512)
                part = dot(o_b[layer, first, :], wo[layer, pl.ds(0, HD), cols])
                part += dot(o_b[layer, second, :], wo[layer, pl.ds(HD, HD), cols])
                rsrc[0, half_rows(half), cols] = part.astype(BF16)
                return c

            lax.fori_loop(0, 3, out_part, 0)
            rs_start(0, half)

        both(attend_half)

        def kv_sent(k, c):
            kv_copy(d, k, 0).wait_send()
            kv_copy(d, k, 1).wait_send()
            return c

        lax.fori_loop(d + 1, 8, kv_sent, 0)

        def middle(half):
            v = x_own[layer, kept(half), :] + rs_sum(0, half)
            h_own[layer, kept(half), :] = v
            n2[layer, rows_of(half, t), :] = (v * factor_of(v) * gains[layer, 8:9, :]).astype(BF16)
            ag_start(n2.at[layer], 1, half)
            rs_sent(0, half)

        both(middle)
        weight_ready(layer, 4, 5)
        weight_ready(layer, 6)

        def feed(half):
            rows = half_rows(half)
            ag_wait(n2.at[layer], 1, half)

            def units(n, c):
                cols = pl.ds(pl.multiple_of(n * 256, 256), 256)
                above = pl.ds(pl.multiple_of(n * 256 + FF, 256), 256)
                g = dot(n2[layer, rows, :], wgu[layer, :, cols])
                up = dot(n2[layer, rows, :], wgu[layer, :, above])
                gate_s[layer, rows, cols] = g
                up_s[layer, rows, cols] = up
                u_s[layer, rows, cols] = (g * jax.nn.sigmoid(g) * up).astype(BF16)
                return c

            lax.fori_loop(0, 2, units, 0)

            def down_part(n, c):
                cols = pl.ds(pl.multiple_of(n * 512, 512), 512)
                rsrc[1, rows, cols] = dot(u_s[layer, rows, :], wd[layer, :, cols]).astype(BF16)
                return c

            lax.fori_loop(0, 3, down_part, 0)
            rs_start(1, half)
            ag_sent(n2.at[layer], 1, half)

        both(feed)

        pl.when((layer == 0) & (sec == 0))(gains_arrived)

        def result(half):
            y = (h_own[layer, kept(half), :] + rs_sum(1, half)).astype(BF16)
            yb[layer, kept(half), :] = y

            @pl.when(layer == 0)
            def _():
                v = y.astype(F32)
                x_own[1, kept(half), :] = v
                n1[1, rows_of(half, t), :] = (v * factor_of(v) * gains[1, 0:1, :]).astype(BF16)
                ag_start(n1.at[1], 0, half)

            rs_sent(1, half)

        both(result)
        row_out(layer, yb, y_out, 0)
        return c

    def row_out(layer, buf, out, i):
        @pl.when(layer == sec)
        def _():
            pltpu.make_async_copy(buf.at[layer], out.at[sec], out_l.at[i]).start()

        @pl.when(layer != sec)
        def _():
            pltpu.make_async_remote_copy(
                src_ref=buf.at[layer], dst_ref=out.at[sec], send_sem=out_s.at[i], recv_sem=out_r.at[i],
                device_id={"section": other}, device_id_type=MESH,
            ).start()

    def row_out_wait(buf, out, i):
        pltpu.make_async_copy(buf.at[sec], out.at[sec], out_l.at[i]).wait()
        copy = pltpu.make_async_remote_copy(
            src_ref=buf.at[other], dst_ref=out.at[other], send_sem=out_s.at[i], recv_sem=out_r.at[i],
            device_id={"section": other}, device_id_type=MESH,
        )
        copy.wait_send()
        copy.wait_recv()

    lax.fori_loop(0, 2, forward_layer, 0)

    rows_loaded(ct_hbm, w_l.at[9])

    sets = ((ga, da_in, za, xa, fa, ga_out), (gb, db_in, zb, xb, fb, gb_out))
    before, after = (z + 3) % 4, (z + 1) % 4
    far = (z + 2) % 4

    def dp_at(zz, xx):
        return zz * 2 + xx

    def quarter(i, which):
        size = (288, 144)[i]
        return pl.ds(pl.multiple_of(which * size, 16), size)

    def swap_cores(layer, i):
        return pltpu.make_async_remote_copy(
            src_ref=sets[i][0].at[layer, other], dst_ref=sets[i][1].at[layer], send_sem=ds_s.at[i, layer],
            recv_sem=ds_r.at[i, layer], device_id={"section": other}, device_id_type=MESH,
        )

    def add_rows(target, index, first, size, sources):
        count = 96 if size % 96 == 0 else 48

        def add(n, carry):
            here = pl.ds(pl.multiple_of(first + n * count, 16), count)
            total = target[(*index, here)].astype(F32)
            for ref, place, start in sources:
                total += ref[(*place, pl.ds(pl.multiple_of(start + n * count, 16), count))].astype(F32)
            target[(*index, here)] = total.astype(BF16)
            return carry

        lax.fori_loop(0, size // count, add, 0)

    def z_piece(layer, i, piece, chunk, which, to):
        return pltpu.make_async_remote_copy(
            src_ref=sets[i][0].at[layer, sec, chunk, quarter(i, which)], dst_ref=sets[i][2].at[layer, piece],
            send_sem=z_s.at[i, layer, piece], recv_sem=z_r.at[i, layer, piece], device_id={"dp": dp_at(to, xh)},
            device_id_type=MESH,
        )

    def sum_1(layer, i):
        g, arrived = sets[i][0:2]
        swap_cores(layer, i).wait_recv()
        for chunk, sends in (
            (far, ((0, 0, after), (1, 1, before))),
            (after, ((2, 1, after),)),
            (before, ((3, 0, before),)),
            (z, ()),
        ):
            add_rows(g, (layer, sec, chunk), 0, g.shape[3], [(arrived, (layer, chunk), 0)])
            for piece, which, to in sends:
                z_piece(layer, i, piece, chunk, which, to).start()

    def sum_2(layer, i):
        g, landed = sets[i][0], sets[i][2]
        size = landed.shape[2]
        z_piece(layer, i, 0, far, 0, after).wait_recv()
        add_rows(g, (layer, sec, after), 0, size, [(landed, (layer, 0), 0)])
        z_piece(layer, i, 4, after, 0, after).start()
        z_piece(layer, i, 1, far, 1, before).wait_recv()
        add_rows(g, (layer, sec, before), size, size, [(landed, (layer, 1), 0)])
        z_piece(layer, i, 5, before, 1, before).start()

    def x_over(layer, i):
        return pltpu.make_async_remote_copy(
            src_ref=sets[i][0].at[layer, sec, z, quarter(i, 1 - xh)], dst_ref=sets[i][3].at[layer],
            send_sem=x_s.at[i, 0, layer], recv_sem=x_r.at[i, 0, layer], device_id={"dp": dp_at(z, 1 - xh)},
            device_id_type=MESH,
        )

    def x_back(layer, i, which):
        part = sets[i][4].at[layer, quarter(i, which)]
        return pltpu.make_async_remote_copy(
            src_ref=part, dst_ref=part, send_sem=x_s.at[i, 1, layer], recv_sem=x_r.at[i, 1, layer],
            device_id={"dp": dp_at(z, 1 - xh)}, device_id_type=MESH,
        )

    def sum_3(layer, i):
        g, landed = sets[i][0], sets[i][2]
        size = landed.shape[2]
        for piece in (2, 3, 4, 5):
            z_piece(layer, i, piece, z, 0, after).wait_recv()
        add_rows(g, (layer, sec, z), 0, size, [(landed, (layer, 3), 0), (landed, (layer, 4), 0)])
        add_rows(g, (layer, sec, z), size, size, [(landed, (layer, 2), 0), (landed, (layer, 5), 0)])
        x_over(layer, i).start()

    def spread(layer, i, half, chunk, which, to, k):
        rows = quarter(i, which)
        return pltpu.make_async_remote_copy(
            src_ref=sets[i][4].at[layer, rows], dst_ref=sets[i][5].at[half, chunk, rows], send_sem=a_s.at[i, layer, which, k],
            recv_sem=a_r.at[i, half, chunk, which], device_id={"section": layer, "dp": dp_at(to, xh)}, device_id_type=MESH,
        )

    def keep(layer, i, which):
        rows = quarter(i, which)
        return pltpu.make_async_copy(sets[i][4].at[layer, rows], sets[i][5].at[sec, z, rows], a_l.at[i, which])

    def spread_all(layer, i, which):
        spread(layer, i, sec, z, which, after, 0).start()
        spread(layer, i, sec, z, which, before, 1).start()

        @pl.when(layer == sec)
        def _():
            keep(layer, i, which).start()

        @pl.when(layer != sec)
        def _():
            spread(layer, i, sec, z, which, z, 2).start()

    def sum_4(layer, i):
        g, over, done = sets[i][0], sets[i][3], sets[i][4]
        size = over.shape[1]
        x_over(layer, i).wait_recv()

        def add(n, carry):
            here = pl.ds(pl.multiple_of(n * 48, 16), 48)
            there = pl.ds(pl.multiple_of(xh * size + n * 48, 16), 48)
            done[layer, there, :] = (g[layer, sec, z, there, :].astype(F32) + over[layer, here, :].astype(F32)).astype(BF16)
            return carry

        lax.fori_loop(0, size // 48, add, 0)
        x_back(layer, i, xh).start()
        spread_all(layer, i, xh)

    def sum_5(layer, i):
        x_back(layer, i, 1 - xh).wait_recv()
        spread_all(layer, i, 1 - xh)

    def pass_on(i, half, chunk, which, to):
        part = sets[i][5].at[half, chunk, quarter(i, which)]
        return pltpu.make_async_remote_copy(
            src_ref=part, dst_ref=part, send_sem=f_s.at[i, half, which], recv_sem=f_r.at[i, half, which],
            device_id={"dp": dp_at(to, xh)}, device_id_type=MESH,
        )

    def sum_6(i):
        for half in range(2):
            spread(sec, i, half, before, 0, z, 0).wait_recv()
            pass_on(i, half, before, 0, after).start()
            spread(sec, i, half, after, 1, z, 0).wait_recv()
            pass_on(i, half, after, 1, before).start()

    def sum_7(i):
        for which in range(2):
            keep(sec, i, which).wait()
            spread(sec, i, other, z, which, z, 2).wait_recv()
            spread(other, i, sec, z, which, z, 2).wait_send()
            for half in range(2):
                spread(sec, i, half, (after, before)[which], which, z, 0).wait_recv()
                pass_on(i, half, far, which, z).wait_recv()
                pass_on(i, half, z, which, after).wait_send()
        for layer in range(2):
            swap_cores(layer, i).wait_send()
            for piece in range(6):
                z_piece(layer, i, piece, z, 0, after).wait_send()
            x_over(layer, i).wait_send()
            x_back(layer, i, xh).wait_send()
            for which in range(2):
                spread(layer, i, sec, z, which, after, 0).wait_send()
                spread(layer, i, sec, z, which, before, 1).wait_send()

    def backward_layer(step, c):
        layer = 1 - step

        @pl.when(step == 1)
        def _():
            sum_1(1, 1)
            sum_4(1, 0)

        def feed_back(half):
            rows = half_rows(half)

            @pl.when(step == 1)
            def _():
                ag_wait(df, 2, half)

            dxb[layer, kept(half), :] = df[rows_of(half, t), :].astype(F32)

            def unit_grads(n, c):
                cols = pl.ds(pl.multiple_of(n * 256, 256), 256)
                above = pl.ds(pl.multiple_of(n * 256 + FF, 256), 256)
                du = dot_nt(df[rows, :], wd[layer, cols, :])
                g, up = gate_s[layer, rows, cols], up_s[layer, rows, cols]
                sig = jax.nn.sigmoid(g)
                dgu[rows, cols] = (du * up * sig * (1.0 + g * (1.0 - sig))).astype(BF16)
                dgu[rows, above] = (du * g * sig).astype(BF16)
                return c

            lax.fori_loop(0, 2, unit_grads, 0)

            def normed_part(n, c):
                cols = pl.ds(pl.multiple_of(n * 256, 256), 256)
                rsrc[0, rows, cols] = dot_nt(dgu[rows, :], wgu[layer, cols, :]).astype(BF16)
                return c

            lax.fori_loop(0, 6, normed_part, 0)
            rs_start(0, half)

        both(feed_back)

        @pl.when(step == 1)
        def _():
            both(lambda half: ag_sent(df, 2, half))

        def unit_weights(n, c):
            cols = pl.ds(pl.multiple_of(n * 384, 384), 384)
            got = dot_tn(n2[layer, :, cols], dgu[...]).astype(BF16)
            for h in range(2):
                ga[layer, h, n, pl.ds(0, 192), :] = got[192 * h : 192 * h + 192, 0:FF]
                ga[layer, h, n, pl.ds(192, 192), :] = got[192 * h : 192 * h + 192, FF : 2 * FF]
            cols = pl.ds(pl.multiple_of(n * 128, 128), 128)
            got = dot_tn(u_s[layer, :, cols], df[...]).astype(BF16)
            for h in range(2):
                for i in range(3):
                    ga[layer, h, n, pl.ds(384 + 64 * i, 64), :] = got[64 * h : 64 * h + 64, 512 * i : 512 * i + 512]
            return c

        lax.fori_loop(0, 4, unit_weights, 0)
        swap_cores(layer, 0).start()

        @pl.when(step == 1)
        def _():
            sum_5(1, 0)
            sum_2(1, 1)

        def hidden_grads(half):
            dn = rs_sum(0, half)
            h = h_own[layer, kept(half), :]
            r = factor_of(h)
            tt = dn * gains[layer, 8:9, :]
            dh = dxb[layer, kept(half), :] + r * tt - h * (r * r * r * jnp.mean(h * tt, axis=-1, keepdims=True))
            dgain[layer, 1:2, :] += jnp.sum(dn * h * r, axis=0, keepdims=True)
            dxb[layer, kept(half), :] = dh
            da[rows_of(half, t), :] = dh.astype(BF16)
            ag_start(da, 3, half)
            rs_sent(0, half)

        both(hidden_grads)
        sum_1(layer, 0)

        @pl.when(step == 1)
        def _():
            sum_3(1, 1)

        def mixed_grads(half):
            ag_wait(da, 3, half)
            for h in range(2):
                place = pl.ds(pl.multiple_of(half * ROWS + h * HROWS, HROWS), HROWS)
                got = dot_nt(da[half_rows(half), :], wo[layer, pl.ds(h * HD, HD), :])
                do2[place, :] = got.astype(BF16)
                padded = jnp.concatenate([got, jnp.zeros((HROWS, 128 - HD), F32)], axis=1)
                do2t[:, place] = jnp.transpose(padded)[0:HD, :].astype(BF16)

        both(mixed_grads)
        both(lambda half: ag_sent(da, 3, half))
        dot_rows = jnp.sum(do2[...].astype(F32) * o_f[layer], axis=-1, keepdims=True)
        s_m[...] = dot_rows
        acc[...] = jnp.zeros(acc.shape, F32)

        def dkv_copy(to, sender):
            return pltpu.make_async_remote_copy(
                src_ref=dkv_src.at[to], dst_ref=dkv_land.at[layer, sender], send_sem=dkv_s.at[to], recv_sem=dkv_r.at[layer, sender],
                device_id={"dp": to}, device_id_type=MESH,
            )

        def attend_back(j, c):
            dkt = jnp.zeros((HD, ROWS), F32)
            dvt = jnp.zeros((HD, ROWS), F32)
            for half in range(2):
                rows = pair_rows(half)
                kt = kv[layer, j, pl.ds(0, HD), :]
                s = dot(q2[layer, rows, :], kt) * SCALE + allowed_of(j, half)
                p = jnp.exp(s - stat_m[layer, rows, :])
                dp = dot(do2[rows, :], kv[layer, j, pl.ds(HD, HD), :])
                ds = (p * (dp - s_m[rows, :])).astype(BF16)
                acc[rows, :] += dot_nt(ds, kt)
                dkt += dot(q2t[layer, :, rows], ds)
                dvt += dot(do2t[:, rows], p.astype(BF16))
            dkv_src[j, pl.ds(0, HD), :] = (dkt * SCALE).astype(BF16)
            dkv_src[j, pl.ds(HD, HD), :] = dvt.astype(BF16)

            @pl.when(j < d)
            def _():
                dkv_copy(j, d).start()

            return c

        lax.fori_loop(0, d + 1, attend_back, 0)

        def dkv_sent(k, c):
            dkv_copy(k, d).wait_send()
            return c

        def out_weights(n, c):
            cols = pl.ds(pl.multiple_of(n * 384, 384), 384)
            for h in range(2):
                mixed = [o_b[layer, pl.ds(half * ROWS + h * HROWS, HROWS), :] for half in range(2)]
                got = dot_tn(jnp.concatenate(mixed, axis=0), da[:, cols])
                gb[layer, 0, n, pl.ds(h * HD, HD), :] = got.astype(BF16)
            return c

        lax.fori_loop(0, 4, out_weights, 0)
        lax.fori_loop(0, d, dkv_sent, 0)

        sum_2(layer, 0)

        @pl.when(step == 1)
        def _():
            sum_4(1, 1)

        def dkv_sum(k, total):
            dkv_copy(d, k).wait_recv()
            return total + dkv_land[layer, k].astype(F32)

        dkv_total = lax.fori_loop(d + 1, 8, dkv_sum, dkv_src[d].astype(F32))
        dkv_t[...] = jnp.zeros(dkv_t.shape, F32)
        dkv_t[0, pl.ds(0, HD), :] = dkv_total[0:HD]
        dkv_t[1, pl.ds(0, HD), :] = dkv_total[HD : 2 * HD]
        dk_rot = jnp.transpose(dkv_t[0])
        dv = jnp.transpose(dkv_t[1])
        cosine, sine = cos_ref[...], sin_ref[...]
        dq[...] = jnp.zeros(dq.shape, F32)
        dq[:, 0:HD] = acc[...] * SCALE
        dq0, dq1 = (
            jnp.concatenate([dq[pl.ds(half * ROWS + h * HROWS, HROWS), :] for half in range(2)], axis=0) for h in range(2)
        )
        dq0 = dq0 * cosine - swapped(dq0) * sine
        dq1 = dq1 * cosine - swapped(dq1) * sine
        dk = dk_rot * cosine - swapped(dk_rot) * sine
        lane = lanes_of(dk)
        dqkv[:, 0:128] = jnp.where(lane < HD, dq0, pltpu.roll(dq1, 96, 1)).astype(BF16)
        dqkv[:, 128:256] = jnp.where(lane < 64, pltpu.roll(dq1, 96, 1), pltpu.roll(dk, 64, 1)).astype(BF16)
        dqkv[:, 256:384] = jnp.where(lane < 32, pltpu.roll(dk, 64, 1), pltpu.roll(dv, 32, 1)).astype(BF16)

        def project_back(half):
            rows = half_rows(half)

            def input_part(n, c):
                cols = pl.ds(pl.multiple_of(n * 512, 512), 512)
                rsrc[1, rows, cols] = dot(dqkv[rows, :], wqkv[layer, :, cols]).astype(BF16)
                return c

            lax.fori_loop(0, 3, input_part, 0)
            rs_start(1, half)

        both(project_back)

        def qkv_weights(n, c):
            cols = pl.ds(pl.multiple_of(n * 384, 384), 384)
            got = dot_tn(dqkv[...], n1[layer, :, cols]).astype(BF16)
            gb[layer, 0, n, pl.ds(2 * HD, HD), :] = got[0:HD]
            gb[layer, 1, n] = got[HD : 4 * HD]
            return c

        lax.fori_loop(0, 4, qkv_weights, 0)
        swap_cores(layer, 1).start()
        sum_3(layer, 0)

        @pl.when(step == 1)
        def _():
            sum_5(1, 1)

            @pl.when(sec == 1)
            def _():
                sum_6(0)

        def input_grads(half):
            dn = rs_sum(1, half)
            v = x_own[layer, kept(half), :]
            r = factor_of(v)
            tt = dn * gains[layer, 0:1, :]
            dx = dxb[layer, kept(half), :] + r * tt - v * (r * r * r * jnp.mean(v * tt, axis=-1, keepdims=True))
            dgain[layer, 0:1, :] += jnp.sum(dn * v * r, axis=0, keepdims=True)
            dxb[layer, kept(half), :] = dx

            @pl.when(step == 0)
            def _():
                df[rows_of(half, t), :] = dx.astype(BF16)
                ag_start(df, 2, half)

            rs_sent(1, half)

        both(input_grads)
        row_out(layer, dxb, dx_out, 1)
        return c

    dgain[...] = jnp.zeros(dgain.shape, F32)
    lax.fori_loop(0, 2, backward_layer, 0)

    mate = pltpu.make_async_remote_copy(
        src_ref=dgain.at[other], dst_ref=dg_peer, send_sem=ns.at[0, 0], recv_sem=nr.at[0, 0],
        device_id={"section": other}, device_id_type=MESH,
    )
    mate.start()
    sum_4(0, 0)
    sum_1(0, 1)

    @pl.when(sec == 1)
    def _():
        sum_6(1)


    def gain_copy(axis, i, buf, me, to, sender):
        return pltpu.make_async_remote_copy(
            src_ref=buf.at[me], dst_ref=buf.at[sender], send_sem=ns.at[i, to], recv_sem=nr.at[i, sender],
            device_id={axis: to}, device_id_type=MESH,
        )

    def gain_send(axis, i, buf, me):
        def send(k, c):
            gain_copy(axis, i, buf, me, (me + k) % 8, me).start()
            return c

        lax.fori_loop(1, 8, send, 0)

    def gain_sum(axis, i, buf, me):
        def take(k, total):
            p = (me + k) % 8
            gain_copy(axis, i, buf, me, p, p).wait_recv()
            return total + buf[p]

        def sent(k, c):
            gain_copy(axis, i, buf, me, (me + k) % 8, me).wait_send()
            return c

        total = lax.fori_loop(1, 8, take, buf[me])
        lax.fori_loop(1, 8, sent, 0)
        return total

    mate.wait_recv()
    mate.wait_send()
    dg_t[t] = dgain[sec] + dg_peer[...]
    gain_send("tensor", 1, dg_t, t)
    sum_5(0, 0)
    sum_2(0, 1)
    dg_d[d] = gain_sum("tensor", 1, dg_t, t)
    gain_send("dp", 2, dg_d, d)
    sum_3(0, 1)

    @pl.when(sec == 0)
    def _():
        sum_6(0)

    sum_4(0, 1)
    sum_5(0, 1)

    @pl.when(sec == 0)
    def _():
        sum_6(1)

    gn_out[...] = gain_sum("dp", 2, dg_d, d)
    sum_7(0)
    sum_7(1)
    row_out_wait(yb, y_out, 0)
    row_out_wait(dxb, dx_out, 1)
    for i in range(n_parts):
        sent_parts[i].wait_send()
    gains_sent.wait_send()


def step_call(*args):
    hbm = pl.BlockSpec(memory_space=pl.ANY)
    vmem = pl.BlockSpec(memory_space=pltpu.VMEM)
    dma = pltpu.SemaphoreType.DMA
    scratch = [
        pltpu.VMEM((2, 384, D), BF16), pltpu.VMEM((2, 192, D), BF16), pltpu.VMEM((2, D, 2 * FF), BF16),
        pltpu.VMEM((2, FF, D), BF16), pltpu.VMEM((2, 16, D), F32), pltpu.VMEM((16, D), F32), pltpu.VMEM((16, D), F32), pltpu.VMEM((ROWS, 128), F32),
        pltpu.VMEM((ROWS, 128), F32), pltpu.VMEM((ROWS, 128), jnp.int32), pltpu.VMEM((ROWS, D), BF16),
        pltpu.VMEM((2, ROWS, D), BF16), pltpu.VMEM((2, ROWS, D), BF16), pltpu.VMEM((2, 2 * ROWS, HD), BF16),
        pltpu.VMEM((2, HD, 2 * ROWS), BF16), pltpu.VMEM((2, 8, 2 * HD, ROWS), BF16), pltpu.VMEM((2, 2 * ROWS, HD), F32),
        pltpu.VMEM((2, 2 * ROWS, HD), BF16), pltpu.VMEM((2, 2 * ROWS, 1), F32), pltpu.VMEM((2, 2 * ROWS, 1), F32),
        pltpu.VMEM((2, ROWS, FF), F32), pltpu.VMEM((2, ROWS, FF), F32), pltpu.VMEM((2, ROWS, FF), BF16),
        pltpu.VMEM((2, OWN, D), F32), pltpu.VMEM((2, OWN, D), F32),
        pltpu.VMEM((2, ROWS, D), BF16), pltpu.VMEM((2, 2, 8, HOWN, D), BF16), pltpu.VMEM((ROWS, D), BF16),
        pltpu.VMEM((2 * ROWS, HD), BF16), pltpu.VMEM((HD, 2 * ROWS), BF16), pltpu.VMEM((ROWS, 2 * FF), BF16),
        pltpu.VMEM((2 * ROWS, 128), F32), pltpu.VMEM((ROWS, 384), BF16), pltpu.VMEM((2, 128, ROWS), F32),
        pltpu.VMEM((8, 2 * HD, ROWS), BF16), pltpu.VMEM((2, 8, 2 * HD, ROWS), BF16), pltpu.VMEM((2 * ROWS, HD), F32),
        pltpu.VMEM((2 * ROWS, 1), F32),
        pltpu.VMEM((2, 2, 4, 576, 512), BF16), pltpu.VMEM((2, 2, 4, 288, 384), BF16), pltpu.VMEM((2, 4, 576, 512), BF16),
        pltpu.VMEM((2, 4, 288, 384), BF16), pltpu.VMEM((2, 6, 288, 512), BF16), pltpu.VMEM((2, 6, 144, 384), BF16),
        pltpu.VMEM((2, 288, 512), BF16), pltpu.VMEM((2, 144, 384), BF16), pltpu.VMEM((2, 576, 512), BF16),
        pltpu.VMEM((2, 288, 384), BF16),
        pltpu.VMEM((2, OWN, D), BF16), pltpu.VMEM((2, OWN, D), F32), pltpu.VMEM((2, 8, D), F32), pltpu.VMEM((8, D), F32),
        pltpu.VMEM((8, 8, D), F32), pltpu.VMEM((8, 8, D), F32),
        dma((10,)), dma((8,)), dma((8,)), dma((4, 2, 8)), dma((4, 2, 8)), dma((2, 2, 8)), dma((2, 2, 8)), dma((8, 2)), dma((8, 2, 2)),
        dma((8,)), dma((2, 8)), dma((2,)), dma((2,)), dma((2,)),
        dma((2, 2)), dma((2, 2)), dma((2, 2, 6)), dma((2, 2, 6)), dma((2, 2, 2)), dma((2, 2, 2)), dma((2, 2, 2, 3)),
        dma((2, 2, 4, 2)), dma((2, 2)), dma((2, 2, 2)), dma((2, 2, 2)), dma((3, 8)), dma((3, 8)),
    ]
    return pl.pallas_call(
        kernel,
        out_shape=(
            jax.ShapeDtypeStruct((2, OWN, D), BF16),
            jax.ShapeDtypeStruct((2, OWN, D), F32),
            jax.ShapeDtypeStruct((2, 4, 576, 512), BF16),
            jax.ShapeDtypeStruct((2, 4, 288, 384), BF16),
            jax.ShapeDtypeStruct((8, D), F32),
        ),
        in_specs=[hbm] * 9 + [vmem] * 4,
        out_specs=(hbm, hbm, hbm, hbm, vmem),
        scratch_shapes=scratch,
        compiler_params=pltpu.CompilerParams(
            collective_id=0, has_side_effects=True, vmem_limit_bytes=64 * 1024 * 1024 - 65536
        ),
        name="train_step",
    )(*args)


def widen(
    ga_hbm, gb_hbm, gn_ref, y_ref, dx_ref,
    gate_hbm, up_hbm, down_hbm, out_hbm, query_hbm, key_hbm, value_hbm, one_ref, two_ref, y_out, dx_out,
    ga, gb, gate, up, down, out, query, key, value, a_in, b_in, sent,
):
    parts = [(h, c) for c in range(4) for h in range(2)]
    a_copies = [pltpu.make_async_copy(ga_hbm.at[h, c], ga.at[h, c], a_in.at[h, c]) for h, c in parts]
    b_copies = [pltpu.make_async_copy(gb_hbm.at[:, c], gb.at[:, c], b_in.at[c]) for c in range(4)]
    for copy in b_copies + a_copies:
        copy.start()
    one_ref[...] = gn_ref[0:1, :]
    two_ref[...] = gn_ref[1:2, :]
    y_out[0] = y_ref[...]
    dx_out[0] = dx_ref[...]
    for c in range(4):
        b_copies[c].wait()
        cols = pl.ds(384 * c, 384)
        out[:, cols] = gb[0, c, 0:192, :].astype(F32)
        query[0:HD, cols] = gb[0, c, 192:288, :].astype(F32)
        query[HD : 2 * HD, cols] = gb[1, c, 0:HD, :].astype(F32)
        key[:, cols] = gb[1, c, HD : 2 * HD, :].astype(F32)
        value[:, cols] = gb[1, c, 2 * HD : 3 * HD, :].astype(F32)
    leaving = [
        pltpu.make_async_copy(buf, to, sent.at[i])
        for i, (buf, to) in enumerate(((out, out_hbm), (query, query_hbm), (key, key_hbm), (value, value_hbm)))
    ]
    for copy in leaving:
        copy.start()
    for i, (h, c) in enumerate(parts):
        a_copies[i].wait()
        rows, few = pl.ds(384 * c + 192 * h, 192), pl.ds(128 * c + 64 * h, 64)
        gate[rows, :] = ga[h, c, 0:192, :].astype(F32)
        up[rows, :] = ga[h, c, 192:384, :].astype(F32)
        for k in range(3):
            down[few, pl.ds(512 * k, 512)] = ga[h, c, 384 + 64 * k : 448 + 64 * k, :].astype(F32)
        for k, (buf, to, which) in enumerate(((gate, gate_hbm, rows), (up, up_hbm, rows), (down, down_hbm, few))):
            copy = pltpu.make_async_copy(buf.at[which], to.at[which], sent.at[4 + 3 * i + k])
            copy.start()
            leaving.append(copy)
    for copy in leaving:
        copy.wait()


def widened(ga, gb, gn, y, dx):
    grads = [(D, FF), (D, FF), (FF, D), (192, D), (192, D), (HD, D), (HD, D)]
    shapes = [jax.ShapeDtypeStruct(shape, F32) for shape in grads + [(1, D), (1, D)]]
    shapes += [jax.ShapeDtypeStruct((1, 2, OWN, D), BF16), jax.ShapeDtypeStruct((1, 2, OWN, D), F32)]
    hbm = pl.BlockSpec(memory_space=pl.ANY)
    vmem = pl.BlockSpec(memory_space=pltpu.VMEM)
    dma = pltpu.SemaphoreType.DMA
    return pl.pallas_call(
        widen,
        out_shape=tuple(shapes),
        in_specs=[hbm, hbm, vmem, vmem, vmem],
        out_specs=tuple([hbm] * 7 + [vmem] * 4),
        scratch_shapes=[pltpu.VMEM((2, 4, 576, 512), BF16), pltpu.VMEM((2, 4, 288, 384), BF16)]
        + [pltpu.VMEM(shape, F32) for shape in grads]
        + [dma((2, 4)), dma((4,)), dma((28,))],
        compiler_params=pltpu.CompilerParams(vmem_limit_bytes=63 * 1024 * 1024),
        name="widen",
    )(ga, gb, gn, y, dx)


def on_device(inputs, cotangent, doc_lengths, norm_one, query_w, key_w, value_w, out_w, norm_two, gate_w, up_w, down_w):
    lane = np.arange(128) % HALF
    speed = jnp.asarray(np.exp(lane * (-2.0 * math.log(ROPE) / HD)).astype(np.float32)[None, :])
    y, dx, ga, gb, gn = step_call(
        inputs, cotangent, query_w[0].T, key_w[0].T, value_w[0].T, out_w[0], gate_w[0], up_w[0], down_w[0], norm_one, norm_two,
        doc_lengths, speed,
    )
    gate, up, down, out, query, key, value, one, two, y, dx = widened(ga, gb, gn, y, dx)
    return (y, dx, one, query.T[None], key.T[None], value.T[None], out[None], two, gate[None], up[None], down[None])


def solution(mesh):
    in_specs = (
        P(None, "dp", None),
        P(None, "dp", None),
        P(),
        P("section", None),
        P("section", None, "tensor"),
        P("section", None, "tensor"),
        P("section", None, "tensor"),
        P("section", "tensor", None),
        P("section", None),
        P("section", None, "tensor"),
        P("section", None, "tensor"),
        P("section", "tensor", None),
    )
    out_specs = (
        P("section", None, ("dp", "tensor"), None),
        P("section", None, ("dp", "tensor"), None),
        P("section", None),
        P("section", None, "tensor"),
        P("section", None, "tensor"),
        P("section", None, "tensor"),
        P("section", "tensor", None),
        P("section", None),
        P("section", None, "tensor"),
        P("section", None, "tensor"),
        P("section", "tensor", None),
    )
    return jax.shard_map(on_device, mesh=mesh, in_specs=in_specs, out_specs=out_specs, check_vma=False)
```

```python
import math

import jax
import jax.numpy as jnp
import numpy as np
from jax import lax
from jax.experimental import pallas as pl
from jax.experimental.pallas import tpu as pltpu
from jax.sharding import PartitionSpec as P

MESH = pl.DeviceIdType.MESH
F32 = jnp.float32
BF16 = jnp.bfloat16

HD = 96
HALF = HD // 2
D = 1536
FF = 512
ROWS = 256
OWN = 32
HROWS = 128
HOWN = 16
SCALE = 1.0 / math.sqrt(HD)
EPS = 1e-05
ROPE = 100000.0
MASKED = -1e30


def dot(a, b):
    return lax.dot_general(a, b, (((1,), (0,)), ((), ())), preferred_element_type=F32)


def dot_nt(a, b):
    return lax.dot_general(a, b, (((1,), (1,)), ((), ())), preferred_element_type=F32)


def dot_tn(a, b):
    return lax.dot_general(a, b, (((0,), (0,)), ((), ())), preferred_element_type=F32)


def lanes_of(v):
    return lax.broadcasted_iota(jnp.int32, v.shape, 1)


def swapped(v):
    return jnp.where(lanes_of(v) < HALF, pltpu.roll(v, 128 - HALF, 1), pltpu.roll(v, HALF, 1))


def place_of(i):
    return OWN * ((i // HOWN) % 8) + HOWN * (i // HROWS) + i % HOWN


def factor_of(v):
    return lax.rsqrt(jnp.mean(v * v, axis=-1, keepdims=True) + EPS)


def kernel(
    x_hbm, ct_hbm, wq_hbm, wk_hbm, wv_hbm, wo_hbm, wg_hbm, wu_hbm, wd_hbm, one_ref, two_ref, lengths_ref, speed_ref,
    y_out, dx_out, ga_out, gb_out, gn_out,
    wqkv, wo, wgu, wd, gains, gains_own, gains_in, cos_ref, sin_ref, beg_ref, df,
    n1, n2, q2, q2t, kv, o_f, o_b, stat_m, stat_l, gate_s, up_s, u_s, x_own, h_own,
    rsrc, land, da, do2, do2t, dgu, dq, dqkv, dkv_t, dkv_src, dkv_land, acc, s_m,
    ga, gb, da_in, db_in, za, zb, xa, xb, fa, fb, yb, dxb, dgain, dg_peer, dg_t, dg_d,
    w_l, w_s, w_r, ag_s, ag_r, rs_s, rs_r, kv_s, kv_r, dkv_s, dkv_r, out_l, out_s, out_r,
    ds_s, ds_r, z_s, z_r, x_s, x_r, a_s, a_r, a_l, f_s, f_r, ns, nr,
):
    sec = lax.axis_index("section")
    t = lax.axis_index("tensor")
    d = lax.axis_index("dp")
    other = 1 - sec
    z, xh = d // 2, d % 2

    barrier = pltpu.get_barrier_semaphore()

    def greet(axis, me, k, _):
        pl.semaphore_signal(barrier, inc=1, device_id={axis: (me + k) % 8}, device_id_type=MESH)
        return _

    pl.semaphore_signal(barrier, inc=1, device_id={"section": other}, device_id_type=MESH)
    lax.fori_loop(1, 8, lambda k, c: greet("tensor", t, k, c), 0)
    lax.fori_loop(1, 8, lambda k, c: greet("dp", d, k, c), 0)

    def load_rows(source, sem):
        def body(i, c):
            h, p = i // 8, i % 8
            pltpu.make_async_copy(
                source.at[sec, pl.ds(pl.multiple_of(p * OWN + h * HOWN, HOWN), HOWN)],
                df.at[pl.ds(pl.multiple_of(h * HROWS + p * HOWN, HOWN), HOWN)], sem,
            ).start()
            return c

        lax.fori_loop(0, 16, body, 0)

    def rows_loaded(source, sem):
        pltpu.make_async_copy(source.at[sec], df, sem).wait()

    own_parts = [
        (wq_hbm, lambda i: wqkv.at[i, pl.ds(0, 2 * HD)]),
        (wk_hbm, lambda i: wqkv.at[i, pl.ds(2 * HD, HD)]),
        (wv_hbm, lambda i: wqkv.at[i, pl.ds(3 * HD, HD)]),
        (wo_hbm, lambda i: wo.at[i]),
        (wg_hbm, lambda i: wgu.at[i, :, 0:FF]),
        (wu_hbm, lambda i: wgu.at[i, :, FF : 2 * FF]),
        (wd_hbm, lambda i: wd.at[i]),
    ]
    n_parts = len(own_parts)
    own_copies = [pltpu.make_async_copy(a, b(sec), w_l.at[i]) for i, (a, b) in enumerate(own_parts)]
    load_rows(x_hbm, w_l.at[8])
    for i in range(n_parts):
        own_copies[i].start()
    gains_own[0:8, :] = jnp.broadcast_to(one_ref[...].astype(F32), (8, D))
    gains_own[8:16, :] = jnp.broadcast_to(two_ref[...].astype(F32), (8, D))
    gains[sec] = gains_own[...]

    places = place_of(lax.broadcasted_iota(jnp.int32, (ROWS, 128), 0)) + d * ROWS

    lengths = jnp.where(sec == 0, lengths_ref[0:1, :], lengths_ref[1:2, :])
    start, begins = jnp.zeros((1, 1), jnp.int32), jnp.zeros((ROWS, 128), jnp.int32)
    for n in range(lengths.shape[1]):
        begins = jnp.maximum(begins, jnp.where(start <= places, start, 0))
        start = start + lengths[:, n : n + 1]
    beg_ref[...] = begins
    angles = (places - begins).astype(F32) * speed_ref[0:1, :]
    lane = lanes_of(angles)
    cos_ref[...] = jnp.where(lane < HD, jnp.cos(angles), 0.0)
    sine = jnp.sin(angles)
    sin_ref[...] = jnp.where(lane < HALF, -sine, jnp.where(lane < HD, sine, 0.0))
    pl.semaphore_wait(barrier, 15)
    sent_parts = [
        pltpu.make_async_remote_copy(
            src_ref=a, dst_ref=b(sec), send_sem=w_s.at[i], recv_sem=w_r.at[i],
            device_id={"section": other}, device_id_type=MESH,
        )
        for i, (a, b) in enumerate(own_parts)
    ]
    gains_sent = pltpu.make_async_remote_copy(
        src_ref=gains_own, dst_ref=gains_in, send_sem=w_s.at[n_parts], recv_sem=w_r.at[n_parts],
        device_id={"section": other}, device_id_type=MESH,
    )
    gains_sent.start()
    for i in range(n_parts):
        sent_parts[i].start()

    def gains_arrived():
        pltpu.make_async_remote_copy(
            src_ref=gains_own, dst_ref=gains_in, send_sem=w_s.at[n_parts], recv_sem=w_r.at[n_parts],
            device_id={"section": other}, device_id_type=MESH,
        ).wait_recv()
        gains[other] = gains_in[...]

    def weight_ready(layer, *which):
        @pl.when(layer == sec)
        def _():
            for i in which:
                own_copies[i].wait()

        @pl.when(layer != sec)
        def _():
            for i in which:
                a, b = own_parts[i]
                pltpu.make_async_remote_copy(
                    src_ref=a, dst_ref=b(other), send_sem=w_s.at[i], recv_sem=w_r.at[i],
                    device_id={"section": other}, device_id_type=MESH,
                ).wait_recv()

    def half_rows(half):
        return pl.ds(pl.multiple_of(half * HROWS, HROWS), HROWS)

    def pair_rows(half):
        return pl.ds(pl.multiple_of(half * ROWS, ROWS), ROWS)

    def rows_of(half, owner):
        return pl.ds(pl.multiple_of(half * HROWS + owner * HOWN, HOWN), HOWN)

    def kept(half):
        return pl.ds(pl.multiple_of(half * HOWN, HOWN), HOWN)

    def over_peers(body):
        def step(k, c):
            body((t + k) % 8)
            return c

        lax.fori_loop(1, 8, step, 0)

    def ag_copy(buf, i, half, to, owner):
        rows = rows_of(half, owner)
        return pltpu.make_async_remote_copy(
            src_ref=buf.at[rows], dst_ref=buf.at[rows], send_sem=ag_s.at[i, half, to], recv_sem=ag_r.at[i, half, owner],
            device_id={"tensor": to}, device_id_type=MESH,
        )

    def ag_start(buf, i, half):
        over_peers(lambda p: ag_copy(buf, i, half, p, t).start())

    def ag_wait(buf, i, half):
        over_peers(lambda p: ag_copy(buf, i, half, t, p).wait_recv())

    def ag_sent(buf, i, half):
        over_peers(lambda p: ag_copy(buf, i, half, p, t).wait_send())

    def rs_copy(i, half, to, sender):
        return pltpu.make_async_remote_copy(
            src_ref=rsrc.at[i, rows_of(half, to)], dst_ref=land.at[i, half, sender], send_sem=rs_s.at[i, half, to],
            recv_sem=rs_r.at[i, half, sender], device_id={"tensor": to}, device_id_type=MESH,
        )

    def rs_start(i, half):
        over_peers(lambda p: rs_copy(i, half, p, t).start())

    def rs_sum(i, half):
        def body(k, total):
            p = (t + k) % 8
            rs_copy(i, half, t, p).wait_recv()
            return total + land[i, half, p].astype(F32)

        return lax.fori_loop(1, 8, body, rsrc[i, rows_of(half, t), :].astype(F32))

    def rs_sent(i, half):
        over_peers(lambda p: rs_copy(i, half, p, t).wait_send())

    def both(body):
        def step(half, c):
            body(half)
            return c

        lax.fori_loop(0, 2, step, 0)

    def allowed_of(j, half):
        rows = place_of(lax.broadcasted_iota(jnp.int32, (HROWS, 1), 0) + half * HROWS) + d * ROWS
        cols = place_of(lax.broadcasted_iota(jnp.int32, (1, ROWS), 1)) + j * ROWS
        allowed = (cols <= rows) & (cols >= beg_ref[half_rows(half), 0:1])
        return jnp.concatenate([jnp.where(allowed, 0.0, MASKED)] * 2, axis=0)

    pl.when(sec == 1)(gains_arrived)
    rows_loaded(x_hbm, w_l.at[8])

    def first_norm(i, c):
        rows = pl.ds(pl.multiple_of(i * OWN, OWN), OWN)
        v = df[rows, :].astype(F32)
        n1[0, rows, :] = (v * factor_of(v) * gains[0, 0:1, :]).astype(BF16)
        return c

    lax.fori_loop(0, ROWS // OWN, first_norm, 0)
    for half in range(2):
        x_own[0, kept(half), :] = df[rows_of(half, t), :].astype(F32)
    load_rows(ct_hbm, w_l.at[9])

    def forward_layer(layer, c):
        weight_ready(layer, 0, 1, 2)

        def kv_copy(owner, to, half):
            part = kv.at[layer, owner, :, half_rows(half)]
            return pltpu.make_async_remote_copy(
                src_ref=part, dst_ref=part, send_sem=kv_s.at[to, half], recv_sem=kv_r.at[owner, layer, half],
                device_id={"dp": to}, device_id_type=MESH,
            )

        def project(half):
            rows = half_rows(half)

            @pl.when(layer == 1)
            def _():
                ag_wait(n1.at[1], 0, half)

            raw = dot_nt(n1[layer, rows, :], wqkv[layer])
            c0, c1, c2 = raw[:, 0:128], raw[:, 128:256], raw[:, 256:384]
            lane = lanes_of(c0)
            q1 = jnp.where(lane < 32, pltpu.roll(c0, 32, 1), pltpu.roll(c1, 32, 1))
            k0 = jnp.where(lane < 64, pltpu.roll(c1, 64, 1), pltpu.roll(c2, 64, 1))
            v0 = pltpu.roll(c2, 96, 1)
            cosine, sine = cos_ref[rows, :], sin_ref[rows, :]
            turned = k0 * cosine + swapped(k0) * sine
            kv[layer, d, pl.ds(0, HD), rows] = jnp.transpose(turned)[0:HD, :].astype(BF16)
            kv[layer, d, pl.ds(HD, HD), rows] = jnp.transpose(v0)[0:HD, :].astype(BF16)

            def kv_send(k, c):
                kv_copy(d, 8 + d - k, half).start()
                return c

            lax.fori_loop(d + 1, 8, kv_send, 0)
            for h, part in ((0, c0), (1, q1)):
                turned = part * cosine + swapped(part) * sine
                place = pl.ds(pl.multiple_of(half * ROWS + h * HROWS, HROWS), HROWS)
                q2[layer, place, :] = turned[:, 0:HD].astype(BF16)
                q2t[layer, :, place] = jnp.transpose(turned)[0:HD, :].astype(BF16)

        both(project)

        @pl.when(layer == 1)
        def _():
            both(lambda half: ag_sent(n1.at[1], 0, half))

        weight_ready(layer, 3)

        def attend_half(half):
            rows = pair_rows(half)
            s_m[rows, :] = jnp.full((ROWS, 1), MASKED, F32)
            stat_l[layer, rows, :] = jnp.zeros((ROWS, 1), F32)
            acc[rows, :] = jnp.zeros((ROWS, HD), F32)

            def attend(i, c):
                j = d - i

                @pl.when((i > 0) & (half == 0))
                def _():
                    kv_copy(j, d, 0).wait_recv()
                    kv_copy(j, d, 1).wait_recv()

                s = dot(q2[layer, rows, :], kv[layer, j, pl.ds(0, HD), :]) * SCALE + allowed_of(j, half)
                old = s_m[rows, :]
                new = jnp.maximum(old, jnp.max(s, axis=-1, keepdims=True))
                p = jnp.exp(s - new)
                shrink = jnp.exp(old - new)
                s_m[rows, :] = new
                stat_l[layer, rows, :] = stat_l[layer, rows, :] * shrink + jnp.sum(p, axis=-1, keepdims=True)
                acc[rows, :] = acc[rows, :] * shrink + dot_nt(p.astype(BF16), kv[layer, j, pl.ds(HD, HD), :])
                return c

            lax.fori_loop(0, d + 1, attend, 0)
            total = stat_l[layer, rows, :]
            mixed = acc[rows, :] / total
            o_f[layer, rows, :] = mixed
            o_b[layer, rows, :] = mixed.astype(BF16)
            stat_m[layer, rows, :] = s_m[rows, :] + jnp.log(total)
            first = pl.ds(pl.multiple_of(half * ROWS, HROWS), HROWS)
            second = pl.ds(pl.multiple_of(half * ROWS + HROWS, HROWS), HROWS)

            def out_part(n, c):
                cols = pl.ds(pl.multiple_of(n * 512, 512), 512)
                part = dot(o_b[layer, first, :], wo[layer, pl.ds(0, HD), cols])
                part += dot(o_b[layer, second, :], wo[layer, pl.ds(HD, HD), cols])
                rsrc[0, half_rows(half), cols] = part.astype(BF16)
                return c

            lax.fori_loop(0, 3, out_part, 0)
            rs_start(0, half)

        both(attend_half)

        def middle(half):
            v = x_own[layer, kept(half), :] + rs_sum(0, half)
            h_own[layer, kept(half), :] = v
            n2[layer, rows_of(half, t), :] = (v * factor_of(v) * gains[layer, 8:9, :]).astype(BF16)
            ag_start(n2.at[layer], 1, half)
            rs_sent(0, half)

        both(middle)
        weight_ready(layer, 4, 5)
        weight_ready(layer, 6)

        def feed(half):
            rows = half_rows(half)
            ag_wait(n2.at[layer], 1, half)

            def units(n, c):
                cols = pl.ds(pl.multiple_of(n * 256, 256), 256)
                above = pl.ds(pl.multiple_of(n * 256 + FF, 256), 256)
                g = dot(n2[layer, rows, :], wgu[layer, :, cols])
                up = dot(n2[layer, rows, :], wgu[layer, :, above])
                gate_s[layer, rows, cols] = g
                up_s[layer, rows, cols] = up
                u_s[layer, rows, cols] = (g * jax.nn.sigmoid(g) * up).astype(BF16)
                return c

            lax.fori_loop(0, 2, units, 0)

            def down_part(n, c):
                cols = pl.ds(pl.multiple_of(n * 512, 512), 512)
                rsrc[1, rows, cols] = dot(u_s[layer, rows, :], wd[layer, :, cols]).astype(BF16)
                return c

            lax.fori_loop(0, 3, down_part, 0)
            rs_start(1, half)
            ag_sent(n2.at[layer], 1, half)

        both(feed)

        pl.when((layer == 0) & (sec == 0))(gains_arrived)

        def result(half):
            y = (h_own[layer, kept(half), :] + rs_sum(1, half)).astype(BF16)
            yb[layer, kept(half), :] = y

            @pl.when(layer == 0)
            def _():
                v = y.astype(F32)
                x_own[1, kept(half), :] = v
                n1[1, rows_of(half, t), :] = (v * factor_of(v) * gains[1, 0:1, :]).astype(BF16)
                ag_start(n1.at[1], 0, half)

            rs_sent(1, half)

        both(result)

        def kv_sent(k, c):
            kv_copy(d, k, 0).wait_send()
            kv_copy(d, k, 1).wait_send()
            return c

        lax.fori_loop(d + 1, 8, kv_sent, 0)
        row_out(layer, yb, y_out, 0)
        return c

    def row_out(layer, buf, out, i):
        @pl.when(layer == sec)
        def _():
            pltpu.make_async_copy(buf.at[layer], out.at[sec], out_l.at[i]).start()

        @pl.when(layer != sec)
        def _():
            pltpu.make_async_remote_copy(
                src_ref=buf.at[layer], dst_ref=out.at[sec], send_sem=out_s.at[i], recv_sem=out_r.at[i],
                device_id={"section": other}, device_id_type=MESH,
            ).start()

    def row_out_wait(buf, out, i):
        pltpu.make_async_copy(buf.at[sec], out.at[sec], out_l.at[i]).wait()
        copy = pltpu.make_async_remote_copy(
            src_ref=buf.at[other], dst_ref=out.at[other], send_sem=out_s.at[i], recv_sem=out_r.at[i],
            device_id={"section": other}, device_id_type=MESH,
        )
        copy.wait_send()
        copy.wait_recv()

    lax.fori_loop(0, 2, forward_layer, 0)

    rows_loaded(ct_hbm, w_l.at[9])

    sets = ((ga, da_in, za, xa, fa, ga_out), (gb, db_in, zb, xb, fb, gb_out))
    before, after = (z + 3) % 4, (z + 1) % 4
    far = (z + 2) % 4

    def dp_at(zz, xx):
        return zz * 2 + xx

    def quarter(i, which):
        size = (288, 144)[i]
        return pl.ds(pl.multiple_of(which * size, 16), size)

    def swap_cores(layer, i, chunk):
        return pltpu.make_async_remote_copy(
            src_ref=sets[i][0].at[layer, other, chunk], dst_ref=sets[i][1].at[layer, chunk], send_sem=ds_s.at[i, layer, chunk],
            recv_sem=ds_r.at[i, layer, chunk], device_id={"section": other}, device_id_type=MESH,
        )

    def chunk_at(n):
        return (z + jnp.where(n == 0, 2, jnp.where(n == 3, 0, 2 * n - 1))) % 4

    def add_rows(target, index, first, size, sources):
        count = 96 if size % 96 == 0 else 48

        def add(n, carry):
            here = pl.ds(pl.multiple_of(first + n * count, 16), count)
            total = target[(*index, here)].astype(F32)
            for ref, place, start in sources:
                total += ref[(*place, pl.ds(pl.multiple_of(start + n * count, 16), count))].astype(F32)
            target[(*index, here)] = total.astype(BF16)
            return carry

        lax.fori_loop(0, size // count, add, 0)

    def z_piece(layer, i, piece, chunk, which, to):
        return pltpu.make_async_remote_copy(
            src_ref=sets[i][0].at[layer, sec, chunk, quarter(i, which)], dst_ref=sets[i][2].at[layer, piece],
            send_sem=z_s.at[i, layer, piece], recv_sem=z_r.at[i, layer, piece], device_id={"dp": dp_at(to, xh)},
            device_id_type=MESH,
        )

    def sum_1(layer, i):
        g, arrived = sets[i][0:2]
        for chunk, sends in (
            (far, ((0, 0, after), (1, 1, before))),
            (after, ((2, 1, after),)),
            (before, ((3, 0, before),)),
            (z, ()),
        ):
            swap_cores(layer, i, chunk).wait_recv()
            add_rows(g, (layer, sec, chunk), 0, g.shape[3], [(arrived, (layer, chunk), 0)])
            for piece, which, to in sends:
                z_piece(layer, i, piece, chunk, which, to).start()

    def sum_2(layer, i):
        g, landed = sets[i][0], sets[i][2]
        size = landed.shape[2]
        z_piece(layer, i, 0, far, 0, after).wait_recv()
        add_rows(g, (layer, sec, after), 0, size, [(landed, (layer, 0), 0)])
        z_piece(layer, i, 4, after, 0, after).start()
        z_piece(layer, i, 1, far, 1, before).wait_recv()
        add_rows(g, (layer, sec, before), size, size, [(landed, (layer, 1), 0)])
        z_piece(layer, i, 5, before, 1, before).start()

    def x_over(layer, i):
        return pltpu.make_async_remote_copy(
            src_ref=sets[i][0].at[layer, sec, z, quarter(i, 1 - xh)], dst_ref=sets[i][3].at[layer],
            send_sem=x_s.at[i, 0, layer], recv_sem=x_r.at[i, 0, layer], device_id={"dp": dp_at(z, 1 - xh)},
            device_id_type=MESH,
        )

    def x_back(layer, i, which):
        part = sets[i][4].at[layer, quarter(i, which)]
        return pltpu.make_async_remote_copy(
            src_ref=part, dst_ref=part, send_sem=x_s.at[i, 1, layer], recv_sem=x_r.at[i, 1, layer],
            device_id={"dp": dp_at(z, 1 - xh)}, device_id_type=MESH,
        )

    def sum_3(layer, i):
        g, landed = sets[i][0], sets[i][2]
        size = landed.shape[2]
        for piece in (2, 3, 4, 5):
            z_piece(layer, i, piece, z, 0, after).wait_recv()
        add_rows(g, (layer, sec, z), 0, size, [(landed, (layer, 3), 0), (landed, (layer, 4), 0)])
        add_rows(g, (layer, sec, z), size, size, [(landed, (layer, 2), 0), (landed, (layer, 5), 0)])
        x_over(layer, i).start()

    def spread(layer, i, half, chunk, which, to, k):
        rows = quarter(i, which)
        return pltpu.make_async_remote_copy(
            src_ref=sets[i][4].at[layer, rows], dst_ref=sets[i][5].at[half, chunk, rows], send_sem=a_s.at[i, layer, which, k],
            recv_sem=a_r.at[i, half, chunk, which], device_id={"section": layer, "dp": dp_at(to, xh)}, device_id_type=MESH,
        )

    def keep(layer, i, which):
        rows = quarter(i, which)
        return pltpu.make_async_copy(sets[i][4].at[layer, rows], sets[i][5].at[sec, z, rows], a_l.at[i, which])

    def spread_all(layer, i, which):
        spread(layer, i, sec, z, which, after, 0).start()
        spread(layer, i, sec, z, which, before, 1).start()

        @pl.when(layer == sec)
        def _():
            keep(layer, i, which).start()

        @pl.when(layer != sec)
        def _():
            spread(layer, i, sec, z, which, z, 2).start()

    def sum_4(layer, i):
        g, over, done = sets[i][0], sets[i][3], sets[i][4]
        size = over.shape[1]
        x_over(layer, i).wait_recv()

        def add(n, carry):
            here = pl.ds(pl.multiple_of(n * 48, 16), 48)
            there = pl.ds(pl.multiple_of(xh * size + n * 48, 16), 48)
            done[layer, there, :] = (g[layer, sec, z, there, :].astype(F32) + over[layer, here, :].astype(F32)).astype(BF16)
            return carry

        lax.fori_loop(0, size // 48, add, 0)
        x_back(layer, i, xh).start()
        spread_all(layer, i, xh)

    def sum_5(layer, i):
        x_back(layer, i, 1 - xh).wait_recv()
        spread_all(layer, i, 1 - xh)

    def pass_on(i, half, chunk, which, to):
        part = sets[i][5].at[half, chunk, quarter(i, which)]
        return pltpu.make_async_remote_copy(
            src_ref=part, dst_ref=part, send_sem=f_s.at[i, half, which], recv_sem=f_r.at[i, half, which],
            device_id={"dp": dp_at(to, xh)}, device_id_type=MESH,
        )

    def sum_6(i):
        for half in range(2):
            spread(sec, i, half, before, 0, z, 0).wait_recv()
            pass_on(i, half, before, 0, after).start()
            spread(sec, i, half, after, 1, z, 0).wait_recv()
            pass_on(i, half, after, 1, before).start()

    def sum_7(i):
        for which in range(2):
            keep(sec, i, which).wait()
            spread(sec, i, other, z, which, z, 2).wait_recv()
            spread(other, i, sec, z, which, z, 2).wait_send()
            for half in range(2):
                spread(sec, i, half, (after, before)[which], which, z, 0).wait_recv()
                pass_on(i, half, far, which, z).wait_recv()
                pass_on(i, half, z, which, after).wait_send()
        for layer in range(2):
            for chunk in range(4):
                swap_cores(layer, i, chunk).wait_send()
            for piece in range(6):
                z_piece(layer, i, piece, z, 0, after).wait_send()
            x_over(layer, i).wait_send()
            x_back(layer, i, xh).wait_send()
            for which in range(2):
                spread(layer, i, sec, z, which, after, 0).wait_send()
                spread(layer, i, sec, z, which, before, 1).wait_send()

    def backward_layer(step, c):
        layer = 1 - step


        @pl.when(step == 1)
        def _():
            sum_5(1, 0)
            sum_2(1, 1)

        def feed_back(half):
            rows = half_rows(half)

            @pl.when(step == 1)
            def _():
                ag_wait(df, 2, half)

            dxb[layer, kept(half), :] = df[rows_of(half, t), :].astype(F32)

            def unit_grads(n, c):
                cols = pl.ds(pl.multiple_of(n * 256, 256), 256)
                above = pl.ds(pl.multiple_of(n * 256 + FF, 256), 256)
                du = dot_nt(df[rows, :], wd[layer, cols, :])
                g, up = gate_s[layer, rows, cols], up_s[layer, rows, cols]
                sig = jax.nn.sigmoid(g)
                dgu[rows, cols] = (du * up * sig * (1.0 + g * (1.0 - sig))).astype(BF16)
                dgu[rows, above] = (du * g * sig).astype(BF16)
                return c

            lax.fori_loop(0, 2, unit_grads, 0)

            def normed_part(n, c):
                cols = pl.ds(pl.multiple_of(n * 256, 256), 256)
                rsrc[0, rows, cols] = dot_nt(dgu[rows, :], wgu[layer, cols, :]).astype(BF16)
                return c

            lax.fori_loop(0, 6, normed_part, 0)
            rs_start(0, half)

        both(feed_back)

        @pl.when(step == 1)
        def _():
            both(lambda half: ag_sent(df, 2, half))

        def unit_weights(k, c):
            n = chunk_at(k)
            cols = pl.ds(pl.multiple_of(n * 384, 384), 384)
            got = dot_tn(n2[layer, :, cols], dgu[...]).astype(BF16)
            for h in range(2):
                ga[layer, h, n, pl.ds(0, 192), :] = got[192 * h : 192 * h + 192, 0:FF]
                ga[layer, h, n, pl.ds(192, 192), :] = got[192 * h : 192 * h + 192, FF : 2 * FF]
            cols = pl.ds(pl.multiple_of(n * 128, 128), 128)
            got = dot_tn(u_s[layer, :, cols], df[...]).astype(BF16)
            for h in range(2):
                for i in range(3):
                    ga[layer, h, n, pl.ds(384 + 64 * i, 64), :] = got[64 * h : 64 * h + 64, 512 * i : 512 * i + 512]
            swap_cores(layer, 0, n).start()
            return c

        lax.fori_loop(0, 4, unit_weights, 0)
        sum_1(layer, 0)

        @pl.when((step == 1) & (sec == 1))
        def _():
            sum_6(0)


        def hidden_grads(half):
            dn = rs_sum(0, half)
            h = h_own[layer, kept(half), :]
            r = factor_of(h)
            tt = dn * gains[layer, 8:9, :]
            dh = dxb[layer, kept(half), :] + r * tt - h * (r * r * r * jnp.mean(h * tt, axis=-1, keepdims=True))
            dgain[layer, 1:2, :] += jnp.sum(dn * h * r, axis=0, keepdims=True)
            dxb[layer, kept(half), :] = dh
            da[rows_of(half, t), :] = dh.astype(BF16)
            ag_start(da, 3, half)
            rs_sent(0, half)

        both(hidden_grads)
        sum_2(layer, 0)

        @pl.when(step == 1)
        def _():
            sum_3(1, 1)


        def mixed_grads(half):
            ag_wait(da, 3, half)
            for h in range(2):
                place = pl.ds(pl.multiple_of(half * ROWS + h * HROWS, HROWS), HROWS)
                got = dot_nt(da[half_rows(half), :], wo[layer, pl.ds(h * HD, HD), :])
                do2[place, :] = got.astype(BF16)
                padded = jnp.concatenate([got, jnp.zeros((HROWS, 128 - HD), F32)], axis=1)
                do2t[:, place] = jnp.transpose(padded)[0:HD, :].astype(BF16)

        both(mixed_grads)
        both(lambda half: ag_sent(da, 3, half))
        dot_rows = jnp.sum(do2[...].astype(F32) * o_f[layer], axis=-1, keepdims=True)
        s_m[...] = dot_rows
        acc[...] = jnp.zeros(acc.shape, F32)

        def dkv_copy(to, sender):
            return pltpu.make_async_remote_copy(
                src_ref=dkv_src.at[to], dst_ref=dkv_land.at[layer, sender], send_sem=dkv_s.at[to], recv_sem=dkv_r.at[layer, sender],
                device_id={"dp": to}, device_id_type=MESH,
            )

        def attend_back(j, c):
            dkt = jnp.zeros((HD, ROWS), F32)
            dvt = jnp.zeros((HD, ROWS), F32)
            for half in range(2):
                rows = pair_rows(half)
                kt = kv[layer, j, pl.ds(0, HD), :]
                s = dot(q2[layer, rows, :], kt) * SCALE + allowed_of(j, half)
                p = jnp.exp(s - stat_m[layer, rows, :])
                dp = dot(do2[rows, :], kv[layer, j, pl.ds(HD, HD), :])
                ds = (p * (dp - s_m[rows, :])).astype(BF16)
                acc[rows, :] += dot_nt(ds, kt)
                dkt += dot(q2t[layer, :, rows], ds)
                dvt += dot(do2t[:, rows], p.astype(BF16))
            dkv_src[j, pl.ds(0, HD), :] = (dkt * SCALE).astype(BF16)
            dkv_src[j, pl.ds(HD, HD), :] = dvt.astype(BF16)

            @pl.when(j < d)
            def _():
                dkv_copy(j, d).start()

            return c

        lax.fori_loop(0, d + 1, attend_back, 0)

        def out_weights(n, c):
            cols = pl.ds(pl.multiple_of(n * 384, 384), 384)
            for h in range(2):
                mixed = [o_b[layer, pl.ds(half * ROWS + h * HROWS, HROWS), :] for half in range(2)]
                got = dot_tn(jnp.concatenate(mixed, axis=0), da[:, cols])
                gb[layer, 0, n, pl.ds(h * HD, HD), :] = got.astype(BF16)
            return c

        lax.fori_loop(0, 4, out_weights, 0)

        sum_3(layer, 0)

        @pl.when(step == 1)
        def _():
            sum_4(1, 1)

        def dkv_sum(k, total):
            dkv_copy(d, k).wait_recv()
            return total + dkv_land[layer, k].astype(F32)

        dkv_total = lax.fori_loop(d + 1, 8, dkv_sum, dkv_src[d].astype(F32))
        dkv_t[...] = jnp.zeros(dkv_t.shape, F32)
        dkv_t[0, pl.ds(0, HD), :] = dkv_total[0:HD]
        dkv_t[1, pl.ds(0, HD), :] = dkv_total[HD : 2 * HD]
        dk_rot = jnp.transpose(dkv_t[0])
        dv = jnp.transpose(dkv_t[1])
        cosine, sine = cos_ref[...], sin_ref[...]
        dq[...] = jnp.zeros(dq.shape, F32)
        dq[:, 0:HD] = acc[...] * SCALE
        dq0, dq1 = (
            jnp.concatenate([dq[pl.ds(half * ROWS + h * HROWS, HROWS), :] for half in range(2)], axis=0) for h in range(2)
        )
        dq0 = dq0 * cosine - swapped(dq0) * sine
        dq1 = dq1 * cosine - swapped(dq1) * sine
        dk = dk_rot * cosine - swapped(dk_rot) * sine
        lane = lanes_of(dk)
        dqkv[:, 0:128] = jnp.where(lane < HD, dq0, pltpu.roll(dq1, 96, 1)).astype(BF16)
        dqkv[:, 128:256] = jnp.where(lane < 64, pltpu.roll(dq1, 96, 1), pltpu.roll(dk, 64, 1)).astype(BF16)
        dqkv[:, 256:384] = jnp.where(lane < 32, pltpu.roll(dk, 64, 1), pltpu.roll(dv, 32, 1)).astype(BF16)

        def project_back(half):
            rows = half_rows(half)

            def input_part(n, c):
                cols = pl.ds(pl.multiple_of(n * 512, 512), 512)
                rsrc[1, rows, cols] = dot(dqkv[rows, :], wqkv[layer, :, cols]).astype(BF16)
                return c

            lax.fori_loop(0, 3, input_part, 0)
            rs_start(1, half)

        both(project_back)

        def qkv_weights(k, c):
            n = chunk_at(k)
            cols = pl.ds(pl.multiple_of(n * 384, 384), 384)
            got = dot_tn(dqkv[...], n1[layer, :, cols]).astype(BF16)
            gb[layer, 0, n, pl.ds(2 * HD, HD), :] = got[0:HD]
            gb[layer, 1, n] = got[HD : 4 * HD]
            swap_cores(layer, 1, n).start()
            return c

        lax.fori_loop(0, 4, qkv_weights, 0)
        sum_1(layer, 1)
        sum_4(layer, 0)

        @pl.when(step == 1)
        def _():
            sum_5(1, 1)

        def input_grads(half):
            dn = rs_sum(1, half)
            v = x_own[layer, kept(half), :]
            r = factor_of(v)
            tt = dn * gains[layer, 0:1, :]
            dx = dxb[layer, kept(half), :] + r * tt - v * (r * r * r * jnp.mean(v * tt, axis=-1, keepdims=True))
            dgain[layer, 0:1, :] += jnp.sum(dn * v * r, axis=0, keepdims=True)
            dxb[layer, kept(half), :] = dx

            @pl.when(step == 0)
            def _():
                df[rows_of(half, t), :] = dx.astype(BF16)
                ag_start(df, 2, half)

            rs_sent(1, half)

        both(input_grads)

        def dkv_sent(k, c):
            dkv_copy(k, d).wait_send()
            return c

        lax.fori_loop(0, d, dkv_sent, 0)
        row_out(layer, dxb, dx_out, 1)
        return c

    dgain[...] = jnp.zeros(dgain.shape, F32)
    lax.fori_loop(0, 2, backward_layer, 0)

    mate = pltpu.make_async_remote_copy(
        src_ref=dgain.at[other], dst_ref=dg_peer, send_sem=ns.at[0, 0], recv_sem=nr.at[0, 0],
        device_id={"section": other}, device_id_type=MESH,
    )
    mate.start()
    sum_5(0, 0)
    sum_2(0, 1)

    @pl.when(sec == 1)
    def _():
        sum_6(1)

    def gain_copy(axis, i, buf, me, to, sender):
        return pltpu.make_async_remote_copy(
            src_ref=buf.at[me], dst_ref=buf.at[sender], send_sem=ns.at[i, to], recv_sem=nr.at[i, sender],
            device_id={axis: to}, device_id_type=MESH,
        )

    def gain_send(axis, i, buf, me):
        def send(k, c):
            gain_copy(axis, i, buf, me, (me + k) % 8, me).start()
            return c

        lax.fori_loop(1, 8, send, 0)

    def gain_sum(axis, i, buf, me):
        def take(k, total):
            p = (me + k) % 8
            gain_copy(axis, i, buf, me, p, p).wait_recv()
            return total + buf[p]

        def sent(k, c):
            gain_copy(axis, i, buf, me, (me + k) % 8, me).wait_send()
            return c

        total = lax.fori_loop(1, 8, take, buf[me])
        lax.fori_loop(1, 8, sent, 0)
        return total

    mate.wait_recv()
    mate.wait_send()
    dg_t[t] = dgain[sec] + dg_peer[...]
    gain_send("tensor", 1, dg_t, t)

    @pl.when(sec == 0)
    def _():
        sum_6(0)

    sum_3(0, 1)
    dg_d[d] = gain_sum("tensor", 1, dg_t, t)
    gain_send("dp", 2, dg_d, d)
    sum_4(0, 1)
    sum_5(0, 1)

    @pl.when(sec == 0)
    def _():
        sum_6(1)

    gn_out[...] = gain_sum("dp", 2, dg_d, d)
    sum_7(0)
    sum_7(1)
    row_out_wait(yb, y_out, 0)
    row_out_wait(dxb, dx_out, 1)
    for i in range(n_parts):
        sent_parts[i].wait_send()
    gains_sent.wait_send()


def step_call(*args):
    hbm = pl.BlockSpec(memory_space=pl.ANY)
    vmem = pl.BlockSpec(memory_space=pltpu.VMEM)
    dma = pltpu.SemaphoreType.DMA
    scratch = [
        pltpu.VMEM((2, 384, D), BF16), pltpu.VMEM((2, 192, D), BF16), pltpu.VMEM((2, D, 2 * FF), BF16),
        pltpu.VMEM((2, FF, D), BF16), pltpu.VMEM((2, 16, D), F32), pltpu.VMEM((16, D), F32), pltpu.VMEM((16, D), F32), pltpu.VMEM((ROWS, 128), F32),
        pltpu.VMEM((ROWS, 128), F32), pltpu.VMEM((ROWS, 128), jnp.int32), pltpu.VMEM((ROWS, D), BF16),
        pltpu.VMEM((2, ROWS, D), BF16), pltpu.VMEM((2, ROWS, D), BF16), pltpu.VMEM((2, 2 * ROWS, HD), BF16),
        pltpu.VMEM((2, HD, 2 * ROWS), BF16), pltpu.VMEM((2, 8, 2 * HD, ROWS), BF16), pltpu.VMEM((2, 2 * ROWS, HD), F32),
        pltpu.VMEM((2, 2 * ROWS, HD), BF16), pltpu.VMEM((2, 2 * ROWS, 1), F32), pltpu.VMEM((2, 2 * ROWS, 1), F32),
        pltpu.VMEM((2, ROWS, FF), F32), pltpu.VMEM((2, ROWS, FF), F32), pltpu.VMEM((2, ROWS, FF), BF16),
        pltpu.VMEM((2, OWN, D), F32), pltpu.VMEM((2, OWN, D), F32),
        pltpu.VMEM((2, ROWS, D), BF16), pltpu.VMEM((2, 2, 8, HOWN, D), BF16), pltpu.VMEM((ROWS, D), BF16),
        pltpu.VMEM((2 * ROWS, HD), BF16), pltpu.VMEM((HD, 2 * ROWS), BF16), pltpu.VMEM((ROWS, 2 * FF), BF16),
        pltpu.VMEM((2 * ROWS, 128), F32), pltpu.VMEM((ROWS, 384), BF16), pltpu.VMEM((2, 128, ROWS), F32),
        pltpu.VMEM((8, 2 * HD, ROWS), BF16), pltpu.VMEM((2, 8, 2 * HD, ROWS), BF16), pltpu.VMEM((2 * ROWS, HD), F32),
        pltpu.VMEM((2 * ROWS, 1), F32),
        pltpu.VMEM((2, 2, 4, 576, 512), BF16), pltpu.VMEM((2, 2, 4, 288, 384), BF16), pltpu.VMEM((2, 4, 576, 512), BF16),
        pltpu.VMEM((2, 4, 288, 384), BF16), pltpu.VMEM((2, 6, 288, 512), BF16), pltpu.VMEM((2, 6, 144, 384), BF16),
        pltpu.VMEM((2, 288, 512), BF16), pltpu.VMEM((2, 144, 384), BF16), pltpu.VMEM((2, 576, 512), BF16),
        pltpu.VMEM((2, 288, 384), BF16),
        pltpu.VMEM((2, OWN, D), BF16), pltpu.VMEM((2, OWN, D), F32), pltpu.VMEM((2, 8, D), F32), pltpu.VMEM((8, D), F32),
        pltpu.VMEM((8, 8, D), F32), pltpu.VMEM((8, 8, D), F32),
        dma((10,)), dma((8,)), dma((8,)), dma((4, 2, 8)), dma((4, 2, 8)), dma((2, 2, 8)), dma((2, 2, 8)), dma((8, 2)), dma((8, 2, 2)),
        dma((8,)), dma((2, 8)), dma((2,)), dma((2,)), dma((2,)),
        dma((2, 2, 4)), dma((2, 2, 4)), dma((2, 2, 6)), dma((2, 2, 6)), dma((2, 2, 2)), dma((2, 2, 2)), dma((2, 2, 2, 3)),
        dma((2, 2, 4, 2)), dma((2, 2)), dma((2, 2, 2)), dma((2, 2, 2)), dma((3, 8)), dma((3, 8)),
    ]
    return pl.pallas_call(
        kernel,
        out_shape=(
            jax.ShapeDtypeStruct((2, OWN, D), BF16),
            jax.ShapeDtypeStruct((2, OWN, D), F32),
            jax.ShapeDtypeStruct((2, 4, 576, 512), BF16),
            jax.ShapeDtypeStruct((2, 4, 288, 384), BF16),
            jax.ShapeDtypeStruct((8, D), F32),
        ),
        in_specs=[hbm] * 9 + [vmem] * 4,
        out_specs=(hbm, hbm, hbm, hbm, vmem),
        scratch_shapes=scratch,
        compiler_params=pltpu.CompilerParams(
            collective_id=0, has_side_effects=True, vmem_limit_bytes=64 * 1024 * 1024 - 65536
        ),
        name="train_step",
    )(*args)


def widen(
    ga_hbm, gb_hbm, gn_ref, y_ref, dx_ref,
    gate_hbm, up_hbm, down_hbm, out_hbm, query_hbm, key_hbm, value_hbm, one_ref, two_ref, y_out, dx_out,
    ga, gb, gate, up, down, out, query, key, value, a_in, b_in, sent,
):
    parts = [(h, c) for c in range(4) for h in range(2)]
    a_copies = [pltpu.make_async_copy(ga_hbm.at[h, c], ga.at[h, c], a_in.at[h, c]) for h, c in parts]
    b_copies = [pltpu.make_async_copy(gb_hbm.at[:, c], gb.at[:, c], b_in.at[c]) for c in range(4)]
    for copy in b_copies + a_copies:
        copy.start()
    one_ref[...] = gn_ref[0:1, :]
    two_ref[...] = gn_ref[1:2, :]
    y_out[0] = y_ref[...]
    dx_out[0] = dx_ref[...]
    for c in range(4):
        b_copies[c].wait()
        cols = pl.ds(384 * c, 384)
        out[:, cols] = gb[0, c, 0:192, :].astype(F32)
        query[0:HD, cols] = gb[0, c, 192:288, :].astype(F32)
        query[HD : 2 * HD, cols] = gb[1, c, 0:HD, :].astype(F32)
        key[:, cols] = gb[1, c, HD : 2 * HD, :].astype(F32)
        value[:, cols] = gb[1, c, 2 * HD : 3 * HD, :].astype(F32)
    leaving = [
        pltpu.make_async_copy(buf, to, sent.at[i])
        for i, (buf, to) in enumerate(((out, out_hbm), (query, query_hbm), (key, key_hbm), (value, value_hbm)))
    ]
    for copy in leaving:
        copy.start()
    for i, (h, c) in enumerate(parts):
        a_copies[i].wait()
        rows, few = pl.ds(384 * c + 192 * h, 192), pl.ds(128 * c + 64 * h, 64)
        gate[rows, :] = ga[h, c, 0:192, :].astype(F32)
        up[rows, :] = ga[h, c, 192:384, :].astype(F32)
        for k in range(3):
            down[few, pl.ds(512 * k, 512)] = ga[h, c, 384 + 64 * k : 448 + 64 * k, :].astype(F32)
        for k, (buf, to, which) in enumerate(((gate, gate_hbm, rows), (up, up_hbm, rows), (down, down_hbm, few))):
            copy = pltpu.make_async_copy(buf.at[which], to.at[which], sent.at[4 + 3 * i + k])
            copy.start()
            leaving.append(copy)
    for copy in leaving:
        copy.wait()


def widened(ga, gb, gn, y, dx):
    grads = [(D, FF), (D, FF), (FF, D), (192, D), (192, D), (HD, D), (HD, D)]
    shapes = [jax.ShapeDtypeStruct(shape, F32) for shape in grads + [(1, D), (1, D)]]
    shapes += [jax.ShapeDtypeStruct((1, 2, OWN, D), BF16), jax.ShapeDtypeStruct((1, 2, OWN, D), F32)]
    hbm = pl.BlockSpec(memory_space=pl.ANY)
    vmem = pl.BlockSpec(memory_space=pltpu.VMEM)
    dma = pltpu.SemaphoreType.DMA
    return pl.pallas_call(
        widen,
        out_shape=tuple(shapes),
        in_specs=[hbm, hbm, vmem, vmem, vmem],
        out_specs=tuple([hbm] * 7 + [vmem] * 4),
        scratch_shapes=[pltpu.VMEM((2, 4, 576, 512), BF16), pltpu.VMEM((2, 4, 288, 384), BF16)]
        + [pltpu.VMEM(shape, F32) for shape in grads]
        + [dma((2, 4)), dma((4,)), dma((28,))],
        compiler_params=pltpu.CompilerParams(vmem_limit_bytes=63 * 1024 * 1024),
        name="widen",
    )(ga, gb, gn, y, dx)


def on_device(inputs, cotangent, doc_lengths, norm_one, query_w, key_w, value_w, out_w, norm_two, gate_w, up_w, down_w):
    lane = np.arange(128) % HALF
    speed = jnp.asarray(np.exp(lane * (-2.0 * math.log(ROPE) / HD)).astype(np.float32)[None, :])
    y, dx, ga, gb, gn = step_call(
        inputs, cotangent, query_w[0].T, key_w[0].T, value_w[0].T, out_w[0], gate_w[0], up_w[0], down_w[0], norm_one, norm_two,
        doc_lengths, speed,
    )
    gate, up, down, out, query, key, value, one, two, y, dx = widened(ga, gb, gn, y, dx)
    return (y, dx, one, query.T[None], key.T[None], value.T[None], out[None], two, gate[None], up[None], down[None])


def solution(mesh):
    in_specs = (
        P(None, "dp", None),
        P(None, "dp", None),
        P(),
        P("section", None),
        P("section", None, "tensor"),
        P("section", None, "tensor"),
        P("section", None, "tensor"),
        P("section", "tensor", None),
        P("section", None),
        P("section", None, "tensor"),
        P("section", None, "tensor"),
        P("section", "tensor", None),
    )
    out_specs = (
        P("section", None, ("dp", "tensor"), None),
        P("section", None, ("dp", "tensor"), None),
        P("section", None),
        P("section", None, "tensor"),
        P("section", None, "tensor"),
        P("section", None, "tensor"),
        P("section", "tensor", None),
        P("section", None),
        P("section", None, "tensor"),
        P("section", None, "tensor"),
        P("section", "tensor", None),
    )
    return jax.shard_map(on_device, mesh=mesh, in_specs=in_specs, out_specs=out_specs, check_vma=False)
```

```python
import math

import jax
import jax.numpy as jnp
import numpy as np
from jax import lax
from jax.experimental import pallas as pl
from jax.experimental.pallas import tpu as pltpu
from jax.sharding import PartitionSpec as P

MESH = pl.DeviceIdType.MESH
F32 = jnp.float32
BF16 = jnp.bfloat16

HD = 96
HALF = HD // 2
D = 1536
FF = 512
ROWS = 256
OWN = 32
HROWS = 128
HOWN = 16
SCALE = 1.0 / math.sqrt(HD)
EPS = 1e-05
ROPE = 100000.0
MASKED = -1e30


def dot(a, b):
    return lax.dot_general(a, b, (((1,), (0,)), ((), ())), preferred_element_type=F32)


def dot_nt(a, b):
    return lax.dot_general(a, b, (((1,), (1,)), ((), ())), preferred_element_type=F32)


def dot_tn(a, b):
    return lax.dot_general(a, b, (((0,), (0,)), ((), ())), preferred_element_type=F32)


def lanes_of(v):
    return lax.broadcasted_iota(jnp.int32, v.shape, 1)


def swapped(v):
    return jnp.where(lanes_of(v) < HALF, pltpu.roll(v, 128 - HALF, 1), pltpu.roll(v, HALF, 1))


def place_of(i):
    return OWN * ((i // HOWN) % 8) + HOWN * (i // HROWS) + i % HOWN


def factor_of(v):
    return lax.rsqrt(jnp.mean(v * v, axis=-1, keepdims=True) + EPS)


def kernel(
    x_hbm, ct_hbm, wq_hbm, wk_hbm, wv_hbm, wo_hbm, wg_hbm, wu_hbm, wd_hbm, one_ref, two_ref, lengths_ref, speed_ref,
    y_out, dx_out, ga_out, gb_out, gn_out,
    wqkv, wo, wgu, wd, gains, gains_own, gains_in, cos_ref, sin_ref, beg_ref, df,
    n1, n2, q2, q2t, kv, o_f, o_b, stat_m, stat_l, gate_s, up_s, u_s, x_own, h_own,
    rsrc, land, da, do2, do2t, dgu, dq, dqkv, dkv_t, dkv_src, dkv_land, acc, s_m,
    ga, gb, da_in, db_in, za, zb, xa, xb, fa, fb, yb, dxb, dgain, dg_peer, dg_t, dg_d,
    w_l, w_s, w_r, ag_s, ag_r, rs_s, rs_r, kv_s, kv_r, dkv_s, dkv_r, out_l, out_s, out_r,
    ds_s, ds_r, z_s, z_r, x_s, x_r, a_s, a_r, a_l, f_s, f_r, ns, nr,
):
    sec = lax.axis_index("section")
    t = lax.axis_index("tensor")
    d = lax.axis_index("dp")
    other = 1 - sec
    z, xh = d // 2, d % 2

    barrier = pltpu.get_barrier_semaphore()

    def greet(axis, me, k, _):
        pl.semaphore_signal(barrier, inc=1, device_id={axis: (me + k) % 8}, device_id_type=MESH)
        return _

    pl.semaphore_signal(barrier, inc=1, device_id={"section": other}, device_id_type=MESH)
    lax.fori_loop(1, 8, lambda k, c: greet("tensor", t, k, c), 0)
    lax.fori_loop(1, 8, lambda k, c: greet("dp", d, k, c), 0)

    def load_rows(source, sem):
        def body(i, c):
            h, p = i // 8, i % 8
            pltpu.make_async_copy(
                source.at[sec, pl.ds(pl.multiple_of(p * OWN + h * HOWN, HOWN), HOWN)],
                df.at[pl.ds(pl.multiple_of(h * HROWS + p * HOWN, HOWN), HOWN)], sem,
            ).start()
            return c

        lax.fori_loop(0, 16, body, 0)

    def rows_loaded(source, sem):
        pltpu.make_async_copy(source.at[sec], df, sem).wait()

    own_parts = [
        (wq_hbm, lambda i: wqkv.at[i, pl.ds(0, 2 * HD)]),
        (wk_hbm, lambda i: wqkv.at[i, pl.ds(2 * HD, HD)]),
        (wv_hbm, lambda i: wqkv.at[i, pl.ds(3 * HD, HD)]),
        (wo_hbm, lambda i: wo.at[i]),
        (wg_hbm, lambda i: wgu.at[i, :, 0:FF]),
        (wu_hbm, lambda i: wgu.at[i, :, FF : 2 * FF]),
        (wd_hbm, lambda i: wd.at[i]),
    ]
    n_parts = len(own_parts)
    own_copies = [pltpu.make_async_copy(a, b(sec), w_l.at[i]) for i, (a, b) in enumerate(own_parts)]
    load_rows(x_hbm, w_l.at[8])
    for i in range(n_parts):
        own_copies[i].start()
    gains_own[0:8, :] = jnp.broadcast_to(one_ref[...].astype(F32), (8, D))
    gains_own[8:16, :] = jnp.broadcast_to(two_ref[...].astype(F32), (8, D))
    gains[sec] = gains_own[...]

    places = place_of(lax.broadcasted_iota(jnp.int32, (ROWS, 128), 0)) + d * ROWS

    lengths = jnp.where(sec == 0, lengths_ref[0:1, :], lengths_ref[1:2, :])
    start, begins = jnp.zeros((1, 1), jnp.int32), jnp.zeros((ROWS, 128), jnp.int32)
    for n in range(lengths.shape[1]):
        begins = jnp.maximum(begins, jnp.where(start <= places, start, 0))
        start = start + lengths[:, n : n + 1]
    beg_ref[...] = begins
    angles = (places - begins).astype(F32) * speed_ref[0:1, :]
    lane = lanes_of(angles)
    cos_ref[...] = jnp.where(lane < HD, jnp.cos(angles), 0.0)
    sine = jnp.sin(angles)
    sin_ref[...] = jnp.where(lane < HALF, -sine, jnp.where(lane < HD, sine, 0.0))
    pl.semaphore_wait(barrier, 15)
    sent_parts = [
        pltpu.make_async_remote_copy(
            src_ref=a, dst_ref=b(sec), send_sem=w_s.at[i], recv_sem=w_r.at[i],
            device_id={"section": other}, device_id_type=MESH,
        )
        for i, (a, b) in enumerate(own_parts)
    ]
    gains_sent = pltpu.make_async_remote_copy(
        src_ref=gains_own, dst_ref=gains_in, send_sem=w_s.at[n_parts], recv_sem=w_r.at[n_parts],
        device_id={"section": other}, device_id_type=MESH,
    )
    gains_sent.start()
    for i in range(n_parts):
        sent_parts[i].start()

    def gains_arrived():
        pltpu.make_async_remote_copy(
            src_ref=gains_own, dst_ref=gains_in, send_sem=w_s.at[n_parts], recv_sem=w_r.at[n_parts],
            device_id={"section": other}, device_id_type=MESH,
        ).wait_recv()
        gains[other] = gains_in[...]

    def weight_ready(layer, *which):
        @pl.when(layer == sec)
        def _():
            for i in which:
                own_copies[i].wait()

        @pl.when(layer != sec)
        def _():
            for i in which:
                a, b = own_parts[i]
                pltpu.make_async_remote_copy(
                    src_ref=a, dst_ref=b(other), send_sem=w_s.at[i], recv_sem=w_r.at[i],
                    device_id={"section": other}, device_id_type=MESH,
                ).wait_recv()

    def half_rows(half):
        return pl.ds(pl.multiple_of(half * HROWS, HROWS), HROWS)

    def pair_rows(half):
        return pl.ds(pl.multiple_of(half * ROWS, ROWS), ROWS)

    def rows_of(half, owner):
        return pl.ds(pl.multiple_of(half * HROWS + owner * HOWN, HOWN), HOWN)

    def kept(half):
        return pl.ds(pl.multiple_of(half * HOWN, HOWN), HOWN)

    def over_peers(body):
        def step(k, c):
            body((t + k) % 8)
            return c

        lax.fori_loop(1, 8, step, 0)

    def ag_copy(buf, i, half, to, owner):
        rows = rows_of(half, owner)
        return pltpu.make_async_remote_copy(
            src_ref=buf.at[rows], dst_ref=buf.at[rows], send_sem=ag_s.at[i, half, to], recv_sem=ag_r.at[i, half, owner],
            device_id={"tensor": to}, device_id_type=MESH,
        )

    def ag_start(buf, i, half):
        over_peers(lambda p: ag_copy(buf, i, half, p, t).start())

    def ag_wait(buf, i, half):
        over_peers(lambda p: ag_copy(buf, i, half, t, p).wait_recv())

    def ag_sent(buf, i, half):
        over_peers(lambda p: ag_copy(buf, i, half, p, t).wait_send())

    def rs_copy(i, half, to, sender):
        return pltpu.make_async_remote_copy(
            src_ref=rsrc.at[i, rows_of(half, to)], dst_ref=land.at[i, half, sender], send_sem=rs_s.at[i, half, to],
            recv_sem=rs_r.at[i, half, sender], device_id={"tensor": to}, device_id_type=MESH,
        )

    def rs_start(i, half):
        over_peers(lambda p: rs_copy(i, half, p, t).start())

    def rs_sum(i, half):
        def body(k, total):
            p = (t + k) % 8
            rs_copy(i, half, t, p).wait_recv()
            return total + land[i, half, p].astype(F32)

        return lax.fori_loop(1, 8, body, rsrc[i, rows_of(half, t), :].astype(F32))

    def rs_sent(i, half):
        over_peers(lambda p: rs_copy(i, half, p, t).wait_send())

    def both(body):
        def step(half, c):
            body(half)
            return c

        lax.fori_loop(0, 2, step, 0)

    def allowed_of(j, half):
        rows = place_of(lax.broadcasted_iota(jnp.int32, (HROWS, 1), 0) + half * HROWS) + d * ROWS
        cols = place_of(lax.broadcasted_iota(jnp.int32, (1, ROWS), 1)) + j * ROWS
        allowed = (cols <= rows) & (cols >= beg_ref[half_rows(half), 0:1])
        return jnp.concatenate([jnp.where(allowed, 0.0, MASKED)] * 2, axis=0)

    pl.when(sec == 1)(gains_arrived)
    rows_loaded(x_hbm, w_l.at[8])

    def first_norm(i, c):
        rows = pl.ds(pl.multiple_of(i * OWN, OWN), OWN)
        v = df[rows, :].astype(F32)
        n1[0, rows, :] = (v * factor_of(v) * gains[0, 0:1, :]).astype(BF16)
        return c

    lax.fori_loop(0, ROWS // OWN, first_norm, 0)
    for half in range(2):
        x_own[0, kept(half), :] = df[rows_of(half, t), :].astype(F32)
    load_rows(ct_hbm, w_l.at[9])

    def forward_layer(layer, c):
        weight_ready(layer, 0, 1, 2)

        def kv_copy(owner, to, half):
            part = kv.at[layer, owner, :, half_rows(half)]
            return pltpu.make_async_remote_copy(
                src_ref=part, dst_ref=part, send_sem=kv_s.at[to, half], recv_sem=kv_r.at[owner, layer, half],
                device_id={"dp": to}, device_id_type=MESH,
            )

        def project(half):
            rows = half_rows(half)

            @pl.when(layer == 1)
            def _():
                ag_wait(n1.at[1], 0, half)

            raw = dot_nt(n1[layer, rows, :], wqkv[layer])
            c0, c1, c2 = raw[:, 0:128], raw[:, 128:256], raw[:, 256:384]
            lane = lanes_of(c0)
            q1 = jnp.where(lane < 32, pltpu.roll(c0, 32, 1), pltpu.roll(c1, 32, 1))
            k0 = jnp.where(lane < 64, pltpu.roll(c1, 64, 1), pltpu.roll(c2, 64, 1))
            v0 = pltpu.roll(c2, 96, 1)
            cosine, sine = cos_ref[rows, :], sin_ref[rows, :]
            turned = k0 * cosine + swapped(k0) * sine
            kv[layer, d, pl.ds(0, HD), rows] = jnp.transpose(turned)[0:HD, :].astype(BF16)
            kv[layer, d, pl.ds(HD, HD), rows] = jnp.transpose(v0)[0:HD, :].astype(BF16)

            def kv_send(k, c):
                kv_copy(d, 8 + d - k, half).start()
                return c

            lax.fori_loop(d + 1, 8, kv_send, 0)
            for h, part in ((0, c0), (1, q1)):
                turned = part * cosine + swapped(part) * sine
                place = pl.ds(pl.multiple_of(half * ROWS + h * HROWS, HROWS), HROWS)
                q2[layer, place, :] = turned[:, 0:HD].astype(BF16)
                q2t[layer, :, place] = jnp.transpose(turned)[0:HD, :].astype(BF16)

        both(project)

        @pl.when(layer == 1)
        def _():
            both(lambda half: ag_sent(n1.at[1], 0, half))

        weight_ready(layer, 3)

        def attend_half(half):
            rows = pair_rows(half)
            s_m[rows, :] = jnp.full((ROWS, 1), MASKED, F32)
            stat_l[layer, rows, :] = jnp.zeros((ROWS, 1), F32)
            acc[rows, :] = jnp.zeros((ROWS, HD), F32)

            def attend(i, c):
                j = d - i

                @pl.when((i > 0) & (half == 0))
                def _():
                    kv_copy(j, d, 0).wait_recv()
                    kv_copy(j, d, 1).wait_recv()

                s = dot(q2[layer, rows, :], kv[layer, j, pl.ds(0, HD), :]) * SCALE + allowed_of(j, half)
                old = s_m[rows, :]
                new = jnp.maximum(old, jnp.max(s, axis=-1, keepdims=True))
                p = jnp.exp(s - new)
                shrink = jnp.exp(old - new)
                s_m[rows, :] = new
                stat_l[layer, rows, :] = stat_l[layer, rows, :] * shrink + jnp.sum(p, axis=-1, keepdims=True)
                acc[rows, :] = acc[rows, :] * shrink + dot_nt(p.astype(BF16), kv[layer, j, pl.ds(HD, HD), :])
                return c

            lax.fori_loop(0, d + 1, attend, 0)
            total = stat_l[layer, rows, :]
            mixed = acc[rows, :] / total
            o_f[layer, rows, :] = mixed
            o_b[layer, rows, :] = mixed.astype(BF16)
            stat_m[layer, rows, :] = s_m[rows, :] + jnp.log(total)
            first = pl.ds(pl.multiple_of(half * ROWS, HROWS), HROWS)
            second = pl.ds(pl.multiple_of(half * ROWS + HROWS, HROWS), HROWS)

            def out_part(n, c):
                cols = pl.ds(pl.multiple_of(n * 512, 512), 512)
                part = dot(o_b[layer, first, :], wo[layer, pl.ds(0, HD), cols])
                part += dot(o_b[layer, second, :], wo[layer, pl.ds(HD, HD), cols])
                rsrc[0, half_rows(half), cols] = part.astype(BF16)
                return c

            lax.fori_loop(0, 3, out_part, 0)
            rs_start(0, half)

        both(attend_half)

        def middle(half):
            v = x_own[layer, kept(half), :] + rs_sum(0, half)
            h_own[layer, kept(half), :] = v
            n2[layer, rows_of(half, t), :] = (v * factor_of(v) * gains[layer, 8:9, :]).astype(BF16)
            ag_start(n2.at[layer], 1, half)
            rs_sent(0, half)

        both(middle)
        weight_ready(layer, 4, 5)
        weight_ready(layer, 6)

        def feed(half):
            rows = half_rows(half)
            ag_wait(n2.at[layer], 1, half)

            def units(n, c):
                cols = pl.ds(pl.multiple_of(n * 256, 256), 256)
                above = pl.ds(pl.multiple_of(n * 256 + FF, 256), 256)
                g = dot(n2[layer, rows, :], wgu[layer, :, cols])
                up = dot(n2[layer, rows, :], wgu[layer, :, above])
                gate_s[layer, rows, cols] = g
                up_s[layer, rows, cols] = up
                u_s[layer, rows, cols] = (g * jax.nn.sigmoid(g) * up).astype(BF16)
                return c

            lax.fori_loop(0, 2, units, 0)

            def down_part(n, c):
                cols = pl.ds(pl.multiple_of(n * 512, 512), 512)
                rsrc[1, rows, cols] = dot(u_s[layer, rows, :], wd[layer, :, cols]).astype(BF16)
                return c

            lax.fori_loop(0, 3, down_part, 0)
            rs_start(1, half)
            ag_sent(n2.at[layer], 1, half)

        both(feed)

        pl.when((layer == 0) & (sec == 0))(gains_arrived)

        def result(half):
            y = (h_own[layer, kept(half), :] + rs_sum(1, half)).astype(BF16)
            yb[layer, kept(half), :] = y

            @pl.when(layer == 0)
            def _():
                v = y.astype(F32)
                x_own[1, kept(half), :] = v
                n1[1, rows_of(half, t), :] = (v * factor_of(v) * gains[1, 0:1, :]).astype(BF16)
                ag_start(n1.at[1], 0, half)

            rs_sent(1, half)

        both(result)

        def kv_sent(k, c):
            kv_copy(d, k, 0).wait_send()
            kv_copy(d, k, 1).wait_send()
            return c

        lax.fori_loop(d + 1, 8, kv_sent, 0)
        row_out(layer, yb, y_out, 0)
        return c

    def row_out(layer, buf, out, i):
        @pl.when(layer == sec)
        def _():
            pltpu.make_async_copy(buf.at[layer], out.at[sec], out_l.at[i]).start()

        @pl.when(layer != sec)
        def _():
            pltpu.make_async_remote_copy(
                src_ref=buf.at[layer], dst_ref=out.at[sec], send_sem=out_s.at[i], recv_sem=out_r.at[i],
                device_id={"section": other}, device_id_type=MESH,
            ).start()

    def row_out_wait(buf, out, i):
        pltpu.make_async_copy(buf.at[sec], out.at[sec], out_l.at[i]).wait()
        copy = pltpu.make_async_remote_copy(
            src_ref=buf.at[other], dst_ref=out.at[other], send_sem=out_s.at[i], recv_sem=out_r.at[i],
            device_id={"section": other}, device_id_type=MESH,
        )
        copy.wait_send()
        copy.wait_recv()

    lax.fori_loop(0, 2, forward_layer, 0)

    rows_loaded(ct_hbm, w_l.at[9])

    sets = ((ga, da_in, za, xa, fa, ga_out), (gb, db_in, zb, xb, fb, gb_out))
    before, after = (z + 3) % 4, (z + 1) % 4
    far = (z + 2) % 4

    def dp_at(zz, xx):
        return zz * 2 + xx

    def quarter(i, which):
        size = (288, 144)[i]
        return pl.ds(pl.multiple_of(which * size, 16), size)

    def swap_cores(layer, i, chunk):
        return pltpu.make_async_remote_copy(
            src_ref=sets[i][0].at[layer, other, chunk], dst_ref=sets[i][1].at[layer, chunk], send_sem=ds_s.at[i, layer, chunk],
            recv_sem=ds_r.at[i, layer, chunk], device_id={"section": other}, device_id_type=MESH,
        )

    def chunk_at(n):
        return (z + jnp.where(n == 0, 2, jnp.where(n == 3, 0, 2 * n - 1))) % 4

    def add_rows(target, index, first, size, sources):
        count = 96 if size % 96 == 0 else 48

        def add(n, carry):
            here = pl.ds(pl.multiple_of(first + n * count, 16), count)
            total = target[(*index, here)].astype(F32)
            for ref, place, start in sources:
                total += ref[(*place, pl.ds(pl.multiple_of(start + n * count, 16), count))].astype(F32)
            target[(*index, here)] = total.astype(BF16)
            return carry

        lax.fori_loop(0, size // count, add, 0)

    def z_piece(layer, i, piece, chunk, which, to):
        return pltpu.make_async_remote_copy(
            src_ref=sets[i][0].at[layer, sec, chunk, quarter(i, which)], dst_ref=sets[i][2].at[layer, piece],
            send_sem=z_s.at[i, layer, piece], recv_sem=z_r.at[i, layer, piece], device_id={"dp": dp_at(to, xh)},
            device_id_type=MESH,
        )

    def sum_1(layer, i):
        g, arrived = sets[i][0:2]
        for chunk, sends in (
            (far, ((0, 0, after), (1, 1, before))),
            (after, ((2, 1, after),)),
            (before, ((3, 0, before),)),
            (z, ()),
        ):
            swap_cores(layer, i, chunk).wait_recv()
            add_rows(g, (layer, sec, chunk), 0, g.shape[3], [(arrived, (layer, chunk), 0)])
            for piece, which, to in sends:
                z_piece(layer, i, piece, chunk, which, to).start()

    def sum_2(layer, i):
        g, landed = sets[i][0], sets[i][2]
        size = landed.shape[2]
        z_piece(layer, i, 0, far, 0, after).wait_recv()
        add_rows(g, (layer, sec, after), 0, size, [(landed, (layer, 0), 0)])
        z_piece(layer, i, 4, after, 0, after).start()
        z_piece(layer, i, 1, far, 1, before).wait_recv()
        add_rows(g, (layer, sec, before), size, size, [(landed, (layer, 1), 0)])
        z_piece(layer, i, 5, before, 1, before).start()

    def x_over(layer, i):
        return pltpu.make_async_remote_copy(
            src_ref=sets[i][0].at[layer, sec, z, quarter(i, 1 - xh)], dst_ref=sets[i][3].at[layer],
            send_sem=x_s.at[i, 0, layer], recv_sem=x_r.at[i, 0, layer], device_id={"dp": dp_at(z, 1 - xh)},
            device_id_type=MESH,
        )

    def x_back(layer, i, which):
        part = sets[i][4].at[layer, quarter(i, which)]
        return pltpu.make_async_remote_copy(
            src_ref=part, dst_ref=part, send_sem=x_s.at[i, 1, layer], recv_sem=x_r.at[i, 1, layer],
            device_id={"dp": dp_at(z, 1 - xh)}, device_id_type=MESH,
        )

    def sum_3(layer, i):
        g, landed = sets[i][0], sets[i][2]
        size = landed.shape[2]
        for piece in (2, 3, 4, 5):
            z_piece(layer, i, piece, z, 0, after).wait_recv()
        add_rows(g, (layer, sec, z), 0, size, [(landed, (layer, 3), 0), (landed, (layer, 4), 0)])
        add_rows(g, (layer, sec, z), size, size, [(landed, (layer, 2), 0), (landed, (layer, 5), 0)])
        x_over(layer, i).start()

    def spread(layer, i, half, chunk, which, to, k):
        rows = quarter(i, which)
        return pltpu.make_async_remote_copy(
            src_ref=sets[i][4].at[layer, rows], dst_ref=sets[i][5].at[half, chunk, rows], send_sem=a_s.at[i, layer, which, k],
            recv_sem=a_r.at[i, half, chunk, which], device_id={"section": layer, "dp": dp_at(to, xh)}, device_id_type=MESH,
        )

    def keep(layer, i, which):
        rows = quarter(i, which)
        return pltpu.make_async_copy(sets[i][4].at[layer, rows], sets[i][5].at[sec, z, rows], a_l.at[i, which])

    def spread_all(layer, i, which):
        spread(layer, i, sec, z, which, after, 0).start()
        spread(layer, i, sec, z, which, before, 1).start()

        @pl.when(layer == sec)
        def _():
            keep(layer, i, which).start()

        @pl.when(layer != sec)
        def _():
            spread(layer, i, sec, z, which, z, 2).start()

    def sum_4(layer, i):
        g, over, done = sets[i][0], sets[i][3], sets[i][4]
        size = over.shape[1]
        x_over(layer, i).wait_recv()

        def add(n, carry):
            here = pl.ds(pl.multiple_of(n * 48, 16), 48)
            there = pl.ds(pl.multiple_of(xh * size + n * 48, 16), 48)
            done[layer, there, :] = (g[layer, sec, z, there, :].astype(F32) + over[layer, here, :].astype(F32)).astype(BF16)
            return carry

        lax.fori_loop(0, size // 48, add, 0)
        x_back(layer, i, xh).start()
        spread_all(layer, i, xh)

    def sum_5(layer, i):
        x_back(layer, i, 1 - xh).wait_recv()
        spread_all(layer, i, 1 - xh)

    def pass_on(i, half, chunk, which, to):
        part = sets[i][5].at[half, chunk, quarter(i, which)]
        return pltpu.make_async_remote_copy(
            src_ref=part, dst_ref=part, send_sem=f_s.at[i, half, which], recv_sem=f_r.at[i, half, which],
            device_id={"dp": dp_at(to, xh)}, device_id_type=MESH,
        )

    def sum_6(i):
        for half in range(2):
            spread(sec, i, half, before, 0, z, 0).wait_recv()
            pass_on(i, half, before, 0, after).start()
            spread(sec, i, half, after, 1, z, 0).wait_recv()
            pass_on(i, half, after, 1, before).start()

    def sum_7(i):
        for which in range(2):
            keep(sec, i, which).wait()
            spread(sec, i, other, z, which, z, 2).wait_recv()
            spread(other, i, sec, z, which, z, 2).wait_send()
            for half in range(2):
                spread(sec, i, half, (after, before)[which], which, z, 0).wait_recv()
                pass_on(i, half, far, which, z).wait_recv()
                pass_on(i, half, z, which, after).wait_send()
        for layer in range(2):
            for chunk in range(4):
                swap_cores(layer, i, chunk).wait_send()
            for piece in range(6):
                z_piece(layer, i, piece, z, 0, after).wait_send()
            x_over(layer, i).wait_send()
            x_back(layer, i, xh).wait_send()
            for which in range(2):
                spread(layer, i, sec, z, which, after, 0).wait_send()
                spread(layer, i, sec, z, which, before, 1).wait_send()

    def backward_layer(step, c):
        layer = 1 - step


        @pl.when(step == 1)
        def _():
            sum_4(1, 0)
            sum_2(1, 1)

        def feed_back(half):
            rows = half_rows(half)

            @pl.when(step == 1)
            def _():
                ag_wait(df, 2, half)

            dxb[layer, kept(half), :] = df[rows_of(half, t), :].astype(F32)

            def unit_grads(n, c):
                cols = pl.ds(pl.multiple_of(n * 256, 256), 256)
                above = pl.ds(pl.multiple_of(n * 256 + FF, 256), 256)
                du = dot_nt(df[rows, :], wd[layer, cols, :])
                g, up = gate_s[layer, rows, cols], up_s[layer, rows, cols]
                sig = jax.nn.sigmoid(g)
                dgu[rows, cols] = (du * up * sig * (1.0 + g * (1.0 - sig))).astype(BF16)
                dgu[rows, above] = (du * g * sig).astype(BF16)
                return c

            lax.fori_loop(0, 2, unit_grads, 0)

            def normed_part(n, c):
                cols = pl.ds(pl.multiple_of(n * 256, 256), 256)
                rsrc[0, rows, cols] = dot_nt(dgu[rows, :], wgu[layer, cols, :]).astype(BF16)
                return c

            lax.fori_loop(0, 6, normed_part, 0)
            rs_start(0, half)

        both(feed_back)

        @pl.when(step == 1)
        def _():
            both(lambda half: ag_sent(df, 2, half))

        def unit_weights(k, c):
            n = chunk_at(k)
            cols = pl.ds(pl.multiple_of(n * 384, 384), 384)
            got = dot_tn(n2[layer, :, cols], dgu[...]).astype(BF16)
            for h in range(2):
                ga[layer, h, n, pl.ds(0, 192), :] = got[192 * h : 192 * h + 192, 0:FF]
                ga[layer, h, n, pl.ds(192, 192), :] = got[192 * h : 192 * h + 192, FF : 2 * FF]
            cols = pl.ds(pl.multiple_of(n * 128, 128), 128)
            got = dot_tn(u_s[layer, :, cols], df[...]).astype(BF16)
            for h in range(2):
                for i in range(3):
                    ga[layer, h, n, pl.ds(384 + 64 * i, 64), :] = got[64 * h : 64 * h + 64, 512 * i : 512 * i + 512]
            swap_cores(layer, 0, n).start()
            return c

        lax.fori_loop(0, 4, unit_weights, 0)
        sum_1(layer, 0)

        @pl.when(step == 1)
        def _():
            sum_5(1, 0)


        def hidden_grads(half):
            dn = rs_sum(0, half)
            h = h_own[layer, kept(half), :]
            r = factor_of(h)
            tt = dn * gains[layer, 8:9, :]
            dh = dxb[layer, kept(half), :] + r * tt - h * (r * r * r * jnp.mean(h * tt, axis=-1, keepdims=True))
            dgain[layer, 1:2, :] += jnp.sum(dn * h * r, axis=0, keepdims=True)
            dxb[layer, kept(half), :] = dh
            da[rows_of(half, t), :] = dh.astype(BF16)
            ag_start(da, 3, half)
            rs_sent(0, half)

        both(hidden_grads)

        @pl.when(step == 0)
        def _():
            sum_2(1, 0)


        @pl.when(step == 1)
        def _():
            sum_3(1, 1)


        def mixed_grads(half):
            ag_wait(da, 3, half)
            for h in range(2):
                place = pl.ds(pl.multiple_of(half * ROWS + h * HROWS, HROWS), HROWS)
                got = dot_nt(da[half_rows(half), :], wo[layer, pl.ds(h * HD, HD), :])
                do2[place, :] = got.astype(BF16)
                padded = jnp.concatenate([got, jnp.zeros((HROWS, 128 - HD), F32)], axis=1)
                do2t[:, place] = jnp.transpose(padded)[0:HD, :].astype(BF16)

        both(mixed_grads)
        both(lambda half: ag_sent(da, 3, half))
        dot_rows = jnp.sum(do2[...].astype(F32) * o_f[layer], axis=-1, keepdims=True)
        s_m[...] = dot_rows
        acc[...] = jnp.zeros(acc.shape, F32)

        def dkv_copy(to, sender):
            return pltpu.make_async_remote_copy(
                src_ref=dkv_src.at[to], dst_ref=dkv_land.at[layer, sender], send_sem=dkv_s.at[to], recv_sem=dkv_r.at[layer, sender],
                device_id={"dp": to}, device_id_type=MESH,
            )

        def attend_back(j, c):
            dkt = jnp.zeros((HD, ROWS), F32)
            dvt = jnp.zeros((HD, ROWS), F32)
            for half in range(2):
                rows = pair_rows(half)
                kt = kv[layer, j, pl.ds(0, HD), :]
                s = dot(q2[layer, rows, :], kt) * SCALE + allowed_of(j, half)
                p = jnp.exp(s - stat_m[layer, rows, :])
                dp = dot(do2[rows, :], kv[layer, j, pl.ds(HD, HD), :])
                ds = (p * (dp - s_m[rows, :])).astype(BF16)
                acc[rows, :] += dot_nt(ds, kt)
                dkt += dot(q2t[layer, :, rows], ds)
                dvt += dot(do2t[:, rows], p.astype(BF16))
            dkv_src[j, pl.ds(0, HD), :] = (dkt * SCALE).astype(BF16)
            dkv_src[j, pl.ds(HD, HD), :] = dvt.astype(BF16)

            @pl.when(j < d)
            def _():
                dkv_copy(j, d).start()

            return c

        lax.fori_loop(0, d + 1, attend_back, 0)


        @pl.when(step == 1)
        def _():
            sum_2(0, 0)

        def out_weights(n, c):
            cols = pl.ds(pl.multiple_of(n * 384, 384), 384)
            for h in range(2):
                mixed = [o_b[layer, pl.ds(half * ROWS + h * HROWS, HROWS), :] for half in range(2)]
                got = dot_tn(jnp.concatenate(mixed, axis=0), da[:, cols])
                gb[layer, 0, n, pl.ds(h * HD, HD), :] = got.astype(BF16)
            return c

        lax.fori_loop(0, 4, out_weights, 0)


        @pl.when(step == 0)
        def _():
            sum_3(1, 0)


        @pl.when(step == 1)
        def _():
            sum_4(1, 1)


        @pl.when((step == 1) & (sec == 1))
        def _():
            sum_6(0)

        def dkv_sum(k, total):
            dkv_copy(d, k).wait_recv()
            return total + dkv_land[layer, k].astype(F32)

        dkv_total = lax.fori_loop(d + 1, 8, dkv_sum, dkv_src[d].astype(F32))
        dkv_t[...] = jnp.zeros(dkv_t.shape, F32)
        dkv_t[0, pl.ds(0, HD), :] = dkv_total[0:HD]
        dkv_t[1, pl.ds(0, HD), :] = dkv_total[HD : 2 * HD]
        dk_rot = jnp.transpose(dkv_t[0])
        dv = jnp.transpose(dkv_t[1])
        cosine, sine = cos_ref[...], sin_ref[...]
        dq[...] = jnp.zeros(dq.shape, F32)
        dq[:, 0:HD] = acc[...] * SCALE
        dq0, dq1 = (
            jnp.concatenate([dq[pl.ds(half * ROWS + h * HROWS, HROWS), :] for half in range(2)], axis=0) for h in range(2)
        )
        dq0 = dq0 * cosine - swapped(dq0) * sine
        dq1 = dq1 * cosine - swapped(dq1) * sine
        dk = dk_rot * cosine - swapped(dk_rot) * sine
        lane = lanes_of(dk)
        dqkv[:, 0:128] = jnp.where(lane < HD, dq0, pltpu.roll(dq1, 96, 1)).astype(BF16)
        dqkv[:, 128:256] = jnp.where(lane < 64, pltpu.roll(dq1, 96, 1), pltpu.roll(dk, 64, 1)).astype(BF16)
        dqkv[:, 256:384] = jnp.where(lane < 32, pltpu.roll(dk, 64, 1), pltpu.roll(dv, 32, 1)).astype(BF16)

        def project_back(half):
            rows = half_rows(half)

            def input_part(n, c):
                cols = pl.ds(pl.multiple_of(n * 512, 512), 512)
                rsrc[1, rows, cols] = dot(dqkv[rows, :], wqkv[layer, :, cols]).astype(BF16)
                return c

            lax.fori_loop(0, 3, input_part, 0)
            rs_start(1, half)

        both(project_back)

        def qkv_weights(k, c):
            n = chunk_at(k)
            cols = pl.ds(pl.multiple_of(n * 384, 384), 384)
            got = dot_tn(dqkv[...], n1[layer, :, cols]).astype(BF16)
            gb[layer, 0, n, pl.ds(2 * HD, HD), :] = got[0:HD]
            gb[layer, 1, n] = got[HD : 4 * HD]
            swap_cores(layer, 1, n).start()
            return c

        lax.fori_loop(0, 4, qkv_weights, 0)

        @pl.when(step == 1)
        def _():
            sum_3(0, 0)


        @pl.when(step == 0)
        def _():
            sum_1(1, 1)


        @pl.when(step == 1)
        def _():
            sum_5(1, 1)

        def input_grads(half):
            dn = rs_sum(1, half)
            v = x_own[layer, kept(half), :]
            r = factor_of(v)
            tt = dn * gains[layer, 0:1, :]
            dx = dxb[layer, kept(half), :] + r * tt - v * (r * r * r * jnp.mean(v * tt, axis=-1, keepdims=True))
            dgain[layer, 0:1, :] += jnp.sum(dn * v * r, axis=0, keepdims=True)
            dxb[layer, kept(half), :] = dx

            @pl.when(step == 0)
            def _():
                df[rows_of(half, t), :] = dx.astype(BF16)
                ag_start(df, 2, half)

            rs_sent(1, half)

        both(input_grads)

        def dkv_sent(k, c):
            dkv_copy(k, d).wait_send()
            return c

        lax.fori_loop(0, d, dkv_sent, 0)
        row_out(layer, dxb, dx_out, 1)
        return c

    dgain[...] = jnp.zeros(dgain.shape, F32)
    lax.fori_loop(0, 2, backward_layer, 0)

    mate = pltpu.make_async_remote_copy(
        src_ref=dgain.at[other], dst_ref=dg_peer, send_sem=ns.at[0, 0], recv_sem=nr.at[0, 0],
        device_id={"section": other}, device_id_type=MESH,
    )
    mate.start()
    sum_1(0, 1)
    sum_4(0, 0)
    def gain_copy(axis, i, buf, me, to, sender):
        return pltpu.make_async_remote_copy(
            src_ref=buf.at[me], dst_ref=buf.at[sender], send_sem=ns.at[i, to], recv_sem=nr.at[i, sender],
            device_id={axis: to}, device_id_type=MESH,
        )

    def gain_send(axis, i, buf, me):
        def send(k, c):
            gain_copy(axis, i, buf, me, (me + k) % 8, me).start()
            return c

        lax.fori_loop(1, 8, send, 0)

    def gain_sum(axis, i, buf, me):
        def take(k, total):
            p = (me + k) % 8
            gain_copy(axis, i, buf, me, p, p).wait_recv()
            return total + buf[p]

        def sent(k, c):
            gain_copy(axis, i, buf, me, (me + k) % 8, me).wait_send()
            return c

        total = lax.fori_loop(1, 8, take, buf[me])
        lax.fori_loop(1, 8, sent, 0)
        return total

    mate.wait_recv()
    mate.wait_send()
    dg_t[t] = dgain[sec] + dg_peer[...]
    gain_send("tensor", 1, dg_t, t)

    @pl.when(sec == 1)
    def _():
        sum_6(1)

    sum_2(0, 1)
    sum_5(0, 0)
    dg_d[d] = gain_sum("tensor", 1, dg_t, t)
    gain_send("dp", 2, dg_d, d)
    sum_3(0, 1)

    @pl.when(sec == 0)
    def _():
        sum_6(0)

    sum_4(0, 1)
    sum_5(0, 1)

    @pl.when(sec == 0)
    def _():
        sum_6(1)

    gn_out[...] = gain_sum("dp", 2, dg_d, d)
    sum_7(0)
    sum_7(1)
    row_out_wait(yb, y_out, 0)
    row_out_wait(dxb, dx_out, 1)
    for i in range(n_parts):
        sent_parts[i].wait_send()
    gains_sent.wait_send()


def step_call(*args):
    hbm = pl.BlockSpec(memory_space=pl.ANY)
    vmem = pl.BlockSpec(memory_space=pltpu.VMEM)
    dma = pltpu.SemaphoreType.DMA
    scratch = [
        pltpu.VMEM((2, 384, D), BF16), pltpu.VMEM((2, 192, D), BF16), pltpu.VMEM((2, D, 2 * FF), BF16),
        pltpu.VMEM((2, FF, D), BF16), pltpu.VMEM((2, 16, D), F32), pltpu.VMEM((16, D), F32), pltpu.VMEM((16, D), F32), pltpu.VMEM((ROWS, 128), F32),
        pltpu.VMEM((ROWS, 128), F32), pltpu.VMEM((ROWS, 128), jnp.int32), pltpu.VMEM((ROWS, D), BF16),
        pltpu.VMEM((2, ROWS, D), BF16), pltpu.VMEM((2, ROWS, D), BF16), pltpu.VMEM((2, 2 * ROWS, HD), BF16),
        pltpu.VMEM((2, HD, 2 * ROWS), BF16), pltpu.VMEM((2, 8, 2 * HD, ROWS), BF16), pltpu.VMEM((2, 2 * ROWS, HD), F32),
        pltpu.VMEM((2, 2 * ROWS, HD), BF16), pltpu.VMEM((2, 2 * ROWS, 1), F32), pltpu.VMEM((2, 2 * ROWS, 1), F32),
        pltpu.VMEM((2, ROWS, FF), F32), pltpu.VMEM((2, ROWS, FF), F32), pltpu.VMEM((2, ROWS, FF), BF16),
        pltpu.VMEM((2, OWN, D), F32), pltpu.VMEM((2, OWN, D), F32),
        pltpu.VMEM((2, ROWS, D), BF16), pltpu.VMEM((2, 2, 8, HOWN, D), BF16), pltpu.VMEM((ROWS, D), BF16),
        pltpu.VMEM((2 * ROWS, HD), BF16), pltpu.VMEM((HD, 2 * ROWS), BF16), pltpu.VMEM((ROWS, 2 * FF), BF16),
        pltpu.VMEM((2 * ROWS, 128), F32), pltpu.VMEM((ROWS, 384), BF16), pltpu.VMEM((2, 128, ROWS), F32),
        pltpu.VMEM((8, 2 * HD, ROWS), BF16), pltpu.VMEM((2, 8, 2 * HD, ROWS), BF16), pltpu.VMEM((2 * ROWS, HD), F32),
        pltpu.VMEM((2 * ROWS, 1), F32),
        pltpu.VMEM((2, 2, 4, 576, 512), BF16), pltpu.VMEM((2, 2, 4, 288, 384), BF16), pltpu.VMEM((2, 4, 576, 512), BF16),
        pltpu.VMEM((2, 4, 288, 384), BF16), pltpu.VMEM((2, 6, 288, 512), BF16), pltpu.VMEM((2, 6, 144, 384), BF16),
        pltpu.VMEM((2, 288, 512), BF16), pltpu.VMEM((2, 144, 384), BF16), pltpu.VMEM((2, 576, 512), BF16),
        pltpu.VMEM((2, 288, 384), BF16),
        pltpu.VMEM((2, OWN, D), BF16), pltpu.VMEM((2, OWN, D), F32), pltpu.VMEM((2, 8, D), F32), pltpu.VMEM((8, D), F32),
        pltpu.VMEM((8, 8, D), F32), pltpu.VMEM((8, 8, D), F32),
        dma((10,)), dma((8,)), dma((8,)), dma((4, 2, 8)), dma((4, 2, 8)), dma((2, 2, 8)), dma((2, 2, 8)), dma((8, 2)), dma((8, 2, 2)),
        dma((8,)), dma((2, 8)), dma((2,)), dma((2,)), dma((2,)),
        dma((2, 2, 4)), dma((2, 2, 4)), dma((2, 2, 6)), dma((2, 2, 6)), dma((2, 2, 2)), dma((2, 2, 2)), dma((2, 2, 2, 3)),
        dma((2, 2, 4, 2)), dma((2, 2)), dma((2, 2, 2)), dma((2, 2, 2)), dma((3, 8)), dma((3, 8)),
    ]
    return pl.pallas_call(
        kernel,
        out_shape=(
            jax.ShapeDtypeStruct((2, OWN, D), BF16),
            jax.ShapeDtypeStruct((2, OWN, D), F32),
            jax.ShapeDtypeStruct((2, 4, 576, 512), BF16),
            jax.ShapeDtypeStruct((2, 4, 288, 384), BF16),
            jax.ShapeDtypeStruct((8, D), F32),
        ),
        in_specs=[hbm] * 9 + [vmem] * 4,
        out_specs=(hbm, hbm, hbm, hbm, vmem),
        scratch_shapes=scratch,
        compiler_params=pltpu.CompilerParams(
            collective_id=0, has_side_effects=True, vmem_limit_bytes=64 * 1024 * 1024 - 65536
        ),
        name="train_step",
    )(*args)


def widen(
    ga_hbm, gb_hbm, gn_ref, y_ref, dx_ref,
    gate_hbm, up_hbm, down_hbm, out_hbm, query_hbm, key_hbm, value_hbm, one_ref, two_ref, y_out, dx_out,
    ga, gb, gate, up, down, out, query, key, value, a_in, b_in, sent,
):
    parts = [(h, c) for c in range(4) for h in range(2)]
    a_copies = [pltpu.make_async_copy(ga_hbm.at[h, c], ga.at[h, c], a_in.at[h, c]) for h, c in parts]
    b_copies = [pltpu.make_async_copy(gb_hbm.at[:, c], gb.at[:, c], b_in.at[c]) for c in range(4)]
    for copy in b_copies + a_copies:
        copy.start()
    one_ref[...] = gn_ref[0:1, :]
    two_ref[...] = gn_ref[1:2, :]
    y_out[0] = y_ref[...]
    dx_out[0] = dx_ref[...]
    for c in range(4):
        b_copies[c].wait()
        cols = pl.ds(384 * c, 384)
        out[:, cols] = gb[0, c, 0:192, :].astype(F32)
        query[0:HD, cols] = gb[0, c, 192:288, :].astype(F32)
        query[HD : 2 * HD, cols] = gb[1, c, 0:HD, :].astype(F32)
        key[:, cols] = gb[1, c, HD : 2 * HD, :].astype(F32)
        value[:, cols] = gb[1, c, 2 * HD : 3 * HD, :].astype(F32)
    leaving = [
        pltpu.make_async_copy(buf, to, sent.at[i])
        for i, (buf, to) in enumerate(((out, out_hbm), (query, query_hbm), (key, key_hbm), (value, value_hbm)))
    ]
    for copy in leaving:
        copy.start()
    for i, (h, c) in enumerate(parts):
        a_copies[i].wait()
        rows, few = pl.ds(384 * c + 192 * h, 192), pl.ds(128 * c + 64 * h, 64)
        gate[rows, :] = ga[h, c, 0:192, :].astype(F32)
        up[rows, :] = ga[h, c, 192:384, :].astype(F32)
        for k in range(3):
            down[few, pl.ds(512 * k, 512)] = ga[h, c, 384 + 64 * k : 448 + 64 * k, :].astype(F32)
        for k, (buf, to, which) in enumerate(((gate, gate_hbm, rows), (up, up_hbm, rows), (down, down_hbm, few))):
            copy = pltpu.make_async_copy(buf.at[which], to.at[which], sent.at[4 + 3 * i + k])
            copy.start()
            leaving.append(copy)
    for copy in leaving:
        copy.wait()


def widened(ga, gb, gn, y, dx):
    grads = [(D, FF), (D, FF), (FF, D), (192, D), (192, D), (HD, D), (HD, D)]
    shapes = [jax.ShapeDtypeStruct(shape, F32) for shape in grads + [(1, D), (1, D)]]
    shapes += [jax.ShapeDtypeStruct((1, 2, OWN, D), BF16), jax.ShapeDtypeStruct((1, 2, OWN, D), F32)]
    hbm = pl.BlockSpec(memory_space=pl.ANY)
    vmem = pl.BlockSpec(memory_space=pltpu.VMEM)
    dma = pltpu.SemaphoreType.DMA
    return pl.pallas_call(
        widen,
        out_shape=tuple(shapes),
        in_specs=[hbm, hbm, vmem, vmem, vmem],
        out_specs=tuple([hbm] * 7 + [vmem] * 4),
        scratch_shapes=[pltpu.VMEM((2, 4, 576, 512), BF16), pltpu.VMEM((2, 4, 288, 384), BF16)]
        + [pltpu.VMEM(shape, F32) for shape in grads]
        + [dma((2, 4)), dma((4,)), dma((28,))],
        compiler_params=pltpu.CompilerParams(vmem_limit_bytes=63 * 1024 * 1024),
        name="widen",
    )(ga, gb, gn, y, dx)


def on_device(inputs, cotangent, doc_lengths, norm_one, query_w, key_w, value_w, out_w, norm_two, gate_w, up_w, down_w):
    lane = np.arange(128) % HALF
    speed = jnp.asarray(np.exp(lane * (-2.0 * math.log(ROPE) / HD)).astype(np.float32)[None, :])
    y, dx, ga, gb, gn = step_call(
        inputs, cotangent, query_w[0].T, key_w[0].T, value_w[0].T, out_w[0], gate_w[0], up_w[0], down_w[0], norm_one, norm_two,
        doc_lengths, speed,
    )
    gate, up, down, out, query, key, value, one, two, y, dx = widened(ga, gb, gn, y, dx)
    return (y, dx, one, query.T[None], key.T[None], value.T[None], out[None], two, gate[None], up[None], down[None])


def solution(mesh):
    in_specs = (
        P(None, "dp", None),
        P(None, "dp", None),
        P(),
        P("section", None),
        P("section", None, "tensor"),
        P("section", None, "tensor"),
        P("section", None, "tensor"),
        P("section", "tensor", None),
        P("section", None),
        P("section", None, "tensor"),
        P("section", None, "tensor"),
        P("section", "tensor", None),
    )
    out_specs = (
        P("section", None, ("dp", "tensor"), None),
        P("section", None, ("dp", "tensor"), None),
        P("section", None),
        P("section", None, "tensor"),
        P("section", None, "tensor"),
        P("section", None, "tensor"),
        P("section", "tensor", None),
        P("section", None),
        P("section", None, "tensor"),
        P("section", None, "tensor"),
        P("section", "tensor", None),
    )
    return jax.shard_map(on_device, mesh=mesh, in_specs=in_specs, out_specs=out_specs, check_vma=False)
```
